32 devices in a mesh: ctx: 32 (over z, y, x, core), head: 1.
Axes of the slice: x: 2, y: 2, z: 4, core: 2. Of those that a mesh axis runs over, the one named last changes fastest.
Arguments:
- queries: bfloat16 [4096, 4096], P(('ctx', 'head')), may hold values from -5 to 5
- key_states: bfloat16 [4096, 512], P('ctx', 'head'), may hold values from -5 to 5
- value_states: bfloat16 [4096, 512], P('ctx', 'head'), may hold values from -6 to 6
- outputs: bfloat16 [4096, 4096], P(('ctx', 'head')), may hold values from -6 to 6
- out_grad: bfloat16 [4096, 4096], P(('ctx', 'head')), may hold values from -6 to 6
- doc_of_tile: int32 [32], replicated, may hold values from 0 to 3, never falling along the last dimension, each value on 1 to 16 neighbouring positions
- tile_position: int32 [32], replicated, may hold values from 0 to 31, each once
Outputs:
- query_grad: bfloat16 [4096, 4096], P('ctx', 'head')
- key_grad: bfloat16 [4096, 512], P('ctx', 'head')
- value_grad: bfloat16 [4096, 512], P('ctx', 'head')
The draws below stay inside these ranges and needn't reach their ends.
Inputs may be any that keep to these rules, and one draw needn't show every extreme that they name: `doc_of_tile`: each document is a run of whole tiles in sequence order, 1 to 16 tiles long, one exactly 16. `tile_position`: a permutation of the 32 sequence tiles.
All inputs are finite; a program needn't handle non-finite values.
Results may differ from the reference program's by a relative error of at most 0.005.
Values may be sent and summed in bfloat16 or wider, within the bound.
A program may use at most 64 MiB of HBM per device.

```python
import math
import jax
import jax.numpy as jnp
import numpy as np
from jax import lax

HD = 128
HQ = 32
KVH = 4
TILE = 128
TOKENS = 4096
TILES = 32
GROUP = 8
DOCS = 4
DOC_MOST = 16


def drawn_draws(key):
    base_keys = jnp.clip(jax.random.normal(jax.random.fold_in(key, 11), (TOKENS, KVH, HD), jnp.float32), -5.0, 5.0)
    base_queries = jnp.clip(jax.random.normal(jax.random.fold_in(key, 12), (TOKENS, KVH, GROUP, HD), jnp.float32), -5.0, 5.0)
    new_keys = base_keys
    new_queries = base_queries
    return (new_queries.reshape(TOKENS, HQ * HD), new_keys.reshape(TOKENS, KVH * HD))


def draw_queries(key, part):
    return drawn_draws(key)[0].astype(jnp.bfloat16)


def draw_key_states(key, part):
    return drawn_draws(key)[1].astype(jnp.bfloat16)


def steps_of(own_key, extent, split, least, high):
    def one(position, blocks):
        heights = jax.random.uniform(jax.random.fold_in(jax.random.fold_in(own_key, 6), position), (blocks,), jnp.float32, least / len(split), high / len(split))
        return jnp.repeat(jnp.exp(heights), extent[position] // blocks).reshape((-1,) + (1,) * (len(extent) - position - 1))

    gain = one(*split[0])
    for cut in split[1:]:
        gain = gain * one(*cut)
    return gain


def split_up(number_of, total, limit, lean):
    weights = [(1 << 20) // math.isqrt(standing ** lean) + 1 for standing in range(2, number_of + 1)]
    surplus, given = total - limit - (number_of - 1), [1] * (number_of - 1)
    while surplus > 0:
        candidates = [i for i in range(number_of - 1) if given[i] < limit]
        whole, left = sum([weights[i] for i in candidates]), surplus
        for i in candidates:
            extra = min(limit - given[i], max(1, left * weights[i] // whole), surplus)
            given[i] = given[i] + extra
            surplus = surplus - extra
    return np.array([limit] + given)


def uneven(stream_key, amount, total, bound, skew):
    if amount == 2:
        one = jax.random.randint(stream_key, (), max(1, total - bound), min(bound, total - 1) + 1)
        return jnp.stack([one, total - one])
    sizes = jnp.asarray(split_up(amount, total, bound, skew), jnp.int32)
    twos = (amount - 1) // 2
    giver, sink = sizes[1:1 + 2 * twos:2], sizes[2:2 + 2 * twos:2]
    slack = jnp.minimum(giver - 1, bound - sink)
    shifted = jax.random.randint(jax.random.fold_in(stream_key, 1), (twos,), 0, 1 << 20) % (slack + 1)
    sizes = sizes.at[1:1 + 2 * twos:2].set(giver - shifted).at[2:2 + 2 * twos:2].set(sink + shifted)
    return sizes[jax.random.permutation(jax.random.fold_in(stream_key, 2), amount)]


def gaussian(rng, extent, spread, reach, pieces=(), kind=jnp.bfloat16):
    gain = steps_of(rng, extent, pieces, -0.22, 0.18) if pieces else 1.0
    entries = jax.random.normal(rng, extent, jnp.float32) * spread * gain
    return jnp.minimum(jnp.maximum(entries, -reach), reach).astype(kind)


def setup_inputs(seed: int = 0) -> dict:
    key_of = jax.random.split(jax.random.key(seed), 8)
    return {
        "queries": draw_queries(jax.random.fold_in(key_of[7], 71), 0),
        "key_states": draw_key_states(jax.random.fold_in(key_of[7], 71), 0),
        "value_states": gaussian(key_of[2], (TOKENS, KVH * HD), 1.0, 6.0, ((0, 32),)),
        "outputs": gaussian(key_of[3], (TOKENS, HQ * HD), 1.0, 6.0, ((0, 32),)),
        "out_grad": gaussian(key_of[4], (TOKENS, HQ * HD), 1.0, 6.0, ((0, 32),)),
        "doc_of_tile": jnp.searchsorted(jnp.cumsum(uneven(key_of[5], DOCS, TILES, DOC_MOST, 2)), jnp.arange(TILES), side="right").astype(jnp.int32),
        "tile_position": jax.random.permutation(key_of[6], TILES).astype(jnp.int32),
    }


def token_layout(tile_position, doc_of_tile):
    row_ids = jnp.arange(TOKENS, dtype=jnp.int32)
    placed = tile_position[row_ids // TILE]
    return placed * TILE + row_ids % TILE, doc_of_tile[placed]


def reference(queries, key_states, value_states, outputs, out_grad, doc_of_tile, tile_position):
    score_scale = HD ** -0.5
    highest = lax.Precision.HIGHEST
    positions, documents = token_layout(tile_position, doc_of_tile)
    query_heads = queries.astype(jnp.float32).reshape(TOKENS, KVH, GROUP, HD)
    grad_heads = out_grad.astype(jnp.float32).reshape(TOKENS, KVH, GROUP, HD)
    output_heads = outputs.astype(jnp.float32).reshape(TOKENS, KVH, GROUP, HD)
    key_heads = key_states.astype(jnp.float32).reshape(TOKENS, KVH, HD)
    value_heads = value_states.astype(jnp.float32).reshape(TOKENS, KVH, HD)
    delta_all = jnp.sum(grad_heads * output_heads, axis=-1)

    def tile_step(carry, tile_index):
        key_sum, value_sum = carry
        first = (tile_index * TILE).astype(jnp.int32)
        query_tile = lax.dynamic_slice_in_dim(query_heads, first, TILE, 0)
        grad_tile = lax.dynamic_slice_in_dim(grad_heads, first, TILE, 0)
        delta_tile = jnp.transpose(lax.dynamic_slice_in_dim(delta_all, first, TILE, 0), (1, 2, 0))
        query_pos = lax.dynamic_slice_in_dim(positions, first, TILE, 0)
        query_doc = lax.dynamic_slice_in_dim(documents, first, TILE, 0)
        visible = (query_doc[:, None] == documents[None, :]) & (positions[None, :] <= query_pos[:, None])
        scores = jnp.einsum("qkgd,pkd->kgqp", query_tile, key_heads, precision=highest) * score_scale
        top = jnp.max(jnp.where(visible, scores, -1e30), axis=-1)
        total = jnp.sum(jnp.exp(jnp.where(visible, scores - top[..., None], -1e30)), axis=-1)
        log_total = top + jnp.log(total)
        probs = jnp.exp(jnp.where(visible, scores - log_total[..., None], -1e30))
        probs_low = lax.optimization_barrier(probs.astype(jnp.bfloat16)).astype(jnp.float32)
        grad_probs = jnp.einsum("qkgd,pkd->kgqp", grad_tile, value_heads, precision=highest)
        grad_scores = probs * (grad_probs - delta_tile[..., None]) * score_scale
        grad_scores = lax.optimization_barrier(grad_scores.astype(jnp.bfloat16)).astype(jnp.float32)
        query_part = jnp.einsum("kgqp,pkd->qkgd", grad_scores, key_heads, precision=highest)
        key_sum = key_sum + jnp.einsum("kgqp,qkgd->pkd", grad_scores, query_tile, precision=highest)
        value_sum = value_sum + jnp.einsum("kgqp,qkgd->pkd", probs_low, grad_tile, precision=highest)
        return (key_sum, value_sum), query_part.astype(jnp.bfloat16).reshape(TILE, HQ * HD)

    zeros_start = jnp.zeros((TOKENS, KVH, HD), jnp.float32)
    (key_sum, value_sum), query_parts = lax.scan(tile_step, (zeros_start, zeros_start), jnp.arange(TILES))
    query_grad = query_parts.reshape(TOKENS, HQ * HD)
    key_grad = key_sum.reshape(TOKENS, KVH * HD).astype(jnp.bfloat16)
    value_grad = value_sum.reshape(TOKENS, KVH * HD).astype(jnp.bfloat16)
    return (query_grad, key_grad, value_grad)
```

```python
import functools

import jax
import jax.numpy as jnp
from jax import lax
from jax.experimental import pallas as pl
from jax.experimental.pallas import tpu as pltpu
from jax.sharding import PartitionSpec as P

HD = 128
TILE = 128
SPAN = 2
LOW = -1e30
MESH = pl.DeviceIdType.MESH


def attention_kernel(
    heads,
    tiles,
    position_ref,
    doc_ref,
    block_ref,
    q_ref,
    g_ref,
    delta_ref,
    kv_ref,
    dq_ref,
    dkv_ref,
    inverse_ref,
    q_rows,
    q_cols,
    g_rows,
    g_cols,
    score_buf,
    dq_acc,
    dkv_acc,
):
    width = heads * HD
    scale = HD ** (-0.5)
    keys = SPAN * TILE
    count = position_ref.shape[0]
    dkv_acc[...] = jnp.zeros_like(dkv_acc)
    row_id = lax.broadcasted_iota(jnp.int32, (keys, width), 0)
    col_id = lax.broadcasted_iota(jnp.int32, (keys, width), 1) & (TILE - 1)
    gap = row_id - col_id

    @pl.loop(0, count)
    def _(spot):
        inverse_ref[position_ref[spot]] = spot

    def spots(last):
        found = []
        for offset in range(SPAN):
            where = jnp.maximum(last - (SPAN - 1) + offset, 0)
            found.append(pl.multiple_of(inverse_ref[where] * TILE, TILE))
        return found

    def block(last, which):
        return jnp.concatenate(
            [kv_ref[which, pl.ds(spot, TILE), :] for spot in spots(last)], axis=0
        )

    @pl.loop(0, tiles)
    def _(tile):
        first_row = pl.multiple_of(tile * TILE, TILE)
        place = position_ref[block_ref[0] * tiles + tile]
        doc = doc_ref[place]
        start = lax.fori_loop(
            0, count, lambda i, n: n + jnp.where(doc_ref[i] < doc, 1, 0), jnp.int32(0)
        )
        chunks = (place - start + SPAN) // SPAN
        for h in range(heads):
            lanes = slice(h * HD, (h + 1) * HD)
            q_block = q_ref[pl.ds(first_row, TILE), lanes]
            g_block = g_ref[pl.ds(first_row, TILE), lanes]
            q_rows[lanes, :] = q_block
            g_rows[lanes, :] = g_block
            q_cols[:, lanes] = q_block.T
            g_cols[:, lanes] = g_block.T

        def totals(step, state):
            top, total = state
            last = place - SPAN * step
            scores = (
                jnp.dot(block(last, 0), q_cols[...], preferred_element_type=jnp.float32) * scale
            )
            first_key = (last - (SPAN - 1)) * TILE
            visible = (gap <= place * TILE - first_key) & (row_id >= start * TILE - first_key)
            scores = jnp.where(visible, scores, LOW)
            score_buf[step] = scores
            new_top = jnp.maximum(top, jnp.max(scores, axis=0, keepdims=True))
            total = total * jnp.exp(top - new_top) + jnp.sum(
                jnp.exp(scores - new_top), axis=0, keepdims=True
            )
            return new_top, total

        top, total = lax.fori_loop(
            0,
            chunks,
            totals,
            (jnp.full((1, width), LOW, jnp.float32), jnp.zeros((1, width), jnp.float32)),
        )
        log_total = top + jnp.log(total)
        delta = delta_ref[tile, 0:1, :]
        dq_acc[...] = jnp.zeros_like(dq_acc)

        @pl.loop(0, chunks)
        def _(step):
            last = place - SPAN * step
            k_block = block(last, 0)
            probs = jnp.exp(score_buf[step] - log_total)
            grad_probs = jnp.dot(
                block(last, 1), g_cols[...], preferred_element_type=jnp.float32
            )
            low = probs.astype(jnp.bfloat16)
            grad_scores = (probs * (grad_probs - delta) * scale).astype(jnp.bfloat16)
            dv = jnp.dot(low, g_rows[...], preferred_element_type=jnp.float32)
            dk = jnp.dot(grad_scores, q_rows[...], preferred_element_type=jnp.float32)
            dq_acc[...] += lax.dot_general(
                k_block,
                grad_scores,
                (((0,), (0,)), ((), ())),
                preferred_element_type=jnp.float32,
            )
            for offset, spot in enumerate(spots(last)):
                rows = slice(offset * TILE, (offset + 1) * TILE)
                dkv_acc[0, pl.ds(spot, TILE), :] += dk[rows]
                dkv_acc[1, pl.ds(spot, TILE), :] += dv[rows]

        for h in range(heads):
            lanes = slice(h * HD, (h + 1) * HD)
            dq_ref[pl.ds(first_row, TILE), lanes] = dq_acc[:, lanes].T.astype(jnp.bfloat16)

    dkv_ref[...] = dkv_acc[...].astype(jnp.bfloat16)


def attention_backward(positions, docs, block, q, g, delta, kv):
    rows, width = q.shape
    heads = width // HD
    tokens = kv.shape[1]
    tiles = rows // TILE
    count = tokens // TILE
    smem = pl.BlockSpec(memory_space=pltpu.SMEM)
    vmem = pl.BlockSpec(memory_space=pltpu.VMEM)
    return pl.pallas_call(
        functools.partial(attention_kernel, heads, tiles),
        out_shape=(
            jax.ShapeDtypeStruct((rows, width), jnp.bfloat16),
            jax.ShapeDtypeStruct((2, tokens, HD), jnp.bfloat16),
        ),
        in_specs=[smem, smem, smem, vmem, vmem, vmem, vmem],
        out_specs=(vmem, vmem),
        scratch_shapes=[
            pltpu.SMEM((count,), jnp.int32),
            pltpu.VMEM((width, HD), jnp.bfloat16),
            pltpu.VMEM((HD, width), jnp.bfloat16),
            pltpu.VMEM((width, HD), jnp.bfloat16),
            pltpu.VMEM((HD, width), jnp.bfloat16),
            pltpu.VMEM((count // SPAN // 2 + 1, SPAN * TILE, width), jnp.float32),
            pltpu.VMEM((HD, width), jnp.float32),
            pltpu.VMEM((2, tokens, HD), jnp.float32),
        ],
        compiler_params=pltpu.CompilerParams(vmem_limit_bytes=40 * 1024 * 1024),
        cost_estimate=pl.CostEstimate(
            flops=rows * width * tokens * 3, bytes_accessed=12 << 20, transcendentals=0
        ),
    )(positions, docs, block, q, g, delta, kv)


def bring_kernel(
    team,
    planes,
    q_ref,
    g_ref,
    k_ref,
    v_ref,
    o_ref,
    q_out,
    g_out,
    delta_out,
    kv_out,
    kv_own,
    g_own,
    o_own,
    delta_own,
    load_sem,
    local_sem,
    flat_send,
    flat_recv,
    chain_send,
    chain_recv,
    core_send,
    core_recv,
):
    me = lax.axis_index("ctx")
    slot = me % team
    plane = me // team
    core = slot % 2
    mate = me + 1 - 2 * core
    width = q_out.shape[1]
    span = team * TILE
    tall = pl.ds(pl.multiple_of(slot * TILE, TILE), TILE)
    wide = pl.ds(pl.multiple_of(slot * width, HD), width)

    loads = [
        pltpu.make_async_copy(k_ref, kv_own.at[0], load_sem.at[0]),
        pltpu.make_async_copy(v_ref, kv_own.at[1], load_sem.at[1]),
        pltpu.make_async_copy(g_ref, g_own, load_sem.at[2]),
        pltpu.make_async_copy(o_ref, o_own, load_sem.at[3]),
    ]
    for load in loads:
        load.start()

    barrier = pltpu.get_barrier_semaphore()
    for shift in range(1, team):
        pl.semaphore_signal(
            barrier,
            inc=1,
            device_id=(plane * team + (slot + shift) % team, 0),
            device_id_type=MESH,
        )

    @pl.when(plane < planes - 1)
    def _():
        pl.semaphore_signal(barrier, inc=1, device_id=(me + team, 0), device_id_type=MESH)

    @pl.when(plane > 0)
    def _():
        pl.semaphore_signal(barrier, inc=1, device_id=(me - team, 0), device_id_type=MESH)

    near = jnp.where(plane < planes - 1, 1, 0) + jnp.where(plane > 0, 1, 0)
    pl.semaphore_wait(barrier, team - 1 + near)

    def flat(kind, shift, src, dst):
        return pltpu.make_async_remote_copy(
            src_ref=src,
            dst_ref=dst,
            send_sem=flat_send.at[kind, shift - 1],
            recv_sem=flat_recv.at[kind, shift - 1],
            device_id=(plane * team + (slot + shift) % team, 0),
            device_id_type=MESH,
        )

    loads[0].wait()
    loads[1].wait()
    home = pl.ds(pl.multiple_of(me * TILE, TILE), TILE)
    flats = []
    for shift in range(1, team):
        other = (slot + shift) % team
        lanes = pl.ds(pl.multiple_of(other // 2 * HD, HD), HD)
        copy = flat(
            0, shift, kv_own.at[other % 2, :, lanes], kv_out.at[other % 2, home, :]
        )
        copy.start()
        flats.append(copy)
    locals_ = [
        pltpu.make_async_copy(
            kv_own.at[core, :, pl.ds(pl.multiple_of(slot // 2 * HD, HD), HD)],
            kv_out.at[core, home, :],
            local_sem.at[0],
        ),
        pltpu.make_async_copy(q_ref.at[:, wide], q_out.at[tall, :], local_sem.at[1]),
        pltpu.make_async_copy(g_ref.at[:, wide], g_out.at[tall, :], local_sem.at[2]),
    ]
    for copy in locals_:
        copy.start()
    rest = []
    for kind, (src, dst) in enumerate(((q_ref, q_out), (g_ref, g_out))):
        for shift in range(1, team):
            other = (slot + shift) % team
            lanes = pl.ds(pl.multiple_of(other * width, HD), width)
            copy = flat(1 + kind, shift, src.at[:, lanes], dst.at[tall, :])
            copy.start()
            rest.append(copy)
    locals_[0].wait()
    for copy in flats:
        copy.wait_recv()

    def part(which):
        return kv_out.at[core, pl.ds(pl.multiple_of(which * span, TILE), span), :]

    def chain(way, step, which):
        return pltpu.make_async_remote_copy(
            src_ref=part(which),
            dst_ref=part(which),
            send_sem=chain_send.at[way, step],
            recv_sem=chain_recv.at[way, step],
            device_id=(me + team - 2 * way * team, 0),
            device_id_type=MESH,
        )

    def share(index, which):
        return pltpu.make_async_remote_copy(
            src_ref=part(which),
            dst_ref=part(which),
            send_sem=core_send.at[index],
            recv_sem=core_recv.at[index],
            device_id=(mate, 0),
            device_id_type=MESH,
        )

    def up_ok(step):
        return (plane < planes - 1) & (plane - step >= 0)

    def down_ok(step):
        return (plane > 0) & (plane + step <= planes - 1)

    def up_come(step):
        return plane - 1 - step >= 0

    def down_come(step):
        return plane + 1 + step <= planes - 1

    def send(step):
        @pl.when(up_ok(step))
        def _():
            chain(0, step, plane - step).start()

        @pl.when(down_ok(step))
        def _():
            chain(1, step, plane + step).start()

    send(0)
    share(0, plane).start()

    loads[2].wait()
    loads[3].wait()
    for index in range(team):
        for head in range(width // HD):
            lanes = slice(index * width + head * HD, index * width + (head + 1) * HD)
            product = g_own[:, lanes].astype(jnp.float32) * o_own[:, lanes].astype(jnp.float32)
            row = jnp.sum(product.T, axis=0, keepdims=True)
            delta_own[index, :, head * HD : (head + 1) * HD] = jnp.broadcast_to(row, (8, HD))
    for shift in range(1, team):
        other = (slot + shift) % team
        copy = flat(3, shift, delta_own.at[other], delta_out.at[slot])
        copy.start()
        rest.append(copy)
    own_delta = pltpu.make_async_copy(delta_own.at[slot], delta_out.at[slot], local_sem.at[3])
    own_delta.start()

    for step in range(planes - 1):
        @pl.when(up_come(step))
        def _():
            chain(0, step, plane - 1 - step).wait_recv()
            if step < planes - 2:
                @pl.when(up_ok(step + 1))
                def _():
                    chain(0, step + 1, plane - 1 - step).start()
            share(1 + step, plane - 1 - step).start()

        @pl.when(down_come(step))
        def _():
            chain(1, step, plane + 1 + step).wait_recv()
            if step < planes - 2:
                @pl.when(down_ok(step + 1))
                def _():
                    chain(1, step + 1, plane + 1 + step).start()
            share(planes + step, plane + 1 + step).start()

    share(0, plane).wait()
    for step in range(planes - 1):
        @pl.when(up_come(step))
        def _():
            share(1 + step, plane - 1 - step).wait()

        @pl.when(down_come(step))
        def _():
            share(planes + step, plane + 1 + step).wait()

        @pl.when(up_ok(step))
        def _():
            chain(0, step, plane - step).wait_send()

        @pl.when(down_ok(step))
        def _():
            chain(1, step, plane + step).wait_send()

    for copy in locals_[1:] + [own_delta]:
        copy.wait()
    for copy in rest:
        copy.wait()
    for copy in flats:
        copy.wait_send()


def bring(team, planes, queries, out_grad, key_states, value_states, outputs):
    rows, columns = queries.shape
    width = columns // team
    tokens = rows * team * planes
    vmem = pl.BlockSpec(memory_space=pltpu.VMEM)
    hbm = pl.BlockSpec(memory_space=pltpu.HBM)
    dma = pltpu.SemaphoreType.DMA
    return pl.pallas_call(
        functools.partial(bring_kernel, team, planes),
        out_shape=(
            jax.ShapeDtypeStruct((rows * team, width), jnp.bfloat16),
            jax.ShapeDtypeStruct((rows * team, width), jnp.bfloat16),
            jax.ShapeDtypeStruct((team, 8, width), jnp.float32),
            jax.ShapeDtypeStruct((2, tokens, HD), jnp.bfloat16),
        ),
        in_specs=[hbm, hbm, hbm, hbm, hbm],
        out_specs=(vmem, vmem, vmem, vmem),
        scratch_shapes=[
            pltpu.VMEM((2, rows, key_states.shape[1]), jnp.bfloat16),
            pltpu.VMEM((rows, columns), jnp.bfloat16),
            pltpu.VMEM((rows, columns), jnp.bfloat16),
            pltpu.VMEM((team, 8, width), jnp.float32),
            dma((4,)),
            dma((4,)),
            dma((4, team - 1)),
            dma((4, team - 1)),
            dma((2, planes - 1)),
            dma((2, planes - 1)),
            dma((2 * planes - 1,)),
            dma((2 * planes - 1,)),
        ],
        compiler_params=pltpu.CompilerParams(
            collective_id=0, has_side_effects=True, vmem_limit_bytes=24 * 1024 * 1024
        ),
        cost_estimate=pl.CostEstimate(flops=0, bytes_accessed=60 << 20, transcendentals=0),
    )(queries, out_grad, key_states, value_states, outputs)


def return_kernel(
    team,
    planes,
    dq_ref,
    dkv_ref,
    dq_out,
    dkv_out,
    mate_in,
    up_in,
    down_in,
    up_own,
    down_own,
    total,
    local_sem,
    flat_send,
    flat_recv,
    chain_send,
    chain_recv,
    core_send,
    core_recv,
):
    me = lax.axis_index("ctx")
    slot = me % team
    plane = me // team
    core = slot % 2
    mate = me + 1 - 2 * core
    width = dq_ref.shape[1]
    span = team * TILE

    barrier = pltpu.get_barrier_semaphore()
    for shift in range(1, team):
        pl.semaphore_signal(
            barrier,
            inc=1,
            device_id=(plane * team + (slot + shift) % team, 0),
            device_id_type=MESH,
        )

    @pl.when(plane < planes - 1)
    def _():
        pl.semaphore_signal(barrier, inc=1, device_id=(me + team, 0), device_id_type=MESH)

    @pl.when(plane > 0)
    def _():
        pl.semaphore_signal(barrier, inc=1, device_id=(me - team, 0), device_id_type=MESH)

    near = jnp.where(plane < planes - 1, 1, 0) + jnp.where(plane > 0, 1, 0)
    pl.semaphore_wait(barrier, team - 1 + near)

    def rows_of(which):
        return pl.ds(pl.multiple_of(which * span, TILE), span)

    order = []
    for step in range(planes):
        which = planes - 1 - step // 2 if step % 2 == 0 else step // 2
        order.append(which)
    shares = {}
    for which in order:
        copy = pltpu.make_async_remote_copy(
            src_ref=dkv_ref.at[1 - core, rows_of(which), :],
            dst_ref=mate_in.at[which],
            send_sem=core_send.at[which],
            recv_sem=core_recv.at[which],
            device_id=(mate, 0),
            device_id_type=MESH,
        )
        copy.start()
        shares[which] = copy

    def flat(kind, shift, src, dst):
        return pltpu.make_async_remote_copy(
            src_ref=src,
            dst_ref=dst,
            send_sem=flat_send.at[kind, shift - 1],
            recv_sem=flat_recv.at[kind, shift - 1],
            device_id=(plane * team + (slot + shift) % team, 0),
            device_id_type=MESH,
        )

    def tile_rows(which):
        return pl.ds(pl.multiple_of(which * TILE, TILE), TILE)

    wide = pl.ds(pl.multiple_of(slot * width, HD), width)
    rest = []
    own_dq = pltpu.make_async_copy(
        dq_ref.at[tile_rows(slot), :], dq_out.at[:, wide], local_sem.at[0]
    )
    own_dq.start()
    for shift in range(1, team):
        other = (slot + shift) % team
        copy = flat(0, shift, dq_ref.at[tile_rows(other), :], dq_out.at[:, wide])
        copy.start()
        rest.append(copy)

    def chain(way, index):
        own, into = ((up_own, up_in), (down_own, down_in))[way]
        return pltpu.make_async_remote_copy(
            src_ref=own.at[index],
            dst_ref=into.at[index],
            send_sem=chain_send.at[way, index],
            recv_sem=chain_recv.at[way, index],
            device_id=(me + team - 2 * way * team, 0),
            device_id_type=MESH,
        )

    def local_sum(which):
        return dkv_ref[core, rows_of(which), :].astype(jnp.float32) + mate_in[which].astype(
            jnp.float32
        )

    waited = set()

    def ready(which):
        if which not in waited:
            shares[which].wait_recv()
            waited.add(which)

    for index in range(planes - 1):
        up_to = planes - 1 - index
        down_to = index
        ready(up_to)

        @pl.when((plane < up_to) & (plane > 0))
        def _():
            chain(0, index).wait_recv()
            up_own[index] = (local_sum(up_to) + up_in[index].astype(jnp.float32)).astype(
                jnp.bfloat16
            )
            chain(0, index).start()

        @pl.when(plane == 0)
        def _():
            up_own[index] = local_sum(up_to).astype(jnp.bfloat16)
            chain(0, index).start()

        ready(down_to)

        @pl.when((plane > down_to) & (plane < planes - 1))
        def _():
            chain(1, index).wait_recv()
            down_own[index] = (local_sum(down_to) + down_in[index].astype(jnp.float32)).astype(
                jnp.bfloat16
            )
            chain(1, index).start()

        @pl.when(plane == planes - 1)
        def _():
            down_own[index] = local_sum(down_to).astype(jnp.bfloat16)
            chain(1, index).start()

    mine = local_sum(plane)

    @pl.when(plane == 0)
    def _():
        chain(1, plane).wait_recv()
        total[...] = (mine + down_in[plane].astype(jnp.float32)).astype(jnp.bfloat16)

    @pl.when(plane == planes - 1)
    def _():
        chain(0, planes - 1 - plane).wait_recv()
        total[...] = (mine + up_in[planes - 1 - plane].astype(jnp.float32)).astype(jnp.bfloat16)

    @pl.when((plane > 0) & (plane < planes - 1))
    def _():
        chain(0, planes - 1 - plane).wait_recv()
        chain(1, plane).wait_recv()
        total[...] = (
            mine
            + up_in[planes - 1 - plane].astype(jnp.float32)
            + down_in[plane].astype(jnp.float32)
        ).astype(jnp.bfloat16)

    lanes = pl.ds(pl.multiple_of(slot // 2 * HD, HD), HD)
    own_dkv = pltpu.make_async_copy(
        total.at[tile_rows(slot), :], dkv_out.at[core, :, lanes], local_sem.at[1]
    )
    own_dkv.start()
    for shift in range(1, team):
        other = (slot + shift) % team
        copy = flat(1, shift, total.at[tile_rows(other), :], dkv_out.at[core, :, lanes])
        copy.start()
        rest.append(copy)
    own_dq.wait()
    own_dkv.wait()
    for index in range(planes - 1):
        @pl.when(plane < planes - 1 - index)
        def _():
            chain(0, index).wait_send()

        @pl.when(plane > index)
        def _():
            chain(1, index).wait_send()

    for which in order:
        shares[which].wait_send()
    for copy in rest:
        copy.wait()


def give_back(team, planes, dq, dkv):
    tall, width = dq.shape
    rows = tall // team
    heads = team // 2
    vmem = pl.BlockSpec(memory_space=pltpu.VMEM)
    hbm = pl.BlockSpec(memory_space=pltpu.HBM)
    dma = pltpu.SemaphoreType.DMA
    part = pltpu.VMEM((planes - 1, tall, HD), jnp.bfloat16)
    return pl.pallas_call(
        functools.partial(return_kernel, team, planes),
        out_shape=(
            jax.ShapeDtypeStruct((rows, width * team), jnp.bfloat16),
            jax.ShapeDtypeStruct((2, rows, heads * HD), jnp.bfloat16),
        ),
        in_specs=[vmem, vmem],
        out_specs=(hbm, hbm),
        scratch_shapes=[
            pltpu.VMEM((planes, tall, HD), jnp.bfloat16),
            part,
            part,
            part,
            part,
            pltpu.VMEM((tall, HD), jnp.bfloat16),
            dma((2,)),
            dma((2, team - 1)),
            dma((2, team - 1)),
            dma((2, planes - 1)),
            dma((2, planes - 1)),
            dma((planes,)),
            dma((planes,)),
        ],
        compiler_params=pltpu.CompilerParams(
            collective_id=1, has_side_effects=True, vmem_limit_bytes=24 * 1024 * 1024
        ),
        cost_estimate=pl.CostEstimate(flops=0, bytes_accessed=60 << 20, transcendentals=0),
    )(dq, dkv)


def local_planes(queries, key_states, value_states, outputs, out_grad, doc_of_tile, tile_position):
    team = 2 * (key_states.shape[1] // HD)
    planes = lax.axis_size("ctx") // team
    q, g, delta, kv = bring(team, planes, queries, out_grad, key_states, value_states, outputs)
    block = (lax.axis_index("ctx") // team).astype(jnp.int32).reshape(1)
    dq, dkv = attention_backward(tile_position, doc_of_tile, block, q, g, delta, kv)
    dq, dkv = give_back(team, planes, dq, dkv)
    return dq, dkv[0], dkv[1]


def local_any(queries, key_states, value_states, outputs, out_grad, doc_of_tile, tile_position):
    rows = queries.shape[0]
    kv_heads = key_states.shape[1] // HD
    head_count = lax.axis_size("head")
    ctx_count = lax.axis_size("ctx")
    ctx_index = lax.axis_index("ctx")
    split = kv_heads * head_count
    team = kv_heads
    parts = ctx_count // team
    near = [[b * team + s for s in range(team)] for b in range(parts)]
    far = [[b * team + s for b in range(parts)] for s in range(team)]

    def swap(value, split_axis, concat_axis):
        if head_count > 1:
            return lax.all_to_all(value, "head", split_axis, concat_axis, tiled=True)
        return lax.all_to_all(
            value, "ctx", split_axis, concat_axis, axis_index_groups=near, tiled=True
        )

    heads = queries.shape[1] // split // HD
    products = out_grad.astype(jnp.float32) * outputs.astype(jnp.float32)
    delta = jnp.sum(products.reshape(rows, split * heads, HD), axis=-1)
    kv = jnp.concatenate([key_states, value_states], axis=1)
    if head_count == 1:
        kv = kv.reshape(rows, 2, team, HD).transpose(0, 2, 1, 3).reshape(rows, team * 2 * HD)
        kv = swap(kv, 1, 0)
    kv = lax.all_gather(kv, "ctx", axis=0, tiled=True, axis_index_groups=far)
    kv = kv.reshape(-1, 2, HD).transpose(1, 0, 2)
    qd = jnp.concatenate(
        [
            queries.reshape(rows, split, heads * HD),
            out_grad.reshape(rows, split, heads * HD),
        ],
        axis=2,
    ).reshape(rows, split * 2 * heads * HD)
    qd = swap(qd, 1, 0)
    delta = swap(delta, 1, 0)
    tiles = qd.shape[0] // TILE
    delta = jnp.transpose(delta.reshape(tiles, TILE, heads), (0, 2, 1)).reshape(
        tiles, 1, heads * TILE
    )
    delta = jnp.broadcast_to(delta, (tiles, 8, heads * TILE))
    block = (ctx_index // team).astype(jnp.int32).reshape(1)
    width = heads * HD
    dq, dkv = attention_backward(
        tile_position, doc_of_tile, block, qd[:, :width], qd[:, width:], delta, kv
    )
    if head_count == 1:
        dq = swap(dq, 0, 1)
    dkv = dkv.transpose(1, 0, 2).reshape(-1, 2 * HD)
    dkv = lax.all_to_all(dkv, "ctx", 0, 0, axis_index_groups=far, tiled=True)
    dkv = jnp.sum(dkv.reshape(parts, -1, 2 * HD).astype(jnp.float32), axis=0).astype(jnp.bfloat16)
    if head_count == 1:
        dkv = swap(dkv, 0, 1)
    dkv = dkv.reshape(dkv.shape[0], kv_heads, 2, HD)
    return (
        dq,
        dkv[:, :, 0].reshape(-1, kv_heads * HD),
        dkv[:, :, 1].reshape(-1, kv_heads * HD),
    )


def solution(mesh):
    placed = (
        P(("ctx", "head"), None),
        P("ctx", "head"),
        P("ctx", "head"),
        P(("ctx", "head"), None),
        P(("ctx", "head"), None),
        P(),
        P(),
    )
    slabs = mesh.shape["head"] == 1 and mesh.shape["ctx"] == 32
    return jax.shard_map(
        local_planes if slabs else local_any,
        mesh=mesh,
        in_specs=placed,
        out_specs=(P("ctx", "head"), P("ctx", "head"), P("ctx", "head")),
        check_vma=False,
    )
```

```python
import functools

import jax
import jax.numpy as jnp
from jax import lax
from jax.experimental import pallas as pl
from jax.experimental.pallas import tpu as pltpu
from jax.sharding import PartitionSpec as P

HD = 128
TILE = 128
SPAN = 2
LOW = -1e30
LOG2E = 1.4426950408889634
DEEP = 4
SUB = 2
GIVE_LIMIT = 60 * 1024 * 1024
ATTENTION_LIMIT = 56 * 1024 * 1024
MESH = pl.DeviceIdType.MESH


def attention_kernel(
    heads,
    tiles,
    team,
    position_ref,
    doc_ref,
    q_hbm,
    g_hbm,
    delta_hbm,
    kv_hbm,
    dq_ref,
    dkv_ref,
    start_ref,
    item_tile,
    item_first,
    item_bound,
    q_rows,
    g_rows,
    q_cols,
    g_cols,
    delta_ref,
    kv_ref,
    gap_ref,
    scores_a,
    scores_b,
    low_a,
    low_b,
    grad_a,
    grad_b,
    probs_buf,
    top_buf,
    top_ref,
    total_ref,
    share_ref,
    dq_acc,
    dkv_acc,
    dq_own,
    dkv_own,
    sems,
):
    width = heads * HD
    scale = HD ** (-0.5)
    pair = SPAN * TILE
    count = position_ref.shape[0]
    block = lax.axis_index("ctx") // team

    def tile_at(index):
        return pl.ds(pl.multiple_of(index * TILE, TILE), TILE)

    heads_in = []
    for h in range(heads):
        lanes = slice(h * HD, (h + 1) * HD)
        for which, (src, dst) in enumerate(((q_hbm, q_rows), (g_hbm, g_rows))):
            copy = pltpu.make_async_copy(
                src.at[:, :, lanes], dst.at[0:tiles, h], sems.at[2 + 2 * h + which]
            )
            copy.start()
            heads_in.append(copy)
    delta_in = pltpu.make_async_copy(delta_hbm, delta_ref.at[0:tiles], sems.at[0])
    delta_in.start()

    @pl.loop(0, count)
    def _(spot):
        place = position_ref[spot]
        for which in range(2):
            pltpu.make_async_copy(
                kv_hbm.at[which, tile_at(spot), :],
                kv_ref.at[which, tile_at(place), :],
                sems.at[1],
            ).start()

    def find(index, start):
        fresh = doc_ref[index] != doc_ref[jnp.maximum(index - 1, 0)]
        start = jnp.where(fresh, index, start)
        start_ref[index] = start
        return start

    lax.fori_loop(0, count, find, jnp.int32(0))

    def put(index, tile, first, bound):
        item_tile[index] = tile
        item_first[index] = first
        item_bound[index] = bound

    def listed(tile, total):
        place = position_ref[block * tiles + tile]
        start = start_ref[place]
        pieces = (place - start + 2) // 2

        @pl.loop(0, pieces)
        def _(step):
            first = start + 2 * step
            put(total + step, tile, first, (place - first) * TILE)

        return total + pieces

    items = lax.fori_loop(0, tiles, listed, jnp.int32(0))
    for extra in range(4):
        put(items + extra, tiles, 0, pair)

    gap_ref[...] = lax.broadcasted_iota(jnp.int32, (pair, TILE), 0) - lax.broadcasted_iota(
        jnp.int32, (pair, TILE), 1
    )
    dkv_acc[...] = jnp.zeros_like(dkv_acc)
    dq_acc[...] = jnp.zeros_like(dq_acc)
    top_ref[...] = jnp.full_like(top_ref, LOW)
    total_ref[...] = jnp.zeros_like(total_ref)
    q_cols[tiles] = jnp.zeros((HD, width), jnp.bfloat16)
    g_cols[tiles] = jnp.zeros((HD, width), jnp.bfloat16)
    q_rows[tiles] = jnp.zeros((heads, TILE, HD), jnp.bfloat16)
    g_rows[tiles] = jnp.zeros((heads, TILE, HD), jnp.bfloat16)
    delta_ref[tiles] = jnp.zeros((8, width), jnp.float32)
    kv_ref[:, count * TILE :, :] = jnp.zeros((2, TILE, HD), jnp.bfloat16)
    low_b[...] = jnp.zeros_like(low_b)
    grad_b[...] = jnp.zeros_like(grad_b)

    for copy in heads_in:
        copy.wait()

    @pl.loop(0, tiles)
    def _(tile):
        for h in range(heads):
            lanes = slice(h * HD, (h + 1) * HD)
            q_cols[tile, :, lanes] = q_rows[tile, h].T
            g_cols[tile, :, lanes] = g_rows[tile, h].T

    delta_in.wait()
    pltpu.make_async_copy(kv_hbm, kv_ref.at[:, 0 : count * TILE], sems.at[1]).wait()

    def groups(value):
        return value.reshape(value.shape[0] // 8, 8, width)

    def area(index):
        return pl.ds(pl.multiple_of(item_first[index] * TILE, TILE), pair)

    def score(index, into):
        into[...] = jnp.dot(
            kv_ref[0, area(index), :],
            q_cols[item_tile[index]],
            preferred_element_type=jnp.float32,
        )

    def weigh(index, source):
        tile = item_tile[index]
        gap = jnp.concatenate([gap_ref[...]] * heads, axis=1)
        scores = groups(
            jnp.where(gap <= item_bound[index], source[...] * (scale * LOG2E), LOW)
        )
        old = top_ref[tile]
        top = jnp.maximum(old, jnp.max(scores, axis=0))
        probs = jnp.exp2(scores - top[None])
        probs_buf[index] = probs.reshape(pair, width)
        top_buf[index] = top
        top_ref[tile] = top
        total_ref[tile] = total_ref[tile] * jnp.exp2(old - top) + jnp.sum(probs, axis=0)

    score(0, scores_a)

    def weigh_two(index):
        score(index + 1, scores_b)
        weigh(index, scores_a)
        score(index + 2, scores_a)
        weigh(index + 1, scores_b)

    rounds = (items + 1) // 2

    @pl.loop(0, rounds // DEEP)
    def _(step):
        for part in range(DEEP):
            weigh_two(2 * (DEEP * step + part))

    @pl.loop(rounds // DEEP * DEEP, rounds)
    def _(step):
        weigh_two(2 * step)

    for tile in range(tiles):
        top = top_ref[tile]
        peak = jnp.broadcast_to(jnp.max(top, axis=0, keepdims=True), (8, width))
        total = jnp.sum(total_ref[tile] * jnp.exp2(top - peak), axis=0, keepdims=True)
        top_ref[tile] = peak
        share_ref[tile] = 1.0 / jnp.broadcast_to(total, (8, width))
    top_ref[tiles] = jnp.zeros((8, width), jnp.float32)
    share_ref[tiles] = jnp.zeros((8, width), jnp.float32)
    for extra in range(2):
        probs_buf[items + extra] = jnp.zeros((pair, width), jnp.float32)
        top_buf[items + extra] = jnp.zeros((8, width), jnp.float32)

    def value_scores(index, into):
        into[...] = jnp.dot(
            kv_ref[1, area(index), :],
            g_cols[item_tile[index]],
            preferred_element_type=jnp.float32,
        )

    def combine(index, source, low, grad):
        tile = item_tile[index]
        factor = jnp.exp2(top_buf[index] - top_ref[tile]) * share_ref[tile]
        probs = groups(probs_buf[index]) * factor[None]
        low[...] = probs.reshape(pair, width).astype(jnp.bfloat16)
        grad[...] = (
            (probs * (groups(source[...]) - delta_ref[tile][None]))
            .reshape(pair, width)
            .astype(jnp.bfloat16)
        )

    def add(index, low, grad):
        tile = item_tile[index]
        spot = area(index)
        dkv_acc[1, spot, :] += jnp.dot(
            low[...], g_rows[tile].reshape(width, HD), preferred_element_type=jnp.float32
        )
        dkv_acc[0, spot, :] += jnp.dot(
            grad[...], q_rows[tile].reshape(width, HD), preferred_element_type=jnp.float32
        )
        dq_acc[tile] += lax.dot_general(
            kv_ref[0, spot, :],
            grad[...],
            (((0,), (0,)), ((), ())),
            preferred_element_type=jnp.float32,
        )

    value_scores(0, scores_a)

    def add_two(index):
        value_scores(index + 1, scores_b)
        add(jnp.where(index == 0, items, index - 1), low_b, grad_b)
        combine(index, scores_a, low_a, grad_a)
        value_scores(index + 2, scores_a)
        add(index, low_a, grad_a)
        combine(index + 1, scores_b, low_b, grad_b)

    turns = (items + 2) // 2

    @pl.loop(0, turns // DEEP)
    def _(step):
        for part in range(DEEP):
            add_two(2 * (DEEP * step + part))

    @pl.loop(turns // DEEP * DEEP, turns)
    def _(step):
        add_two(2 * step)

    outs = [pltpu.make_async_copy(dkv_own.at[w], dkv_ref.at[w], sems.at[w]) for w in range(2)]
    for which, factor in enumerate((scale, 1.0)):
        @pl.loop(0, count, unroll=4)
        def _(spot):
            place = position_ref[spot]
            dkv_own[which, tile_at(spot), :] = (
                dkv_acc[which, tile_at(place), :] * factor
            ).astype(jnp.bfloat16)

        outs[which].start()

    for tile in range(tiles):
        rows = slice(tile * TILE, (tile + 1) * TILE)
        for h in range(heads):
            lanes = slice(h * HD, (h + 1) * HD)
            dq_own[rows, lanes] = (dq_acc[tile, :, lanes] * scale).T.astype(jnp.bfloat16)
        copy = pltpu.make_async_copy(dq_own.at[rows], dq_ref.at[rows], sems.at[2 + tile])
        copy.start()
        outs.append(copy)
    for copy in outs:
        copy.wait()


def attention_backward(positions, docs, team, q, g, delta, kv):
    rows, width = q.shape
    heads = width // HD
    tokens = kv.shape[1]
    tiles = rows // TILE
    count = tokens // TILE
    longest = count // 2
    most = sum((longest - i + 1) // 2 for i in range(min(tiles, longest)))
    most = max(most, tiles) + 4
    pair = SPAN * TILE
    smem = pl.BlockSpec(memory_space=pltpu.SMEM)
    hbm = pl.BlockSpec(memory_space=pl.ANY)
    slots = tiles + 1
    stat = pltpu.VMEM((slots, 8, width), jnp.float32)
    return pl.pallas_call(
        functools.partial(attention_kernel, heads, tiles, team),
        out_shape=(
            jax.ShapeDtypeStruct((rows, width), jnp.bfloat16),
            jax.ShapeDtypeStruct((2, tokens, HD), jnp.bfloat16),
        ),
        in_specs=[smem, smem, hbm, hbm, hbm, hbm],
        out_specs=(hbm, hbm),
        scratch_shapes=[
            pltpu.SMEM((count,), jnp.int32),
            pltpu.SMEM((most,), jnp.int32),
            pltpu.SMEM((most,), jnp.int32),
            pltpu.SMEM((most,), jnp.int32),
            pltpu.VMEM((slots, heads, TILE, HD), jnp.bfloat16),
            pltpu.VMEM((slots, heads, TILE, HD), jnp.bfloat16),
            pltpu.VMEM((slots, HD, width), jnp.bfloat16),
            pltpu.VMEM((slots, HD, width), jnp.bfloat16),
            stat,
            pltpu.VMEM((2, tokens + TILE, HD), jnp.bfloat16),
            pltpu.VMEM((pair, TILE), jnp.int32),
            pltpu.VMEM((pair, width), jnp.float32),
            pltpu.VMEM((pair, width), jnp.float32),
            pltpu.VMEM((pair, width), jnp.bfloat16),
            pltpu.VMEM((pair, width), jnp.bfloat16),
            pltpu.VMEM((pair, width), jnp.bfloat16),
            pltpu.VMEM((pair, width), jnp.bfloat16),
            pltpu.VMEM((most, pair, width), jnp.float32),
            pltpu.VMEM((most, 8, width), jnp.float32),
            stat,
            stat,
            stat,
            pltpu.VMEM((slots, HD, width), jnp.float32),
            pltpu.VMEM((2, tokens + TILE, HD), jnp.float32),
            pltpu.VMEM((rows, width), jnp.bfloat16),
            pltpu.VMEM((2, tokens, HD), jnp.bfloat16),
            pltpu.SemaphoreType.DMA((2 + max(2 * heads, tiles),)),
        ],
        compiler_params=pltpu.CompilerParams(vmem_limit_bytes=ATTENTION_LIMIT),
        cost_estimate=pl.CostEstimate(
            flops=rows * width * tokens * 3, bytes_accessed=12 << 20, transcendentals=0
        ),
    )(positions, docs, q.reshape(tiles, TILE, width), g.reshape(tiles, TILE, width), delta, kv)


def bring_kernel(
    team,
    planes,
    q_ref,
    g_ref,
    k_ref,
    v_ref,
    o_ref,
    q_out,
    g_out,
    delta_out,
    kv_out,
    kv_own,
    g_own,
    o_own,
    delta_own,
    load_sem,
    local_sem,
    flat_send,
    flat_recv,
    chain_send,
    chain_recv,
    core_send,
    core_recv,
):
    me = lax.axis_index("ctx")
    slot = me % team
    plane = me // team
    core = slot % 2
    mate = me + 1 - 2 * core
    width = q_out.shape[1]
    span = team * TILE
    tall = pl.ds(pl.multiple_of(slot * TILE, TILE), TILE)
    wide = pl.ds(pl.multiple_of(slot * width, HD), width)

    loads = [
        pltpu.make_async_copy(k_ref, kv_own.at[0], load_sem.at[0]),
        pltpu.make_async_copy(v_ref, kv_own.at[1], load_sem.at[1]),
        pltpu.make_async_copy(g_ref, g_own, load_sem.at[2]),
        pltpu.make_async_copy(o_ref, o_own, load_sem.at[3]),
    ]
    for load in loads:
        load.start()

    barrier = pltpu.get_barrier_semaphore()
    for shift in range(1, team):
        pl.semaphore_signal(
            barrier,
            inc=1,
            device_id=(plane * team + (slot + shift) % team, 0),
            device_id_type=MESH,
        )

    @pl.when(plane < planes - 1)
    def _():
        pl.semaphore_signal(barrier, inc=1, device_id=(me + team, 0), device_id_type=MESH)

    @pl.when(plane > 0)
    def _():
        pl.semaphore_signal(barrier, inc=1, device_id=(me - team, 0), device_id_type=MESH)

    near = jnp.where(plane < planes - 1, 1, 0) + jnp.where(plane > 0, 1, 0)
    pl.semaphore_wait(barrier, team - 1 + near)

    def flat(kind, shift, src, dst):
        return pltpu.make_async_remote_copy(
            src_ref=src,
            dst_ref=dst,
            send_sem=flat_send.at[kind, shift - 1],
            recv_sem=flat_recv.at[kind, slot],
            device_id=(plane * team + (slot + shift) % team, 0),
            device_id_type=MESH,
        )

    loads[0].wait()
    loads[1].wait()
    home = pl.ds(pl.multiple_of(me * TILE, TILE), TILE)
    flats = []
    for shift in range(1, team):
        other = (slot + shift) % team
        lanes = pl.ds(pl.multiple_of(other // 2 * HD, HD), HD)
        copy = flat(
            0, shift, kv_own.at[other % 2, :, lanes], kv_out.at[other % 2, home, :]
        )
        copy.start()
        flats.append(copy)
    locals_ = [
        pltpu.make_async_copy(
            kv_own.at[core, :, pl.ds(pl.multiple_of(slot // 2 * HD, HD), HD)],
            kv_out.at[core, home, :],
            local_sem.at[0],
        ),
        pltpu.make_async_copy(q_ref.at[:, wide], q_out.at[tall, :], local_sem.at[1]),
        pltpu.make_async_copy(g_ref.at[:, wide], g_out.at[tall, :], local_sem.at[2]),
    ]
    for copy in locals_:
        copy.start()
    rest = []
    for kind, (src, dst) in enumerate(((q_ref, q_out), (g_ref, g_out))):
        for shift in range(1, team):
            other = (slot + shift) % team
            lanes = pl.ds(pl.multiple_of(other * width, HD), width)
            copy = flat(1 + kind, shift, src.at[:, lanes], dst.at[tall, :])
            copy.start()
            rest.append(copy)
    locals_[0].wait()
    part_rows = span // SUB
    per_part = team // SUB

    def arrived(kind, source, dst):
        return pltpu.make_async_remote_copy(
            src_ref=dst,
            dst_ref=dst,
            send_sem=flat_send.at[kind, 0],
            recv_sem=flat_recv.at[kind, source],
            device_id=(mate, 0),
            device_id_type=MESH,
        )

    def part(which, sub):
        first = pl.multiple_of(which * span + sub * part_rows, TILE)
        return kv_out.at[core, pl.ds(first, part_rows), :]

    def chain(way, step, which, sub):
        return pltpu.make_async_remote_copy(
            src_ref=part(which, sub),
            dst_ref=part(which, sub),
            send_sem=chain_send.at[way, step, sub],
            recv_sem=chain_recv.at[way, step, sub],
            device_id=(me + team - 2 * way * team, 0),
            device_id_type=MESH,
        )

    def share(index, which, sub):
        return pltpu.make_async_remote_copy(
            src_ref=part(which, sub),
            dst_ref=part(which, sub),
            send_sem=core_send.at[index, sub],
            recv_sem=core_recv.at[index, sub],
            device_id=(mate, 0),
            device_id_type=MESH,
        )

    def up_ok(step):
        return (plane < planes - 1) & (plane - step >= 0)

    def down_ok(step):
        return (plane > 0) & (plane + step <= planes - 1)

    def up_come(step):
        return plane - 1 - step >= 0

    def down_come(step):
        return plane + 1 + step <= planes - 1

    for sub in range(SUB):
        for source in range(sub * per_part, (sub + 1) * per_part):
            @pl.when(slot != source)
            def _():
                arrived(0, source, kv_out.at[core, home, :]).wait_recv()

        @pl.when(up_ok(0))
        def _():
            chain(0, 0, plane, sub).start()

        @pl.when(down_ok(0))
        def _():
            chain(1, 0, plane, sub).start()

        share(0, plane, sub).start()

    loads[2].wait()
    loads[3].wait()
    for index in range(team):
        for head in range(width // HD):
            lanes = slice(index * width + head * HD, index * width + (head + 1) * HD)
            product = g_own[:, lanes].astype(jnp.float32) * o_own[:, lanes].astype(jnp.float32)
            row = jnp.sum(product.T, axis=0, keepdims=True)
            delta_own[index, :, head * HD : (head + 1) * HD] = jnp.broadcast_to(row, (8, HD))
    for shift in range(1, team):
        other = (slot + shift) % team
        copy = flat(3, shift, delta_own.at[other], delta_out.at[slot])
        copy.start()
        rest.append(copy)
    own_delta = pltpu.make_async_copy(delta_own.at[slot], delta_out.at[slot], local_sem.at[3])
    own_delta.start()

    for step in range(planes - 1):
        for sub in range(SUB):
            @pl.when(up_come(step))
            def _():
                chain(0, step, plane - 1 - step, sub).wait_recv()
                if step < planes - 2:
                    @pl.when(up_ok(step + 1))
                    def _():
                        chain(0, step + 1, plane - 1 - step, sub).start()
                share(1 + step, plane - 1 - step, sub).start()

            @pl.when(down_come(step))
            def _():
                chain(1, step, plane + 1 + step, sub).wait_recv()
                if step < planes - 2:
                    @pl.when(down_ok(step + 1))
                    def _():
                        chain(1, step + 1, plane + 1 + step, sub).start()
                share(planes + step, plane + 1 + step, sub).start()

    for sub in range(SUB):
        share(0, plane, sub).wait()
        for step in range(planes - 1):
            @pl.when(up_come(step))
            def _():
                share(1 + step, plane - 1 - step, sub).wait()

            @pl.when(down_come(step))
            def _():
                share(planes + step, plane + 1 + step, sub).wait()

            @pl.when(up_ok(step))
            def _():
                chain(0, step, plane - step, sub).wait_send()

            @pl.when(down_ok(step))
            def _():
                chain(1, step, plane + step, sub).wait_send()

    for copy in locals_[1:] + [own_delta]:
        copy.wait()
    for copy in rest + flats:
        copy.wait_send()
    for source in range(team):
        @pl.when(slot != source)
        def _():
            arrived(1, source, q_out.at[tall, :]).wait_recv()
            arrived(2, source, g_out.at[tall, :]).wait_recv()
            arrived(3, source, delta_out.at[slot]).wait_recv()


def bring(team, planes, queries, out_grad, key_states, value_states, outputs):
    rows, columns = queries.shape
    width = columns // team
    tokens = rows * team * planes
    vmem = pl.BlockSpec(memory_space=pltpu.VMEM)
    hbm = pl.BlockSpec(memory_space=pltpu.HBM)
    dma = pltpu.SemaphoreType.DMA
    return pl.pallas_call(
        functools.partial(bring_kernel, team, planes),
        out_shape=(
            jax.ShapeDtypeStruct((rows * team, width), jnp.bfloat16),
            jax.ShapeDtypeStruct((rows * team, width), jnp.bfloat16),
            jax.ShapeDtypeStruct((team, 8, width), jnp.float32),
            jax.ShapeDtypeStruct((2, tokens, HD), jnp.bfloat16),
        ),
        in_specs=[hbm, hbm, hbm, hbm, hbm],
        out_specs=(hbm, hbm, hbm, hbm),
        scratch_shapes=[
            pltpu.VMEM((2, rows, key_states.shape[1]), jnp.bfloat16),
            pltpu.VMEM((rows, columns), jnp.bfloat16),
            pltpu.VMEM((rows, columns), jnp.bfloat16),
            pltpu.VMEM((team, 8, width), jnp.float32),
            dma((4,)),
            dma((4,)),
            dma((4, team - 1)),
            dma((4, team)),
            dma((2, planes - 1, SUB)),
            dma((2, planes - 1, SUB)),
            dma((2 * planes - 1, SUB)),
            dma((2 * planes - 1, SUB)),
        ],
        compiler_params=pltpu.CompilerParams(
            collective_id=0, has_side_effects=True, vmem_limit_bytes=60 * 1024 * 1024
        ),
        cost_estimate=pl.CostEstimate(flops=0, bytes_accessed=60 << 20, transcendentals=0),
    )(queries, out_grad, key_states, value_states, outputs)


def return_kernel(
    team,
    planes,
    dq_ref,
    dkv_ref,
    dq_out,
    dkv_out,
    own,
    mate_in,
    up_in,
    down_in,
    up_own,
    down_own,
    total,
    local_sem,
    dq_send,
    dq_recv,
    flat_send,
    flat_recv,
    chain_send,
    chain_recv,
    core_send,
    core_recv,
):
    me = lax.axis_index("ctx")
    slot = me % team
    plane = me // team
    core = slot % 2
    mate = me + 1 - 2 * core
    width = dq_ref.shape[1]
    span = team * TILE
    part_rows = span // SUB
    per_part = team // SUB

    load = pltpu.make_async_copy(dkv_ref.at[core], own, local_sem.at[2])
    load.start()
    barrier = pltpu.get_barrier_semaphore()
    for shift in range(1, team):
        pl.semaphore_signal(
            barrier,
            inc=1,
            device_id=(plane * team + (slot + shift) % team, 0),
            device_id_type=MESH,
        )

    @pl.when(plane < planes - 1)
    def _():
        pl.semaphore_signal(barrier, inc=1, device_id=(me + team, 0), device_id_type=MESH)

    @pl.when(plane > 0)
    def _():
        pl.semaphore_signal(barrier, inc=1, device_id=(me - team, 0), device_id_type=MESH)

    near = jnp.where(plane < planes - 1, 1, 0) + jnp.where(plane > 0, 1, 0)
    pl.semaphore_wait(barrier, team - 1 + near)

    def rows_of(which, sub):
        return pl.ds(pl.multiple_of(which * span + sub * part_rows, TILE), part_rows)

    def inner(sub):
        return pl.ds(sub * part_rows, part_rows)

    def tile_rows(which):
        return pl.ds(pl.multiple_of(which * TILE, TILE), TILE)

    order = []
    for step in range(planes):
        which = planes - 1 - step // 2 if step % 2 == 0 else step // 2
        order.extend((which, sub) for sub in range(SUB))
    shares = {}
    for which, sub in order:
        copy = pltpu.make_async_remote_copy(
            src_ref=dkv_ref.at[1 - core, rows_of(which, sub), :],
            dst_ref=mate_in.at[which, inner(sub)],
            send_sem=core_send.at[which, sub],
            recv_sem=core_recv.at[which, sub],
            device_id=(mate, 0),
            device_id_type=MESH,
        )
        copy.start()
        shares[which, sub] = copy

    wide = pl.ds(pl.multiple_of(slot * width, HD), width)
    rest = []
    own_dq = pltpu.make_async_copy(
        dq_ref.at[tile_rows(slot), :], dq_out.at[:, wide], local_sem.at[0]
    )
    own_dq.start()
    for shift in range(1, team):
        other = (slot + shift) % team
        copy = pltpu.make_async_remote_copy(
            src_ref=dq_ref.at[tile_rows(other), :],
            dst_ref=dq_out.at[:, wide],
            send_sem=dq_send.at[shift - 1],
            recv_sem=dq_recv.at[shift - 1],
            device_id=(plane * team + other, 0),
            device_id_type=MESH,
        )
        copy.start()
        rest.append(copy)

    def chain(way, index, sub):
        source, into = ((up_own, up_in), (down_own, down_in))[way]
        return pltpu.make_async_remote_copy(
            src_ref=source.at[index, inner(sub)],
            dst_ref=into.at[index, inner(sub)],
            send_sem=chain_send.at[way, index, sub],
            recv_sem=chain_recv.at[way, index, sub],
            device_id=(me + team - 2 * way * team, 0),
            device_id_type=MESH,
        )

    def local_sum(which, sub):
        return own[rows_of(which, sub), :].astype(jnp.float32) + mate_in[
            which, inner(sub)
        ].astype(jnp.float32)

    load.wait()
    waited = set()

    def ready(which, sub):
        if (which, sub) not in waited:
            shares[which, sub].wait_recv()
            waited.add((which, sub))

    for index in range(planes - 1):
        up_to = planes - 1 - index
        down_to = index
        for sub in range(SUB):
            ready(up_to, sub)

            @pl.when((plane < up_to) & (plane > 0))
            def _():
                chain(0, index, sub).wait_recv()
                up_own[index, inner(sub)] = (
                    local_sum(up_to, sub) + up_in[index, inner(sub)].astype(jnp.float32)
                ).astype(jnp.bfloat16)
                chain(0, index, sub).start()

            @pl.when(plane == 0)
            def _():
                up_own[index, inner(sub)] = local_sum(up_to, sub).astype(jnp.bfloat16)
                chain(0, index, sub).start()

            ready(down_to, sub)

            @pl.when((plane > down_to) & (plane < planes - 1))
            def _():
                chain(1, index, sub).wait_recv()
                down_own[index, inner(sub)] = (
                    local_sum(down_to, sub) + down_in[index, inner(sub)].astype(jnp.float32)
                ).astype(jnp.bfloat16)
                chain(1, index, sub).start()

            @pl.when(plane == planes - 1)
            def _():
                down_own[index, inner(sub)] = local_sum(down_to, sub).astype(jnp.bfloat16)
                chain(1, index, sub).start()

    lanes = pl.ds(pl.multiple_of(slot // 2 * HD, HD), HD)
    up_last = planes - 1 - plane

    def flat(target):
        return pltpu.make_async_remote_copy(
            src_ref=total.at[tile_rows(target), :],
            dst_ref=dkv_out.at[core, :, lanes],
            send_sem=flat_send.at[target],
            recv_sem=flat_recv.at[slot],
            device_id=(plane * team + target, 0),
            device_id_type=MESH,
        )

    for sub in range(SUB):
        mine = local_sum(plane, sub)

        @pl.when(plane == 0)
        def _():
            chain(1, plane, sub).wait_recv()
            total[inner(sub)] = (
                mine + down_in[plane, inner(sub)].astype(jnp.float32)
            ).astype(jnp.bfloat16)

        @pl.when(plane == planes - 1)
        def _():
            chain(0, up_last, sub).wait_recv()
            total[inner(sub)] = (
                mine + up_in[up_last, inner(sub)].astype(jnp.float32)
            ).astype(jnp.bfloat16)

        @pl.when((plane > 0) & (plane < planes - 1))
        def _():
            chain(0, up_last, sub).wait_recv()
            chain(1, plane, sub).wait_recv()
            total[inner(sub)] = (
                mine
                + up_in[up_last, inner(sub)].astype(jnp.float32)
                + down_in[plane, inner(sub)].astype(jnp.float32)
            ).astype(jnp.bfloat16)

        for target in range(sub * per_part, (sub + 1) * per_part):
            @pl.when(slot != target)
            def _():
                flat(target).start()

    own_dkv = pltpu.make_async_copy(
        total.at[tile_rows(slot), :], dkv_out.at[core, :, lanes], local_sem.at[1]
    )
    own_dkv.start()
    own_dq.wait()
    own_dkv.wait()
    for sub in range(SUB):
        for index in range(planes - 1):
            @pl.when(plane < planes - 1 - index)
            def _():
                chain(0, index, sub).wait_send()

            @pl.when(plane > index)
            def _():
                chain(1, index, sub).wait_send()

    for key in order:
        shares[key].wait_send()
    for copy in rest:
        copy.wait()
    for target in range(team):
        @pl.when(slot != target)
        def _():
            flat(target).wait_send()
            pltpu.make_async_remote_copy(
                src_ref=total.at[tile_rows(slot), :],
                dst_ref=dkv_out.at[core, :, lanes],
                send_sem=flat_send.at[target],
                recv_sem=flat_recv.at[target],
                device_id=(mate, 0),
                device_id_type=MESH,
            ).wait_recv()


def give_back(team, planes, dq, dkv):
    tall, width = dq.shape
    rows = tall // team
    heads = team // 2
    hbm = pl.BlockSpec(memory_space=pl.ANY)
    dma = pltpu.SemaphoreType.DMA
    part = pltpu.VMEM((planes - 1, tall, HD), jnp.bfloat16)
    return pl.pallas_call(
        functools.partial(return_kernel, team, planes),
        out_shape=(
            jax.ShapeDtypeStruct((rows, width * team), jnp.bfloat16),
            jax.ShapeDtypeStruct((2, rows, heads * HD), jnp.bfloat16),
        ),
        in_specs=[hbm, hbm],
        out_specs=(hbm, hbm),
        scratch_shapes=[
            pltpu.VMEM((planes * tall, HD), jnp.bfloat16),
            pltpu.VMEM((planes, tall, HD), jnp.bfloat16),
            part,
            part,
            part,
            part,
            pltpu.VMEM((tall, HD), jnp.bfloat16),
            dma((3,)),
            dma((team - 1,)),
            dma((team - 1,)),
            dma((team,)),
            dma((team,)),
            dma((2, planes - 1, SUB)),
            dma((2, planes - 1, SUB)),
            dma((planes, SUB)),
            dma((planes, SUB)),
        ],
        compiler_params=pltpu.CompilerParams(
            collective_id=1, has_side_effects=True, vmem_limit_bytes=GIVE_LIMIT
        ),
        cost_estimate=pl.CostEstimate(flops=0, bytes_accessed=60 << 20, transcendentals=0),
    )(dq, dkv)


def local_planes(queries, key_states, value_states, outputs, out_grad, doc_of_tile, tile_position):
    team = 2 * (key_states.shape[1] // HD)
    planes = lax.axis_size("ctx") // team
    q, g, delta, kv = bring(team, planes, queries, out_grad, key_states, value_states, outputs)
    dq, dkv = attention_backward(tile_position, doc_of_tile, team, q, g, delta, kv)
    dq, dkv = give_back(team, planes, dq, dkv)
    return dq, dkv[0], dkv[1]


def local_any(queries, key_states, value_states, outputs, out_grad, doc_of_tile, tile_position):
    rows = queries.shape[0]
    kv_heads = key_states.shape[1] // HD
    head_count = lax.axis_size("head")
    ctx_count = lax.axis_size("ctx")
    ctx_index = lax.axis_index("ctx")
    split = kv_heads * head_count
    team = kv_heads
    parts = ctx_count // team
    near = [[b * team + s for s in range(team)] for b in range(parts)]
    far = [[b * team + s for b in range(parts)] for s in range(team)]

    def swap(value, split_axis, concat_axis):
        if head_count > 1:
            return lax.all_to_all(value, "head", split_axis, concat_axis, tiled=True)
        return lax.all_to_all(
            value, "ctx", split_axis, concat_axis, axis_index_groups=near, tiled=True
        )

    heads = queries.shape[1] // split // HD
    products = out_grad.astype(jnp.float32) * outputs.astype(jnp.float32)
    delta = jnp.sum(products.reshape(rows, split * heads, HD), axis=-1)
    kv = jnp.concatenate([key_states, value_states], axis=1)
    if head_count == 1:
        kv = kv.reshape(rows, 2, team, HD).transpose(0, 2, 1, 3).reshape(rows, team * 2 * HD)
        kv = swap(kv, 1, 0)
    kv = lax.all_gather(kv, "ctx", axis=0, tiled=True, axis_index_groups=far)
    kv = kv.reshape(-1, 2, HD).transpose(1, 0, 2)
    qd = jnp.concatenate(
        [
            queries.reshape(rows, split, heads * HD),
            out_grad.reshape(rows, split, heads * HD),
        ],
        axis=2,
    ).reshape(rows, split * 2 * heads * HD)
    qd = swap(qd, 1, 0)
    delta = swap(delta, 1, 0)
    tiles = qd.shape[0] // TILE
    delta = jnp.transpose(delta.reshape(tiles, TILE, heads), (0, 2, 1)).reshape(
        tiles, 1, heads * TILE
    )
    delta = jnp.broadcast_to(delta, (tiles, 8, heads * TILE))
    width = heads * HD
    dq, dkv = attention_backward(
        tile_position, doc_of_tile, team, qd[:, :width], qd[:, width:], delta, kv
    )
    if head_count == 1:
        dq = swap(dq, 0, 1)
    dkv = dkv.transpose(1, 0, 2).reshape(-1, 2 * HD)
    dkv = lax.all_to_all(dkv, "ctx", 0, 0, axis_index_groups=far, tiled=True)
    dkv = jnp.sum(dkv.reshape(parts, -1, 2 * HD).astype(jnp.float32), axis=0).astype(jnp.bfloat16)
    if head_count == 1:
        dkv = swap(dkv, 0, 1)
    dkv = dkv.reshape(dkv.shape[0], kv_heads, 2, HD)
    return (
        dq,
        dkv[:, :, 0].reshape(-1, kv_heads * HD),
        dkv[:, :, 1].reshape(-1, kv_heads * HD),
    )


def solution(mesh):
    placed = (
        P(("ctx", "head"), None),
        P("ctx", "head"),
        P("ctx", "head"),
        P(("ctx", "head"), None),
        P(("ctx", "head"), None),
        P(),
        P(),
    )
    slabs = mesh.shape["head"] == 1 and mesh.shape["ctx"] == 32
    return jax.shard_map(
        local_planes if slabs else local_any,
        mesh=mesh,
        in_specs=placed,
        out_specs=(P("ctx", "head"), P("ctx", "head"), P("ctx", "head")),
        check_vma=False,
    )
```

```python
import functools

import jax
import jax.numpy as jnp
from jax import lax
from jax.experimental import pallas as pl
from jax.experimental.pallas import tpu as pltpu
from jax.sharding import PartitionSpec as P

HD = 128
TILE = 128
SPAN = 2
LOW = -1e30
LOG2E = 1.4426950408889634
DEEP = 4
SUB = 2
FINE = 4
FLIGHT = 2
GIVE_LIMIT = 52 * 1024 * 1024
ATTENTION_LIMIT = 56 * 1024 * 1024
MESH = pl.DeviceIdType.MESH


def attention_kernel(
    heads,
    tiles,
    team,
    position_ref,
    doc_ref,
    q_hbm,
    g_hbm,
    delta_hbm,
    kv_hbm,
    dq_ref,
    dkv_ref,
    start_ref,
    item_tile,
    item_first,
    item_bound,
    q_rows,
    g_rows,
    q_cols,
    g_cols,
    delta_ref,
    kv_ref,
    gap_ref,
    scores_a,
    scores_b,
    low_a,
    low_b,
    grad_a,
    grad_b,
    probs_buf,
    top_buf,
    top_ref,
    total_ref,
    share_ref,
    dq_acc,
    dkv_acc,
    dq_own,
    dkv_own,
    sems,
):
    width = heads * HD
    scale = HD ** (-0.5)
    pair = SPAN * TILE
    count = position_ref.shape[0]
    block = lax.axis_index("ctx") // team

    def tile_at(index):
        return pl.ds(pl.multiple_of(index * TILE, TILE), TILE)

    heads_in = []
    for h in range(heads):
        lanes = slice(h * HD, (h + 1) * HD)
        for which, (src, dst) in enumerate(((q_hbm, q_rows), (g_hbm, g_rows))):
            copy = pltpu.make_async_copy(
                src.at[:, :, lanes], dst.at[0:tiles, h], sems.at[2 + 2 * h + which]
            )
            copy.start()
            heads_in.append(copy)
    delta_in = pltpu.make_async_copy(delta_hbm, delta_ref.at[0:tiles], sems.at[0])
    delta_in.start()

    @pl.loop(0, count)
    def _(spot):
        place = position_ref[spot]
        for which in range(2):
            pltpu.make_async_copy(
                kv_hbm.at[which, tile_at(spot), :],
                kv_ref.at[which, tile_at(place), :],
                sems.at[1],
            ).start()

    def find(index, start):
        fresh = doc_ref[index] != doc_ref[jnp.maximum(index - 1, 0)]
        start = jnp.where(fresh, index, start)
        start_ref[index] = start
        return start

    lax.fori_loop(0, count, find, jnp.int32(0))

    def put(index, tile, first, bound):
        item_tile[index] = tile
        item_first[index] = first
        item_bound[index] = bound

    def listed(tile, total):
        place = position_ref[block * tiles + tile]
        start = start_ref[place]
        pieces = (place - start + 2) // 2

        @pl.loop(0, pieces)
        def _(step):
            first = start + 2 * step
            put(total + step, tile, first, (place - first) * TILE)

        return total + pieces

    items = lax.fori_loop(0, tiles, listed, jnp.int32(0))
    for extra in range(4):
        put(items + extra, tiles, 0, pair)

    gap_ref[...] = lax.broadcasted_iota(jnp.int32, (pair, TILE), 0) - lax.broadcasted_iota(
        jnp.int32, (pair, TILE), 1
    )
    dkv_acc[...] = jnp.zeros_like(dkv_acc)
    dq_acc[...] = jnp.zeros_like(dq_acc)
    top_ref[...] = jnp.full_like(top_ref, LOW)
    total_ref[...] = jnp.zeros_like(total_ref)
    q_cols[tiles] = jnp.zeros((HD, width), jnp.bfloat16)
    g_cols[tiles] = jnp.zeros((HD, width), jnp.bfloat16)
    q_rows[tiles] = jnp.zeros((heads, TILE, HD), jnp.bfloat16)
    g_rows[tiles] = jnp.zeros((heads, TILE, HD), jnp.bfloat16)
    delta_ref[tiles] = jnp.zeros((8, width), jnp.float32)
    kv_ref[:, count * TILE :, :] = jnp.zeros((2, TILE, HD), jnp.bfloat16)
    low_b[...] = jnp.zeros_like(low_b)
    grad_b[...] = jnp.zeros_like(grad_b)

    for copy in heads_in:
        copy.wait()

    @pl.loop(0, tiles)
    def _(tile):
        for h in range(heads):
            lanes = slice(h * HD, (h + 1) * HD)
            q_cols[tile, :, lanes] = q_rows[tile, h].T
            g_cols[tile, :, lanes] = g_rows[tile, h].T

    delta_in.wait()
    pltpu.make_async_copy(kv_hbm, kv_ref.at[:, 0 : count * TILE], sems.at[1]).wait()

    def groups(value):
        return value.reshape(value.shape[0] // 8, 8, width)

    def area(index):
        return pl.ds(pl.multiple_of(item_first[index] * TILE, TILE), pair)

    def score(index, into):
        into[...] = jnp.dot(
            kv_ref[0, area(index), :],
            q_cols[item_tile[index]],
            preferred_element_type=jnp.float32,
        )

    def weigh(index, source):
        tile = item_tile[index]
        gap = jnp.concatenate([gap_ref[...]] * heads, axis=1)
        scores = groups(
            jnp.where(gap <= item_bound[index], source[...] * (scale * LOG2E), LOW)
        )
        old = top_ref[tile]
        top = jnp.maximum(old, jnp.max(scores, axis=0))
        probs = jnp.exp2(scores - top[None])
        probs_buf[index] = probs.reshape(pair, width)
        top_buf[index] = top
        top_ref[tile] = top
        total_ref[tile] = total_ref[tile] * jnp.exp2(old - top) + jnp.sum(probs, axis=0)

    score(0, scores_a)

    def weigh_two(index):
        score(index + 1, scores_b)
        weigh(index, scores_a)
        score(index + 2, scores_a)
        weigh(index + 1, scores_b)

    rounds = (items + 1) // 2

    @pl.loop(0, rounds // DEEP)
    def _(step):
        for part in range(DEEP):
            weigh_two(2 * (DEEP * step + part))

    @pl.loop(rounds // DEEP * DEEP, rounds)
    def _(step):
        weigh_two(2 * step)

    for tile in range(tiles):
        top = top_ref[tile]
        peak = jnp.broadcast_to(jnp.max(top, axis=0, keepdims=True), (8, width))
        total = jnp.sum(total_ref[tile] * jnp.exp2(top - peak), axis=0, keepdims=True)
        top_ref[tile] = peak
        share_ref[tile] = 1.0 / jnp.broadcast_to(total, (8, width))
    top_ref[tiles] = jnp.zeros((8, width), jnp.float32)
    share_ref[tiles] = jnp.zeros((8, width), jnp.float32)
    for extra in range(2):
        probs_buf[items + extra] = jnp.zeros((pair, width), jnp.float32)
        top_buf[items + extra] = jnp.zeros((8, width), jnp.float32)

    def value_scores(index, into):
        into[...] = jnp.dot(
            kv_ref[1, area(index), :],
            g_cols[item_tile[index]],
            preferred_element_type=jnp.float32,
        )

    def combine(index, source, low, grad):
        tile = item_tile[index]
        factor = jnp.exp2(top_buf[index] - top_ref[tile]) * share_ref[tile]
        probs = groups(probs_buf[index]) * factor[None]
        low[...] = probs.reshape(pair, width).astype(jnp.bfloat16)
        grad[...] = (
            (probs * (groups(source[...]) - delta_ref[tile][None]) * scale)
            .reshape(pair, width)
            .astype(jnp.bfloat16)
        )

    def add(index, low, grad):
        tile = item_tile[index]
        spot = area(index)
        dkv_acc[1, spot, :] += jnp.dot(
            low[...], g_rows[tile].reshape(width, HD), preferred_element_type=jnp.float32
        )
        dkv_acc[0, spot, :] += jnp.dot(
            grad[...], q_rows[tile].reshape(width, HD), preferred_element_type=jnp.float32
        )
        dq_acc[tile] += lax.dot_general(
            kv_ref[0, spot, :],
            grad[...],
            (((0,), (0,)), ((), ())),
            preferred_element_type=jnp.float32,
        )

    value_scores(0, scores_a)

    def add_two(index):
        value_scores(index + 1, scores_b)
        add(jnp.where(index == 0, items, index - 1), low_b, grad_b)
        combine(index, scores_a, low_a, grad_a)
        value_scores(index + 2, scores_a)
        add(index, low_a, grad_a)
        combine(index + 1, scores_b, low_b, grad_b)

    turns = (items + 2) // 2

    @pl.loop(0, turns // DEEP)
    def _(step):
        for part in range(DEEP):
            add_two(2 * (DEEP * step + part))

    @pl.loop(turns // DEEP * DEEP, turns)
    def _(step):
        add_two(2 * step)

    outs = [pltpu.make_async_copy(dkv_own.at[w], dkv_ref.at[w], sems.at[w]) for w in range(2)]
    for which in range(2):
        @pl.loop(0, count, unroll=4)
        def _(spot):
            place = position_ref[spot]
            dkv_own[which, tile_at(spot), :] = dkv_acc[which, tile_at(place), :].astype(
                jnp.bfloat16
            )

        outs[which].start()

    for tile in range(tiles):
        rows = slice(tile * TILE, (tile + 1) * TILE)
        for h in range(heads):
            lanes = slice(h * HD, (h + 1) * HD)
            dq_own[rows, lanes] = dq_acc[tile, :, lanes].T.astype(jnp.bfloat16)
        copy = pltpu.make_async_copy(dq_own.at[rows], dq_ref.at[rows], sems.at[2 + tile])
        copy.start()
        outs.append(copy)
    for copy in outs:
        copy.wait()


def attention_backward(positions, docs, team, q, g, delta, kv):
    rows, width = q.shape
    heads = width // HD
    tokens = kv.shape[1]
    tiles = rows // TILE
    count = tokens // TILE
    longest = count // 2
    most = sum((longest - i + 1) // 2 for i in range(min(tiles, longest)))
    most = max(most, tiles) + 4
    pair = SPAN * TILE
    smem = pl.BlockSpec(memory_space=pltpu.SMEM)
    hbm = pl.BlockSpec(memory_space=pl.ANY)
    slots = tiles + 1
    stat = pltpu.VMEM((slots, 8, width), jnp.float32)
    return pl.pallas_call(
        functools.partial(attention_kernel, heads, tiles, team),
        out_shape=(
            jax.ShapeDtypeStruct((rows, width), jnp.bfloat16),
            jax.ShapeDtypeStruct((2, tokens, HD), jnp.bfloat16),
        ),
        in_specs=[smem, smem, hbm, hbm, hbm, hbm],
        out_specs=(hbm, hbm),
        scratch_shapes=[
            pltpu.SMEM((count,), jnp.int32),
            pltpu.SMEM((most,), jnp.int32),
            pltpu.SMEM((most,), jnp.int32),
            pltpu.SMEM((most,), jnp.int32),
            pltpu.VMEM((slots, heads, TILE, HD), jnp.bfloat16),
            pltpu.VMEM((slots, heads, TILE, HD), jnp.bfloat16),
            pltpu.VMEM((slots, HD, width), jnp.bfloat16),
            pltpu.VMEM((slots, HD, width), jnp.bfloat16),
            stat,
            pltpu.VMEM((2, tokens + TILE, HD), jnp.bfloat16),
            pltpu.VMEM((pair, TILE), jnp.int32),
            pltpu.VMEM((pair, width), jnp.float32),
            pltpu.VMEM((pair, width), jnp.float32),
            pltpu.VMEM((pair, width), jnp.bfloat16),
            pltpu.VMEM((pair, width), jnp.bfloat16),
            pltpu.VMEM((pair, width), jnp.bfloat16),
            pltpu.VMEM((pair, width), jnp.bfloat16),
            pltpu.VMEM((most, pair, width), jnp.float32),
            pltpu.VMEM((most, 8, width), jnp.float32),
            stat,
            stat,
            stat,
            pltpu.VMEM((slots, HD, width), jnp.float32),
            pltpu.VMEM((2, tokens + TILE, HD), jnp.float32),
            pltpu.VMEM((rows, width), jnp.bfloat16),
            pltpu.VMEM((2, tokens, HD), jnp.bfloat16),
            pltpu.SemaphoreType.DMA((2 + max(2 * heads, tiles),)),
        ],
        compiler_params=pltpu.CompilerParams(vmem_limit_bytes=ATTENTION_LIMIT),
        cost_estimate=pl.CostEstimate(
            flops=rows * width * tokens * 3, bytes_accessed=12 << 20, transcendentals=0
        ),
    )(positions, docs, q.reshape(tiles, TILE, width), g.reshape(tiles, TILE, width), delta, kv)


def bring_kernel(
    team,
    planes,
    q_ref,
    g_ref,
    k_ref,
    v_ref,
    o_ref,
    q_out,
    g_out,
    delta_out,
    kv_out,
    kv_own,
    g_own,
    o_own,
    delta_own,
    load_sem,
    local_sem,
    flat_send,
    flat_recv,
    chain_send,
    chain_recv,
    core_send,
    core_recv,
):
    me = lax.axis_index("ctx")
    slot = me % team
    plane = me // team
    core = slot % 2
    mate = me + 1 - 2 * core
    width = q_out.shape[1]
    span = team * TILE
    tall = pl.ds(pl.multiple_of(slot * TILE, TILE), TILE)
    wide = pl.ds(pl.multiple_of(slot * width, HD), width)

    loads = [
        pltpu.make_async_copy(k_ref, kv_own.at[0], load_sem.at[0]),
        pltpu.make_async_copy(v_ref, kv_own.at[1], load_sem.at[1]),
        pltpu.make_async_copy(g_ref, g_own, load_sem.at[2]),
        pltpu.make_async_copy(o_ref, o_own, load_sem.at[3]),
    ]
    for load in loads:
        load.start()

    barrier = pltpu.get_barrier_semaphore()
    for shift in range(1, team):
        pl.semaphore_signal(
            barrier,
            inc=1,
            device_id=(plane * team + (slot + shift) % team, 0),
            device_id_type=MESH,
        )

    @pl.when(plane < planes - 1)
    def _():
        pl.semaphore_signal(barrier, inc=1, device_id=(me + team, 0), device_id_type=MESH)

    @pl.when(plane > 0)
    def _():
        pl.semaphore_signal(barrier, inc=1, device_id=(me - team, 0), device_id_type=MESH)

    near = jnp.where(plane < planes - 1, 1, 0) + jnp.where(plane > 0, 1, 0)
    pl.semaphore_wait(barrier, team - 1 + near)

    def flat(kind, shift, src, dst):
        return pltpu.make_async_remote_copy(
            src_ref=src,
            dst_ref=dst,
            send_sem=flat_send.at[kind, shift - 1],
            recv_sem=flat_recv.at[kind, slot],
            device_id=(plane * team + (slot + shift) % team, 0),
            device_id_type=MESH,
        )

    loads[0].wait()
    loads[1].wait()
    home = pl.ds(pl.multiple_of(me * TILE, TILE), TILE)
    flats = []
    for shift in range(1, team):
        other = (slot + shift) % team
        lanes = pl.ds(pl.multiple_of(other // 2 * HD, HD), HD)
        copy = flat(
            0, shift, kv_own.at[other % 2, :, lanes], kv_out.at[other % 2, home, :]
        )
        copy.start()
        flats.append(copy)
    locals_ = [
        pltpu.make_async_copy(
            kv_own.at[core, :, pl.ds(pl.multiple_of(slot // 2 * HD, HD), HD)],
            kv_out.at[core, home, :],
            local_sem.at[0],
        ),
        pltpu.make_async_copy(q_ref.at[:, wide], q_out.at[tall, :], local_sem.at[1]),
        pltpu.make_async_copy(g_ref.at[:, wide], g_out.at[tall, :], local_sem.at[2]),
    ]
    for copy in locals_:
        copy.start()
    rest = []
    for kind, (src, dst) in enumerate(((q_ref, q_out), (g_ref, g_out))):
        for shift in range(1, team):
            other = (slot + shift) % team
            lanes = pl.ds(pl.multiple_of(other * width, HD), width)
            copy = flat(1 + kind, shift, src.at[:, lanes], dst.at[tall, :])
            copy.start()
            rest.append(copy)
    locals_[0].wait()
    part_rows = span // SUB
    per_part = team // SUB

    def arrived(kind, source, dst):
        return pltpu.make_async_remote_copy(
            src_ref=dst,
            dst_ref=dst,
            send_sem=flat_send.at[kind, 0],
            recv_sem=flat_recv.at[kind, source],
            device_id=(mate, 0),
            device_id_type=MESH,
        )

    def part(which, sub):
        first = pl.multiple_of(which * span + sub * part_rows, TILE)
        return kv_out.at[core, pl.ds(first, part_rows), :]

    def chain(way, step, which, sub):
        return pltpu.make_async_remote_copy(
            src_ref=part(which, sub),
            dst_ref=part(which, sub),
            send_sem=chain_send.at[way, step, sub],
            recv_sem=chain_recv.at[way, step, sub],
            device_id=(me + team - 2 * way * team, 0),
            device_id_type=MESH,
        )

    def share(index, which, sub):
        return pltpu.make_async_remote_copy(
            src_ref=part(which, sub),
            dst_ref=part(which, sub),
            send_sem=core_send.at[index, sub],
            recv_sem=core_recv.at[index, sub],
            device_id=(mate, 0),
            device_id_type=MESH,
        )

    def up_ok(step):
        return (plane < planes - 1) & (plane - step >= 0)

    def down_ok(step):
        return (plane > 0) & (plane + step <= planes - 1)

    def up_come(step):
        return plane - 1 - step >= 0

    def down_come(step):
        return plane + 1 + step <= planes - 1

    for sub in range(SUB):
        for source in range(sub * per_part, (sub + 1) * per_part):
            @pl.when(slot != source)
            def _():
                arrived(0, source, kv_out.at[core, home, :]).wait_recv()

        @pl.when(up_ok(0))
        def _():
            chain(0, 0, plane, sub).start()

        @pl.when(down_ok(0))
        def _():
            chain(1, 0, plane, sub).start()

        share(0, plane, sub).start()

    loads[2].wait()
    loads[3].wait()
    for index in range(team):
        for head in range(width // HD):
            lanes = slice(index * width + head * HD, index * width + (head + 1) * HD)
            product = g_own[:, lanes].astype(jnp.float32) * o_own[:, lanes].astype(jnp.float32)
            row = jnp.sum(product.T, axis=0, keepdims=True)
            delta_own[index, :, head * HD : (head + 1) * HD] = jnp.broadcast_to(row, (8, HD))
    for shift in range(1, team):
        other = (slot + shift) % team
        copy = flat(3, shift, delta_own.at[other], delta_out.at[slot])
        copy.start()
        rest.append(copy)
    own_delta = pltpu.make_async_copy(delta_own.at[slot], delta_out.at[slot], local_sem.at[3])
    own_delta.start()

    for step in range(planes - 1):
        for sub in range(SUB):
            @pl.when(up_come(step))
            def _():
                chain(0, step, plane - 1 - step, sub).wait_recv()
                if step < planes - 2:
                    @pl.when(up_ok(step + 1))
                    def _():
                        chain(0, step + 1, plane - 1 - step, sub).start()
                share(1 + step, plane - 1 - step, sub).start()

            @pl.when(down_come(step))
            def _():
                chain(1, step, plane + 1 + step, sub).wait_recv()
                if step < planes - 2:
                    @pl.when(down_ok(step + 1))
                    def _():
                        chain(1, step + 1, plane + 1 + step, sub).start()
                share(planes + step, plane + 1 + step, sub).start()

    for sub in range(SUB):
        share(0, plane, sub).wait()
        for step in range(planes - 1):
            @pl.when(up_come(step))
            def _():
                share(1 + step, plane - 1 - step, sub).wait()

            @pl.when(down_come(step))
            def _():
                share(planes + step, plane + 1 + step, sub).wait()

            @pl.when(up_ok(step))
            def _():
                chain(0, step, plane - step, sub).wait_send()

            @pl.when(down_ok(step))
            def _():
                chain(1, step, plane + step, sub).wait_send()

    for copy in locals_[1:] + [own_delta]:
        copy.wait()
    for copy in rest + flats:
        copy.wait_send()
    for source in range(team):
        @pl.when(slot != source)
        def _():
            arrived(1, source, q_out.at[tall, :]).wait_recv()
            arrived(2, source, g_out.at[tall, :]).wait_recv()
            arrived(3, source, delta_out.at[slot]).wait_recv()


def bring(team, planes, queries, out_grad, key_states, value_states, outputs):
    rows, columns = queries.shape
    width = columns // team
    tokens = rows * team * planes
    vmem = pl.BlockSpec(memory_space=pltpu.VMEM)
    hbm = pl.BlockSpec(memory_space=pltpu.HBM)
    dma = pltpu.SemaphoreType.DMA
    return pl.pallas_call(
        functools.partial(bring_kernel, team, planes),
        out_shape=(
            jax.ShapeDtypeStruct((rows * team, width), jnp.bfloat16),
            jax.ShapeDtypeStruct((rows * team, width), jnp.bfloat16),
            jax.ShapeDtypeStruct((team, 8, width), jnp.float32),
            jax.ShapeDtypeStruct((2, tokens, HD), jnp.bfloat16),
        ),
        in_specs=[hbm, hbm, hbm, hbm, hbm],
        out_specs=(hbm, hbm, hbm, hbm),
        scratch_shapes=[
            pltpu.VMEM((2, rows, key_states.shape[1]), jnp.bfloat16),
            pltpu.VMEM((rows, columns), jnp.bfloat16),
            pltpu.VMEM((rows, columns), jnp.bfloat16),
            pltpu.VMEM((team, 8, width), jnp.float32),
            dma((4,)),
            dma((4,)),
            dma((4, team - 1)),
            dma((4, team)),
            dma((2, planes - 1, SUB)),
            dma((2, planes - 1, SUB)),
            dma((2 * planes - 1, SUB)),
            dma((2 * planes - 1, SUB)),
        ],
        compiler_params=pltpu.CompilerParams(
            collective_id=0, has_side_effects=True, vmem_limit_bytes=60 * 1024 * 1024
        ),
        cost_estimate=pl.CostEstimate(flops=0, bytes_accessed=60 << 20, transcendentals=0),
    )(queries, out_grad, key_states, value_states, outputs)


def return_kernel(
    team,
    planes,
    dq_ref,
    dkv_ref,
    dq_out,
    dkv_out,
    own,
    mate_in,
    chain_in,
    chain_own,
    total,
    local_sem,
    dq_send,
    dq_recv,
    flat_send,
    flat_recv,
    chain_send,
    chain_recv,
    core_send,
    core_recv,
):
    me = lax.axis_index("ctx")
    slot = me % team
    plane = me // team
    core = slot % 2
    mate = me + 1 - 2 * core
    width = dq_ref.shape[1]
    span = team * TILE
    part_rows = span // FINE
    per_part = team // FINE

    load = pltpu.make_async_copy(dkv_ref.at[core], own, local_sem.at[2])
    load.start()
    barrier = pltpu.get_barrier_semaphore()
    for shift in range(1, team):
        pl.semaphore_signal(
            barrier,
            inc=1,
            device_id=(plane * team + (slot + shift) % team, 0),
            device_id_type=MESH,
        )

    @pl.when(plane < planes - 1)
    def _():
        pl.semaphore_signal(barrier, inc=1, device_id=(me + team, 0), device_id_type=MESH)

    @pl.when(plane > 0)
    def _():
        pl.semaphore_signal(barrier, inc=1, device_id=(me - team, 0), device_id_type=MESH)

    near = jnp.where(plane < planes - 1, 1, 0) + jnp.where(plane > 0, 1, 0)
    pl.semaphore_wait(barrier, team - 1 + near)

    def rows_of(which, sub):
        return pl.ds(pl.multiple_of(which * span + sub * part_rows, TILE), part_rows)

    def inner(sub):
        return pl.ds(sub * part_rows, part_rows)

    def tile_rows(which):
        return pl.ds(pl.multiple_of(which * TILE, TILE), TILE)

    half = plane // (planes // 2)
    depth = plane * (1 - half) + (planes - 1 - plane) * half
    ahead = me + team * (1 - 2 * half)
    behind = me - team * (1 - 2 * half)

    def target_plane(index):
        return (planes - 1 - index) * (1 - half) + index * half

    shares = {}
    for index in range(planes):
        for sub in range(FINE):
            copy = pltpu.make_async_remote_copy(
                src_ref=dkv_ref.at[1 - core, rows_of(target_plane(index), sub), :],
                dst_ref=mate_in.at[index, inner(sub)],
                send_sem=core_send.at[index, sub],
                recv_sem=core_recv.at[index, sub],
                device_id=(mate, 0),
                device_id_type=MESH,
            )
            copy.start()
            shares[index, sub] = copy

    wide = pl.ds(pl.multiple_of(slot * width, HD), width)
    rest = []
    own_dq = pltpu.make_async_copy(
        dq_ref.at[tile_rows(slot), :], dq_out.at[:, wide], local_sem.at[0]
    )
    own_dq.start()
    for shift in range(1, team):
        other = (slot + shift) % team
        copy = pltpu.make_async_remote_copy(
            src_ref=dq_ref.at[tile_rows(other), :],
            dst_ref=dq_out.at[:, wide],
            send_sem=dq_send.at[shift - 1],
            recv_sem=dq_recv.at[shift - 1],
            device_id=(plane * team + other, 0),
            device_id_type=MESH,
        )
        copy.start()
        rest.append(copy)

    def chain(source, into, index, sub, device):
        return pltpu.make_async_remote_copy(
            src_ref=chain_own.at[source, index, inner(sub)],
            dst_ref=chain_in.at[into, index, inner(sub)],
            send_sem=chain_send.at[source, index, sub],
            recv_sem=chain_recv.at[into, index, sub],
            device_id=(device, 0),
            device_id_type=MESH,
        )

    def local_sum(index, sub):
        shares[index, sub].wait_recv()
        return own[rows_of(target_plane(index), sub), :].astype(jnp.float32) + mate_in[
            index, inner(sub)
        ].astype(jnp.float32)

    def come(way, index, sub):
        chain(0, way, index, sub, mate).wait_recv()
        return chain_in[way, index, inner(sub)].astype(jnp.float32)

    load.wait()
    lanes = pl.ds(pl.multiple_of(slot // 2 * HD, HD), HD)
    def flat(target):
        return pltpu.make_async_remote_copy(
            src_ref=total.at[tile_rows(target), :],
            dst_ref=dkv_out.at[core, :, lanes],
            send_sem=flat_send.at[target],
            recv_sem=flat_recv.at[slot],
            device_id=(plane * team + target, 0),
            device_id_type=MESH,
        )

    def finish(value, sub):
        total[inner(sub)] = value.astype(jnp.bfloat16)
        for target in range(sub * per_part, (sub + 1) * per_part):
            @pl.when(slot != target)
            def _():
                flat(target).start()

    pieces = [(index, sub) for index in range(planes - 1) for sub in range(FINE)]

    @pl.when(depth == 0)
    def _():
        moves = []
        for index, sub in pieces:
            chain_own[0, index, inner(sub)] = local_sum(index, sub).astype(jnp.bfloat16)
            if len(moves) >= FLIGHT:
                moves[-FLIGHT].wait_send()
            move = chain(0, 0, index, sub, ahead)
            move.start()
            moves.append(move)
        for sub in range(FINE):
            finish(local_sum(planes - 1, sub) + come(1, 0, sub), sub)
        for move in moves[-FLIGHT:]:
            move.wait_send()

    @pl.when(depth == 1)
    def _():
        moves = []
        near = [(0, 0, index, sub) for index in range(2) for sub in range(FINE)]
        far = [(1, 1, 0, sub) for sub in range(FINE)]
        line = near[:FINE]
        for step in range(FINE):
            line.extend((far[step], near[FINE + step]))
        for way, source, index, sub in line:
            share = planes - 1 if way else index
            chain_own[source, index, inner(sub)] = (
                local_sum(share, sub) + come(way, index, sub)
            ).astype(jnp.bfloat16)
            move = chain(source, 1, index, sub, behind if way else ahead)
            move.start()
            moves.append(move)
        for sub in range(FINE):
            finish(local_sum(2, sub) + come(1, 1, sub) + come(0, 2, sub), sub)
        for move in moves:
            move.wait_send()

    own_dkv = pltpu.make_async_copy(
        total.at[tile_rows(slot), :], dkv_out.at[core, :, lanes], local_sem.at[1]
    )
    own_dkv.start()
    own_dq.wait()
    own_dkv.wait()
    for copy in shares.values():
        copy.wait_send()
    for copy in rest:
        copy.wait()
    for target in range(team):
        @pl.when(slot != target)
        def _():
            flat(target).wait_send()
            pltpu.make_async_remote_copy(
                src_ref=total.at[tile_rows(slot), :],
                dst_ref=dkv_out.at[core, :, lanes],
                send_sem=flat_send.at[target],
                recv_sem=flat_recv.at[target],
                device_id=(mate, 0),
                device_id_type=MESH,
            ).wait_recv()


def give_back(team, planes, dq, dkv):
    tall, width = dq.shape
    rows = tall // team
    heads = team // 2
    hbm = pl.BlockSpec(memory_space=pl.ANY)
    dma = pltpu.SemaphoreType.DMA
    part = pltpu.VMEM((2, planes - 1, tall, HD), jnp.bfloat16)
    return pl.pallas_call(
        functools.partial(return_kernel, team, planes),
        out_shape=(
            jax.ShapeDtypeStruct((rows, width * team), jnp.bfloat16),
            jax.ShapeDtypeStruct((2, rows, heads * HD), jnp.bfloat16),
        ),
        in_specs=[hbm, hbm],
        out_specs=(hbm, hbm),
        scratch_shapes=[
            pltpu.VMEM((planes * tall, HD), jnp.bfloat16),
            pltpu.VMEM((planes, tall, HD), jnp.bfloat16),
            part,
            part,
            pltpu.VMEM((tall, HD), jnp.bfloat16),
            dma((3,)),
            dma((team - 1,)),
            dma((team - 1,)),
            dma((team,)),
            dma((team,)),
            dma((2, planes - 1, FINE)),
            dma((2, planes - 1, FINE)),
            dma((planes, FINE)),
            dma((planes, FINE)),
        ],
        compiler_params=pltpu.CompilerParams(
            collective_id=1, has_side_effects=True, vmem_limit_bytes=GIVE_LIMIT
        ),
        cost_estimate=pl.CostEstimate(flops=0, bytes_accessed=60 << 20, transcendentals=0),
    )(dq, dkv)


def local_planes(queries, key_states, value_states, outputs, out_grad, doc_of_tile, tile_position):
    team = 2 * (key_states.shape[1] // HD)
    planes = lax.axis_size("ctx") // team
    q, g, delta, kv = bring(team, planes, queries, out_grad, key_states, value_states, outputs)
    dq, dkv = attention_backward(tile_position, doc_of_tile, team, q, g, delta, kv)
    dq, dkv = give_back(team, planes, dq, dkv)
    return dq, dkv[0], dkv[1]


def local_any(queries, key_states, value_states, outputs, out_grad, doc_of_tile, tile_position):
    rows = queries.shape[0]
    kv_heads = key_states.shape[1] // HD
    head_count = lax.axis_size("head")
    ctx_count = lax.axis_size("ctx")
    ctx_index = lax.axis_index("ctx")
    split = kv_heads * head_count
    team = kv_heads
    parts = ctx_count // team
    near = [[b * team + s for s in range(team)] for b in range(parts)]
    far = [[b * team + s for b in range(parts)] for s in range(team)]

    def swap(value, split_axis, concat_axis):
        if head_count > 1:
            return lax.all_to_all(value, "head", split_axis, concat_axis, tiled=True)
        return lax.all_to_all(
            value, "ctx", split_axis, concat_axis, axis_index_groups=near, tiled=True
        )

    heads = queries.shape[1] // split // HD
    products = out_grad.astype(jnp.float32) * outputs.astype(jnp.float32)
    delta = jnp.sum(products.reshape(rows, split * heads, HD), axis=-1)
    kv = jnp.concatenate([key_states, value_states], axis=1)
    if head_count == 1:
        kv = kv.reshape(rows, 2, team, HD).transpose(0, 2, 1, 3).reshape(rows, team * 2 * HD)
        kv = swap(kv, 1, 0)
    kv = lax.all_gather(kv, "ctx", axis=0, tiled=True, axis_index_groups=far)
    kv = kv.reshape(-1, 2, HD).transpose(1, 0, 2)
    qd = jnp.concatenate(
        [
            queries.reshape(rows, split, heads * HD),
            out_grad.reshape(rows, split, heads * HD),
        ],
        axis=2,
    ).reshape(rows, split * 2 * heads * HD)
    qd = swap(qd, 1, 0)
    delta = swap(delta, 1, 0)
    tiles = qd.shape[0] // TILE
    delta = jnp.transpose(delta.reshape(tiles, TILE, heads), (0, 2, 1)).reshape(
        tiles, 1, heads * TILE
    )
    delta = jnp.broadcast_to(delta, (tiles, 8, heads * TILE))
    width = heads * HD
    dq, dkv = attention_backward(
        tile_position, doc_of_tile, team, qd[:, :width], qd[:, width:], delta, kv
    )
    if head_count == 1:
        dq = swap(dq, 0, 1)
    dkv = dkv.transpose(1, 0, 2).reshape(-1, 2 * HD)
    dkv = lax.all_to_all(dkv, "ctx", 0, 0, axis_index_groups=far, tiled=True)
    dkv = jnp.sum(dkv.reshape(parts, -1, 2 * HD).astype(jnp.float32), axis=0).astype(jnp.bfloat16)
    if head_count == 1:
        dkv = swap(dkv, 0, 1)
    dkv = dkv.reshape(dkv.shape[0], kv_heads, 2, HD)
    return (
        dq,
        dkv[:, :, 0].reshape(-1, kv_heads * HD),
        dkv[:, :, 1].reshape(-1, kv_heads * HD),
    )


def solution(mesh):
    placed = (
        P(("ctx", "head"), None),
        P("ctx", "head"),
        P("ctx", "head"),
        P(("ctx", "head"), None),
        P(("ctx", "head"), None),
        P(),
        P(),
    )
    slabs = mesh.shape["head"] == 1 and mesh.shape["ctx"] == 32
    return jax.shard_map(
        local_planes if slabs else local_any,
        mesh=mesh,
        in_specs=placed,
        out_specs=(P("ctx", "head"), P("ctx", "head"), P("ctx", "head")),
        check_vma=False,
    )
```

```python
import functools

import jax
import jax.numpy as jnp
from jax import lax
from jax.experimental import pallas as pl
from jax.experimental.pallas import tpu as pltpu
from jax.sharding import PartitionSpec as P

HD = 128
TILE = 128
SPAN = 2
LOW = -1e30
LOG2E = 1.4426950408889634
DEEP = 4
SUB = 2
FINE = 4
FLIGHT = 2
GIVE_LIMIT = 52 * 1024 * 1024
ATTENTION_LIMIT = 56 * 1024 * 1024
MESH = pl.DeviceIdType.MESH


def attention_kernel(
    heads,
    tiles,
    team,
    position_ref,
    doc_ref,
    q_hbm,
    g_hbm,
    delta_hbm,
    kv_hbm,
    dq_ref,
    dkv_ref,
    start_ref,
    item_tile,
    item_first,
    item_bound,
    q_rows,
    g_rows,
    q_cols,
    g_cols,
    delta_ref,
    kv_ref,
    gap_ref,
    scores_a,
    scores_b,
    low_a,
    low_b,
    grad_a,
    grad_b,
    probs_buf,
    top_buf,
    top_ref,
    total_ref,
    share_ref,
    dq_acc,
    dkv_acc,
    dq_own,
    dkv_own,
    sems,
):
    width = heads * HD
    scale = HD ** (-0.5)
    pair = SPAN * TILE
    count = position_ref.shape[0]
    block = lax.axis_index("ctx") // team

    def tile_at(index):
        return pl.ds(pl.multiple_of(index * TILE, TILE), TILE)

    heads_in = []
    for h in range(heads):
        lanes = slice(h * HD, (h + 1) * HD)
        for which, (src, dst) in enumerate(((q_hbm, q_rows), (g_hbm, g_rows))):
            copy = pltpu.make_async_copy(
                src.at[:, :, lanes], dst.at[0:tiles, h], sems.at[2 + 2 * h + which]
            )
            copy.start()
            heads_in.append(copy)
    delta_in = pltpu.make_async_copy(delta_hbm, delta_ref.at[0:tiles], sems.at[0])
    delta_in.start()

    @pl.loop(0, count)
    def _(spot):
        place = position_ref[spot]
        for which in range(2):
            pltpu.make_async_copy(
                kv_hbm.at[which, tile_at(spot), :],
                kv_ref.at[which, tile_at(place), :],
                sems.at[1],
            ).start()

    def find(index, start):
        fresh = doc_ref[index] != doc_ref[jnp.maximum(index - 1, 0)]
        start = jnp.where(fresh, index, start)
        start_ref[index] = start
        return start

    lax.fori_loop(0, count, find, jnp.int32(0))

    def put(index, tile, first, bound):
        item_tile[index] = tile
        item_first[index] = first
        item_bound[index] = bound

    def listed(tile, total):
        place = position_ref[block * tiles + tile]
        start = start_ref[place]
        full = (place - start) // 2
        put(tile, tile, start + 2 * full, (place - start - 2 * full) * TILE)

        @pl.loop(0, full)
        def _(step):
            put(total + step, tile, start + 2 * step, pair)

        return total + full

    items = lax.fori_loop(0, tiles, listed, jnp.int32(tiles))
    for extra in range(4):
        put(items + extra, tiles, 0, pair)

    gap_ref[...] = lax.broadcasted_iota(jnp.int32, (pair, TILE), 0) - lax.broadcasted_iota(
        jnp.int32, (pair, TILE), 1
    )
    dkv_acc[...] = jnp.zeros_like(dkv_acc)
    dq_acc[...] = jnp.zeros_like(dq_acc)
    top_ref[...] = jnp.full_like(top_ref, LOW)
    total_ref[...] = jnp.zeros_like(total_ref)
    q_cols[tiles] = jnp.zeros((HD, width), jnp.bfloat16)
    g_cols[tiles] = jnp.zeros((HD, width), jnp.bfloat16)
    q_rows[tiles] = jnp.zeros((heads, TILE, HD), jnp.bfloat16)
    g_rows[tiles] = jnp.zeros((heads, TILE, HD), jnp.bfloat16)
    delta_ref[tiles] = jnp.zeros((1, width), jnp.float32)
    kv_ref[:, count * TILE :, :] = jnp.zeros((2, TILE, HD), jnp.bfloat16)
    low_b[...] = jnp.zeros_like(low_b)
    grad_b[...] = jnp.zeros_like(grad_b)

    for copy in heads_in:
        copy.wait()

    @pl.loop(0, tiles)
    def _(tile):
        for h in range(heads):
            lanes = slice(h * HD, (h + 1) * HD)
            q_cols[tile, :, lanes] = q_rows[tile, h].T
            g_cols[tile, :, lanes] = g_rows[tile, h].T

    delta_in.wait()
    pltpu.make_async_copy(kv_hbm, kv_ref.at[:, 0 : count * TILE], sems.at[1]).wait()

    def groups(value):
        return value.reshape(value.shape[0] // 8, 8, width)

    def area(index):
        return pl.ds(pl.multiple_of(item_first[index] * TILE, TILE), pair)

    def score(index, into):
        into[...] = jnp.dot(
            kv_ref[0, area(index), :],
            q_cols[item_tile[index]],
            preferred_element_type=jnp.float32,
        )

    def weigh(index, source, edge):
        tile = item_tile[index]
        scores = source[...] * (scale * LOG2E)
        if edge:
            gap = jnp.concatenate([gap_ref[...]] * heads, axis=1)
            scores = jnp.where(gap <= item_bound[index], scores, LOW)
        scores = groups(scores)
        old = top_ref[tile]
        top = jnp.maximum(old, jnp.max(scores, axis=0))
        probs = jnp.exp2(scores - top[None])
        probs_buf[index] = probs.reshape(pair, width)
        top_buf[index] = top
        top_ref[tile] = top
        total_ref[tile] = total_ref[tile] * jnp.exp2(old - top) + jnp.sum(probs, axis=0)

    score(0, scores_a)

    def weigh_two(index, edge=False):
        score(index + 1, scores_b)
        weigh(index, scores_a, edge)
        score(index + 2, scores_a)
        weigh(index + 1, scores_b, edge)

    edges = (tiles + 1) // 2
    rounds = (items + 1) // 2
    for part in range(edges):
        weigh_two(2 * part, edge=True)
    deep = edges + (rounds - edges) // DEEP * DEEP

    @pl.loop(0, (rounds - edges) // DEEP)
    def _(step):
        for part in range(DEEP):
            weigh_two(2 * (edges + DEEP * step + part))

    @pl.loop(deep, rounds)
    def _(step):
        weigh_two(2 * step)

    for tile in range(tiles):
        top = top_ref[tile]
        peak = jnp.broadcast_to(jnp.max(top, axis=0, keepdims=True), (8, width))
        total = jnp.sum(total_ref[tile] * jnp.exp2(top - peak), axis=0, keepdims=True)
        top_ref[tile] = peak
        share_ref[tile] = 1.0 / jnp.broadcast_to(total, (8, width))
    top_ref[tiles] = jnp.zeros((8, width), jnp.float32)
    share_ref[tiles] = jnp.zeros((8, width), jnp.float32)
    for extra in range(2):
        probs_buf[items + extra] = jnp.zeros((pair, width), jnp.float32)
        top_buf[items + extra] = jnp.zeros((8, width), jnp.float32)

    def value_scores(index, into):
        into[...] = jnp.dot(
            kv_ref[1, area(index), :],
            g_cols[item_tile[index]],
            preferred_element_type=jnp.float32,
        )

    def combine(index, source, low, grad):
        tile = item_tile[index]
        factor = jnp.exp2(top_buf[index] - top_ref[tile]) * share_ref[tile]
        probs = groups(probs_buf[index]) * factor[None]
        low[...] = probs.reshape(pair, width).astype(jnp.bfloat16)
        grad[...] = (
            (probs * (groups(source[...]) - delta_ref[tile][None]) * scale)
            .reshape(pair, width)
            .astype(jnp.bfloat16)
        )

    def add(index, low, grad):
        tile = item_tile[index]
        spot = area(index)
        dkv_acc[1, spot, :] += jnp.dot(
            low[...], g_rows[tile].reshape(width, HD), preferred_element_type=jnp.float32
        )
        dkv_acc[0, spot, :] += jnp.dot(
            grad[...], q_rows[tile].reshape(width, HD), preferred_element_type=jnp.float32
        )
        dq_acc[tile] += lax.dot_general(
            kv_ref[0, spot, :],
            grad[...],
            (((0,), (0,)), ((), ())),
            preferred_element_type=jnp.float32,
        )

    value_scores(0, scores_a)

    def add_two(index):
        value_scores(index + 1, scores_b)
        add(jnp.where(index == 0, items, index - 1), low_b, grad_b)
        combine(index, scores_a, low_a, grad_a)
        value_scores(index + 2, scores_a)
        add(index, low_a, grad_a)
        combine(index + 1, scores_b, low_b, grad_b)

    turns = (items + 2) // 2

    @pl.loop(0, turns // DEEP)
    def _(step):
        for part in range(DEEP):
            add_two(2 * (DEEP * step + part))

    @pl.loop(turns // DEEP * DEEP, turns)
    def _(step):
        add_two(2 * step)

    outs = [pltpu.make_async_copy(dkv_own.at[w], dkv_ref.at[w], sems.at[w]) for w in range(2)]
    for which in range(2):
        @pl.loop(0, count, unroll=4)
        def _(spot):
            place = position_ref[spot]
            dkv_own[which, tile_at(spot), :] = dkv_acc[which, tile_at(place), :].astype(
                jnp.bfloat16
            )

        outs[which].start()

    for tile in range(tiles):
        rows = slice(tile * TILE, (tile + 1) * TILE)
        for h in range(heads):
            lanes = slice(h * HD, (h + 1) * HD)
            dq_own[rows, lanes] = dq_acc[tile, :, lanes].T.astype(jnp.bfloat16)
        copy = pltpu.make_async_copy(dq_own.at[rows], dq_ref.at[rows], sems.at[2 + tile])
        copy.start()
        outs.append(copy)
    for copy in outs:
        copy.wait()


def attention_backward(positions, docs, team, q, g, delta, kv):
    rows, width = q.shape
    heads = width // HD
    tokens = kv.shape[1]
    tiles = rows // TILE
    count = tokens // TILE
    longest = count // 2
    most = sum((longest - i + 1) // 2 for i in range(min(tiles, longest)))
    most = max(most, tiles) + 4
    pair = SPAN * TILE
    smem = pl.BlockSpec(memory_space=pltpu.SMEM)
    hbm = pl.BlockSpec(memory_space=pl.ANY)
    slots = tiles + 1
    stat = pltpu.VMEM((slots, 8, width), jnp.float32)
    return pl.pallas_call(
        functools.partial(attention_kernel, heads, tiles, team),
        out_shape=(
            jax.ShapeDtypeStruct((rows, width), jnp.bfloat16),
            jax.ShapeDtypeStruct((2, tokens, HD), jnp.bfloat16),
        ),
        in_specs=[smem, smem, hbm, hbm, hbm, hbm],
        out_specs=(hbm, hbm),
        scratch_shapes=[
            pltpu.SMEM((count,), jnp.int32),
            pltpu.SMEM((most,), jnp.int32),
            pltpu.SMEM((most,), jnp.int32),
            pltpu.SMEM((most,), jnp.int32),
            pltpu.VMEM((slots, heads, TILE, HD), jnp.bfloat16),
            pltpu.VMEM((slots, heads, TILE, HD), jnp.bfloat16),
            pltpu.VMEM((slots, HD, width), jnp.bfloat16),
            pltpu.VMEM((slots, HD, width), jnp.bfloat16),
            pltpu.VMEM((slots, 1, width), jnp.float32),
            pltpu.VMEM((2, tokens + TILE, HD), jnp.bfloat16),
            pltpu.VMEM((pair, TILE), jnp.int32),
            pltpu.VMEM((pair, width), jnp.float32),
            pltpu.VMEM((pair, width), jnp.float32),
            pltpu.VMEM((pair, width), jnp.bfloat16),
            pltpu.VMEM((pair, width), jnp.bfloat16),
            pltpu.VMEM((pair, width), jnp.bfloat16),
            pltpu.VMEM((pair, width), jnp.bfloat16),
            pltpu.VMEM((most, pair, width), jnp.float32),
            pltpu.VMEM((most, 8, width), jnp.float32),
            stat,
            stat,
            stat,
            pltpu.VMEM((slots, HD, width), jnp.float32),
            pltpu.VMEM((2, tokens + TILE, HD), jnp.float32),
            pltpu.VMEM((rows, width), jnp.bfloat16),
            pltpu.VMEM((2, tokens, HD), jnp.bfloat16),
            pltpu.SemaphoreType.DMA((2 + max(2 * heads, tiles),)),
        ],
        compiler_params=pltpu.CompilerParams(vmem_limit_bytes=ATTENTION_LIMIT),
        cost_estimate=pl.CostEstimate(
            flops=rows * width * tokens * 3, bytes_accessed=12 << 20, transcendentals=0
        ),
    )(positions, docs, q.reshape(tiles, TILE, width), g.reshape(tiles, TILE, width), delta, kv)


def bring_kernel(
    team,
    planes,
    q_ref,
    g_ref,
    k_ref,
    v_ref,
    o_ref,
    q_out,
    g_out,
    delta_out,
    kv_out,
    kv_own,
    g_own,
    o_own,
    delta_own,
    load_sem,
    local_sem,
    flat_send,
    flat_recv,
    chain_send,
    chain_recv,
    core_send,
    core_recv,
):
    me = lax.axis_index("ctx")
    slot = me % team
    plane = me // team
    core = slot % 2
    mate = me + 1 - 2 * core
    width = q_out.shape[1]
    span = team * TILE
    tall = pl.ds(pl.multiple_of(slot * TILE, TILE), TILE)
    wide = pl.ds(pl.multiple_of(slot * width, HD), width)

    loads = [
        pltpu.make_async_copy(k_ref, kv_own.at[0], load_sem.at[0]),
        pltpu.make_async_copy(v_ref, kv_own.at[1], load_sem.at[1]),
        pltpu.make_async_copy(g_ref, g_own, load_sem.at[2]),
        pltpu.make_async_copy(o_ref, o_own, load_sem.at[3]),
    ]
    for load in loads:
        load.start()

    barrier = pltpu.get_barrier_semaphore()
    for shift in range(1, team):
        pl.semaphore_signal(
            barrier,
            inc=1,
            device_id=(plane * team + (slot + shift) % team, 0),
            device_id_type=MESH,
        )

    @pl.when(plane < planes - 1)
    def _():
        pl.semaphore_signal(barrier, inc=1, device_id=(me + team, 0), device_id_type=MESH)

    @pl.when(plane > 0)
    def _():
        pl.semaphore_signal(barrier, inc=1, device_id=(me - team, 0), device_id_type=MESH)

    near = jnp.where(plane < planes - 1, 1, 0) + jnp.where(plane > 0, 1, 0)
    pl.semaphore_wait(barrier, team - 1 + near)

    def flat(kind, shift, src, dst):
        return pltpu.make_async_remote_copy(
            src_ref=src,
            dst_ref=dst,
            send_sem=flat_send.at[kind, shift - 1],
            recv_sem=flat_recv.at[kind, slot],
            device_id=(plane * team + (slot + shift) % team, 0),
            device_id_type=MESH,
        )

    loads[0].wait()
    loads[1].wait()
    home = pl.ds(pl.multiple_of(me * TILE, TILE), TILE)
    flats = []
    for shift in range(1, team):
        other = (slot + shift) % team
        lanes = pl.ds(pl.multiple_of(other // 2 * HD, HD), HD)
        copy = flat(
            0, shift, kv_own.at[other % 2, :, lanes], kv_out.at[other % 2, home, :]
        )
        copy.start()
        flats.append(copy)
    locals_ = [
        pltpu.make_async_copy(
            kv_own.at[core, :, pl.ds(pl.multiple_of(slot // 2 * HD, HD), HD)],
            kv_out.at[core, home, :],
            local_sem.at[0],
        ),
        pltpu.make_async_copy(q_ref.at[:, wide], q_out.at[tall, :], local_sem.at[1]),
        pltpu.make_async_copy(g_ref.at[:, wide], g_out.at[tall, :], local_sem.at[2]),
    ]
    for copy in locals_:
        copy.start()
    rest = []
    for kind, (src, dst) in enumerate(((q_ref, q_out), (g_ref, g_out))):
        for shift in range(1, team):
            other = (slot + shift) % team
            lanes = pl.ds(pl.multiple_of(other * width, HD), width)
            copy = flat(1 + kind, shift, src.at[:, lanes], dst.at[tall, :])
            copy.start()
            rest.append(copy)
    locals_[0].wait()
    part_rows = span // SUB
    per_part = team // SUB

    def arrived(kind, source, dst):
        return pltpu.make_async_remote_copy(
            src_ref=dst,
            dst_ref=dst,
            send_sem=flat_send.at[kind, 0],
            recv_sem=flat_recv.at[kind, source],
            device_id=(mate, 0),
            device_id_type=MESH,
        )

    def part(which, sub):
        first = pl.multiple_of(which * span + sub * part_rows, TILE)
        return kv_out.at[core, pl.ds(first, part_rows), :]

    def chain(way, step, which, sub):
        return pltpu.make_async_remote_copy(
            src_ref=part(which, sub),
            dst_ref=part(which, sub),
            send_sem=chain_send.at[way, step, sub],
            recv_sem=chain_recv.at[way, step, sub],
            device_id=(me + team - 2 * way * team, 0),
            device_id_type=MESH,
        )

    def share(index, which, sub):
        return pltpu.make_async_remote_copy(
            src_ref=part(which, sub),
            dst_ref=part(which, sub),
            send_sem=core_send.at[index, sub],
            recv_sem=core_recv.at[index, sub],
            device_id=(mate, 0),
            device_id_type=MESH,
        )

    def up_ok(step):
        return (plane < planes - 1) & (plane - step >= 0)

    def down_ok(step):
        return (plane > 0) & (plane + step <= planes - 1)

    def up_come(step):
        return plane - 1 - step >= 0

    def down_come(step):
        return plane + 1 + step <= planes - 1

    for sub in range(SUB):
        for source in range(sub * per_part, (sub + 1) * per_part):
            @pl.when(slot != source)
            def _():
                arrived(0, source, kv_out.at[core, home, :]).wait_recv()

        @pl.when(up_ok(0))
        def _():
            chain(0, 0, plane, sub).start()

        @pl.when(down_ok(0))
        def _():
            chain(1, 0, plane, sub).start()

        share(0, plane, sub).start()

    loads[2].wait()
    loads[3].wait()
    for index in range(team):
        for head in range(width // HD):
            lanes = slice(index * width + head * HD, index * width + (head + 1) * HD)
            product = g_own[:, lanes].astype(jnp.float32) * o_own[:, lanes].astype(jnp.float32)
            row = jnp.sum(product.T, axis=0, keepdims=True)
            delta_own[index, :, head * HD : (head + 1) * HD] = row
    for shift in range(1, team):
        other = (slot + shift) % team
        copy = flat(3, shift, delta_own.at[other], delta_out.at[slot])
        copy.start()
        rest.append(copy)
    own_delta = pltpu.make_async_copy(delta_own.at[slot], delta_out.at[slot], local_sem.at[3])
    own_delta.start()

    for step in range(planes - 1):
        for sub in range(SUB):
            @pl.when(up_come(step))
            def _():
                chain(0, step, plane - 1 - step, sub).wait_recv()
                if step < planes - 2:
                    @pl.when(up_ok(step + 1))
                    def _():
                        chain(0, step + 1, plane - 1 - step, sub).start()
                share(1 + step, plane - 1 - step, sub).start()

            @pl.when(down_come(step))
            def _():
                chain(1, step, plane + 1 + step, sub).wait_recv()
                if step < planes - 2:
                    @pl.when(down_ok(step + 1))
                    def _():
                        chain(1, step + 1, plane + 1 + step, sub).start()
                share(planes + step, plane + 1 + step, sub).start()

    for sub in range(SUB):
        share(0, plane, sub).wait()
        for step in range(planes - 1):
            @pl.when(up_come(step))
            def _():
                share(1 + step, plane - 1 - step, sub).wait()

            @pl.when(down_come(step))
            def _():
                share(planes + step, plane + 1 + step, sub).wait()

            @pl.when(up_ok(step))
            def _():
                chain(0, step, plane - step, sub).wait_send()

            @pl.when(down_ok(step))
            def _():
                chain(1, step, plane + step, sub).wait_send()

    for copy in locals_[1:] + [own_delta]:
        copy.wait()
    for copy in rest + flats:
        copy.wait_send()
    for source in range(team):
        @pl.when(slot != source)
        def _():
            arrived(1, source, q_out.at[tall, :]).wait_recv()
            arrived(2, source, g_out.at[tall, :]).wait_recv()
            arrived(3, source, delta_out.at[slot]).wait_recv()


def bring(team, planes, queries, out_grad, key_states, value_states, outputs):
    rows, columns = queries.shape
    width = columns // team
    tokens = rows * team * planes
    vmem = pl.BlockSpec(memory_space=pltpu.VMEM)
    hbm = pl.BlockSpec(memory_space=pltpu.HBM)
    dma = pltpu.SemaphoreType.DMA
    return pl.pallas_call(
        functools.partial(bring_kernel, team, planes),
        out_shape=(
            jax.ShapeDtypeStruct((rows * team, width), jnp.bfloat16),
            jax.ShapeDtypeStruct((rows * team, width), jnp.bfloat16),
            jax.ShapeDtypeStruct((team, 1, width), jnp.float32),
            jax.ShapeDtypeStruct((2, tokens, HD), jnp.bfloat16),
        ),
        in_specs=[hbm, hbm, hbm, hbm, hbm],
        out_specs=(hbm, hbm, hbm, hbm),
        scratch_shapes=[
            pltpu.VMEM((2, rows, key_states.shape[1]), jnp.bfloat16),
            pltpu.VMEM((rows, columns), jnp.bfloat16),
            pltpu.VMEM((rows, columns), jnp.bfloat16),
            pltpu.VMEM((team, 1, width), jnp.float32),
            dma((4,)),
            dma((4,)),
            dma((4, team - 1)),
            dma((4, team)),
            dma((2, planes - 1, SUB)),
            dma((2, planes - 1, SUB)),
            dma((2 * planes - 1, SUB)),
            dma((2 * planes - 1, SUB)),
        ],
        compiler_params=pltpu.CompilerParams(
            collective_id=0, has_side_effects=True, vmem_limit_bytes=60 * 1024 * 1024
        ),
        cost_estimate=pl.CostEstimate(flops=0, bytes_accessed=60 << 20, transcendentals=0),
    )(queries, out_grad, key_states, value_states, outputs)


def return_kernel(
    team,
    planes,
    dq_ref,
    dkv_ref,
    dq_out,
    dkv_out,
    own,
    mate_in,
    chain_in,
    chain_own,
    total,
    local_sem,
    dq_send,
    dq_recv,
    flat_send,
    flat_recv,
    chain_send,
    chain_recv,
    core_send,
    core_recv,
):
    me = lax.axis_index("ctx")
    slot = me % team
    plane = me // team
    core = slot % 2
    mate = me + 1 - 2 * core
    width = dq_ref.shape[1]
    span = team * TILE
    part_rows = span // FINE
    per_part = team // FINE

    load = pltpu.make_async_copy(dkv_ref.at[core], own, local_sem.at[2])
    load.start()
    barrier = pltpu.get_barrier_semaphore()
    for shift in range(1, team):
        pl.semaphore_signal(
            barrier,
            inc=1,
            device_id=(plane * team + (slot + shift) % team, 0),
            device_id_type=MESH,
        )

    @pl.when(plane < planes - 1)
    def _():
        pl.semaphore_signal(barrier, inc=1, device_id=(me + team, 0), device_id_type=MESH)

    @pl.when(plane > 0)
    def _():
        pl.semaphore_signal(barrier, inc=1, device_id=(me - team, 0), device_id_type=MESH)

    near = jnp.where(plane < planes - 1, 1, 0) + jnp.where(plane > 0, 1, 0)
    pl.semaphore_wait(barrier, team - 1 + near)

    def rows_of(which, sub):
        return pl.ds(pl.multiple_of(which * span + sub * part_rows, TILE), part_rows)

    def inner(sub):
        return pl.ds(sub * part_rows, part_rows)

    def tile_rows(which):
        return pl.ds(pl.multiple_of(which * TILE, TILE), TILE)

    half = plane // (planes // 2)
    depth = plane * (1 - half) + (planes - 1 - plane) * half
    ahead = me + team * (1 - 2 * half)
    behind = me - team * (1 - 2 * half)

    def target_plane(index):
        return (planes - 1 - index) * (1 - half) + index * half

    shares = {}
    for index in range(planes):
        for sub in range(FINE):
            copy = pltpu.make_async_remote_copy(
                src_ref=dkv_ref.at[1 - core, rows_of(target_plane(index), sub), :],
                dst_ref=mate_in.at[index, inner(sub)],
                send_sem=core_send.at[index, sub],
                recv_sem=core_recv.at[index, sub],
                device_id=(mate, 0),
                device_id_type=MESH,
            )
            shares[index, sub] = copy
    for sub in range(FINE):
        shares[0, sub].start()

    wide = pl.ds(pl.multiple_of(slot * width, HD), width)
    rest = []
    own_dq = pltpu.make_async_copy(
        dq_ref.at[tile_rows(slot), :], dq_out.at[:, wide], local_sem.at[0]
    )
    own_dq.start()
    for shift in range(1, team):
        other = (slot + shift) % team
        copy = pltpu.make_async_remote_copy(
            src_ref=dq_ref.at[tile_rows(other), :],
            dst_ref=dq_out.at[:, wide],
            send_sem=dq_send.at[shift - 1],
            recv_sem=dq_recv.at[shift - 1],
            device_id=(plane * team + other, 0),
            device_id_type=MESH,
        )
        copy.start()
        rest.append(copy)

    def chain(source, into, index, sub, device):
        return pltpu.make_async_remote_copy(
            src_ref=chain_own.at[source, index, inner(sub)],
            dst_ref=chain_in.at[into, index, inner(sub)],
            send_sem=chain_send.at[source, index, sub],
            recv_sem=chain_recv.at[into, index, sub],
            device_id=(device, 0),
            device_id_type=MESH,
        )

    def local_sum(index, sub):
        shares[index, sub].wait_recv()
        return own[rows_of(target_plane(index), sub), :].astype(jnp.float32) + mate_in[
            index, inner(sub)
        ].astype(jnp.float32)

    def come(way, index, sub):
        chain(0, way, index, sub, mate).wait_recv()
        return chain_in[way, index, inner(sub)].astype(jnp.float32)

    load.wait()
    for sub in range(FINE):
        shares[0, sub].wait_send()
    for index in (planes - 1, *range(1, planes - 1)):
        for sub in range(FINE):
            shares[index, sub].start()
    lanes = pl.ds(pl.multiple_of(slot // 2 * HD, HD), HD)
    def flat(target):
        return pltpu.make_async_remote_copy(
            src_ref=total.at[tile_rows(target), :],
            dst_ref=dkv_out.at[core, :, lanes],
            send_sem=flat_send.at[target],
            recv_sem=flat_recv.at[slot],
            device_id=(plane * team + target, 0),
            device_id_type=MESH,
        )

    def finish(value, sub):
        total[inner(sub)] = value.astype(jnp.bfloat16)
        for target in range(sub * per_part, (sub + 1) * per_part):
            @pl.when(slot != target)
            def _():
                flat(target).start()

    pieces = [(index, sub) for index in range(planes - 1) for sub in range(FINE)]

    @pl.when(depth == 0)
    def _():
        moves = []
        for index, sub in pieces:
            chain_own[0, index, inner(sub)] = local_sum(index, sub).astype(jnp.bfloat16)
            if len(moves) >= FLIGHT:
                moves[-FLIGHT].wait_send()
            move = chain(0, 0, index, sub, ahead)
            move.start()
            moves.append(move)
        for sub in range(FINE):
            finish(local_sum(planes - 1, sub) + come(1, 0, sub), sub)
        for move in moves[-FLIGHT:]:
            move.wait_send()

    @pl.when(depth == 1)
    def _():
        moves = []
        near = [(0, 0, index, sub) for index in range(2) for sub in range(FINE)]
        far = [(1, 1, 0, sub) for sub in range(FINE)]
        line = near[:FINE]
        for step in range(FINE):
            line.extend((far[step], near[FINE + step]))
        for way, source, index, sub in line:
            share = planes - 1 if way else index
            chain_own[source, index, inner(sub)] = (
                local_sum(share, sub) + come(way, index, sub)
            ).astype(jnp.bfloat16)
            move = chain(source, 1, index, sub, behind if way else ahead)
            move.start()
            moves.append(move)
        for sub in range(FINE):
            finish(local_sum(2, sub) + come(1, 1, sub) + come(0, 2, sub), sub)
        for move in moves:
            move.wait_send()

    own_dkv = pltpu.make_async_copy(
        total.at[tile_rows(slot), :], dkv_out.at[core, :, lanes], local_sem.at[1]
    )
    own_dkv.start()
    own_dq.wait()
    own_dkv.wait()
    for index in range(1, planes):
        for sub in range(FINE):
            shares[index, sub].wait_send()
    for copy in rest:
        copy.wait()
    for target in range(team):
        @pl.when(slot != target)
        def _():
            flat(target).wait_send()
            pltpu.make_async_remote_copy(
                src_ref=total.at[tile_rows(slot), :],
                dst_ref=dkv_out.at[core, :, lanes],
                send_sem=flat_send.at[target],
                recv_sem=flat_recv.at[target],
                device_id=(mate, 0),
                device_id_type=MESH,
            ).wait_recv()


def give_back(team, planes, dq, dkv):
    tall, width = dq.shape
    rows = tall // team
    heads = team // 2
    hbm = pl.BlockSpec(memory_space=pl.ANY)
    dma = pltpu.SemaphoreType.DMA
    part = pltpu.VMEM((2, planes - 1, tall, HD), jnp.bfloat16)
    return pl.pallas_call(
        functools.partial(return_kernel, team, planes),
        out_shape=(
            jax.ShapeDtypeStruct((rows, width * team), jnp.bfloat16),
            jax.ShapeDtypeStruct((2, rows, heads * HD), jnp.bfloat16),
        ),
        in_specs=[hbm, hbm],
        out_specs=(hbm, hbm),
        scratch_shapes=[
            pltpu.VMEM((planes * tall, HD), jnp.bfloat16),
            pltpu.VMEM((planes, tall, HD), jnp.bfloat16),
            part,
            part,
            pltpu.VMEM((tall, HD), jnp.bfloat16),
            dma((3,)),
            dma((team - 1,)),
            dma((team - 1,)),
            dma((team,)),
            dma((team,)),
            dma((2, planes - 1, FINE)),
            dma((2, planes - 1, FINE)),
            dma((planes, FINE)),
            dma((planes, FINE)),
        ],
        compiler_params=pltpu.CompilerParams(
            collective_id=1, has_side_effects=True, vmem_limit_bytes=GIVE_LIMIT
        ),
        cost_estimate=pl.CostEstimate(flops=0, bytes_accessed=60 << 20, transcendentals=0),
    )(dq, dkv)


def local_planes(queries, key_states, value_states, outputs, out_grad, doc_of_tile, tile_position):
    team = 2 * (key_states.shape[1] // HD)
    planes = lax.axis_size("ctx") // team
    q, g, delta, kv = bring(team, planes, queries, out_grad, key_states, value_states, outputs)
    dq, dkv = attention_backward(tile_position, doc_of_tile, team, q, g, delta, kv)
    dq, dkv = give_back(team, planes, dq, dkv)
    return dq, dkv[0], dkv[1]


def local_any(queries, key_states, value_states, outputs, out_grad, doc_of_tile, tile_position):
    rows = queries.shape[0]
    kv_heads = key_states.shape[1] // HD
    head_count = lax.axis_size("head")
    ctx_count = lax.axis_size("ctx")
    ctx_index = lax.axis_index("ctx")
    split = kv_heads * head_count
    team = kv_heads
    parts = ctx_count // team
    near = [[b * team + s for s in range(team)] for b in range(parts)]
    far = [[b * team + s for b in range(parts)] for s in range(team)]

    def swap(value, split_axis, concat_axis):
        if head_count > 1:
            return lax.all_to_all(value, "head", split_axis, concat_axis, tiled=True)
        return lax.all_to_all(
            value, "ctx", split_axis, concat_axis, axis_index_groups=near, tiled=True
        )

    heads = queries.shape[1] // split // HD
    products = out_grad.astype(jnp.float32) * outputs.astype(jnp.float32)
    delta = jnp.sum(products.reshape(rows, split * heads, HD), axis=-1)
    kv = jnp.concatenate([key_states, value_states], axis=1)
    if head_count == 1:
        kv = kv.reshape(rows, 2, team, HD).transpose(0, 2, 1, 3).reshape(rows, team * 2 * HD)
        kv = swap(kv, 1, 0)
    kv = lax.all_gather(kv, "ctx", axis=0, tiled=True, axis_index_groups=far)
    kv = kv.reshape(-1, 2, HD).transpose(1, 0, 2)
    qd = jnp.concatenate(
        [
            queries.reshape(rows, split, heads * HD),
            out_grad.reshape(rows, split, heads * HD),
        ],
        axis=2,
    ).reshape(rows, split * 2 * heads * HD)
    qd = swap(qd, 1, 0)
    delta = swap(delta, 1, 0)
    tiles = qd.shape[0] // TILE
    delta = jnp.transpose(delta.reshape(tiles, TILE, heads), (0, 2, 1)).reshape(
        tiles, 1, heads * TILE
    )
    width = heads * HD
    dq, dkv = attention_backward(
        tile_position, doc_of_tile, team, qd[:, :width], qd[:, width:], delta, kv
    )
    if head_count == 1:
        dq = swap(dq, 0, 1)
    dkv = dkv.transpose(1, 0, 2).reshape(-1, 2 * HD)
    dkv = lax.all_to_all(dkv, "ctx", 0, 0, axis_index_groups=far, tiled=True)
    dkv = jnp.sum(dkv.reshape(parts, -1, 2 * HD).astype(jnp.float32), axis=0).astype(jnp.bfloat16)
    if head_count == 1:
        dkv = swap(dkv, 0, 1)
    dkv = dkv.reshape(dkv.shape[0], kv_heads, 2, HD)
    return (
        dq,
        dkv[:, :, 0].reshape(-1, kv_heads * HD),
        dkv[:, :, 1].reshape(-1, kv_heads * HD),
    )


def solution(mesh):
    placed = (
        P(("ctx", "head"), None),
        P("ctx", "head"),
        P("ctx", "head"),
        P(("ctx", "head"), None),
        P(("ctx", "head"), None),
        P(),
        P(),
    )
    slabs = mesh.shape["head"] == 1 and mesh.shape["ctx"] == 32
    return jax.shard_map(
        local_planes if slabs else local_any,
        mesh=mesh,
        in_specs=placed,
        out_specs=(P("ctx", "head"), P("ctx", "head"), P("ctx", "head")),
        check_vma=False,
    )
```

```python
import functools

import jax
import jax.numpy as jnp
from jax import lax
from jax.experimental import pallas as pl
from jax.experimental.pallas import tpu as pltpu
from jax.sharding import PartitionSpec as P

HD = 128
TILE = 128
SPAN = 2
LOW = -1e30
LOG2E = 1.4426950408889634
DEEP = 4
SUB = 2
FINE = 2
FLIGHT = 2
GIVE_LIMIT = 52 * 1024 * 1024
ATTENTION_LIMIT = 56 * 1024 * 1024
MESH = pl.DeviceIdType.MESH


def attention_kernel(
    heads,
    tiles,
    team,
    position_ref,
    doc_ref,
    q_hbm,
    g_hbm,
    delta_hbm,
    kv_hbm,
    dq_ref,
    dkv_ref,
    start_ref,
    item_tile,
    item_first,
    item_bound,
    q_rows,
    g_rows,
    q_cols,
    g_cols,
    delta_ref,
    kv_ref,
    gap_ref,
    scores_a,
    scores_b,
    low_a,
    low_b,
    grad_a,
    grad_b,
    probs_buf,
    top_buf,
    top_ref,
    total_ref,
    share_ref,
    dq_acc,
    dkv_acc,
    dq_own,
    dkv_own,
    sems,
):
    width = heads * HD
    scale = HD ** (-0.5)
    pair = SPAN * TILE
    count = position_ref.shape[0]
    block = lax.axis_index("ctx") // team

    def tile_at(index):
        return pl.ds(pl.multiple_of(index * TILE, TILE), TILE)

    heads_in = []
    for h in range(heads):
        lanes = slice(h * HD, (h + 1) * HD)
        for which, (src, dst) in enumerate(((q_hbm, q_rows), (g_hbm, g_rows))):
            copy = pltpu.make_async_copy(
                src.at[:, :, lanes], dst.at[0:tiles, h], sems.at[2 + 2 * h + which]
            )
            copy.start()
            heads_in.append(copy)
    delta_in = pltpu.make_async_copy(delta_hbm, delta_ref.at[0:tiles], sems.at[0])
    delta_in.start()

    @pl.loop(0, count)
    def _(spot):
        place = position_ref[spot]
        for which in range(2):
            pltpu.make_async_copy(
                kv_hbm.at[which, tile_at(spot), :],
                kv_ref.at[which, tile_at(place), :],
                sems.at[1],
            ).start()

    def find(index, start):
        fresh = doc_ref[index] != doc_ref[jnp.maximum(index - 1, 0)]
        start = jnp.where(fresh, index, start)
        start_ref[index] = start
        return start

    lax.fori_loop(0, count, find, jnp.int32(0))

    def put(index, tile, first, bound):
        item_tile[index] = tile
        item_first[index] = first
        item_bound[index] = bound

    def listed(tile, total):
        place = position_ref[block * tiles + tile]
        start = start_ref[place]
        full = (place - start) // 2
        put(tile, tile, start + 2 * full, (place - start - 2 * full) * TILE)

        @pl.loop(0, full)
        def _(step):
            put(total + step, tile, start + 2 * step, pair)

        return total + full

    items = lax.fori_loop(0, tiles, listed, jnp.int32(tiles))
    for extra in range(4):
        put(items + extra, tiles, 0, pair)

    gap_ref[...] = lax.broadcasted_iota(jnp.int32, (pair, TILE), 0) - lax.broadcasted_iota(
        jnp.int32, (pair, TILE), 1
    )
    dkv_acc[...] = jnp.zeros_like(dkv_acc)
    dq_acc[...] = jnp.zeros_like(dq_acc)
    top_ref[...] = jnp.full_like(top_ref, LOW)
    total_ref[...] = jnp.zeros_like(total_ref)
    q_cols[tiles] = jnp.zeros((HD, width), jnp.bfloat16)
    g_cols[tiles] = jnp.zeros((HD, width), jnp.bfloat16)
    q_rows[tiles] = jnp.zeros((heads, TILE, HD), jnp.bfloat16)
    g_rows[tiles] = jnp.zeros((heads, TILE, HD), jnp.bfloat16)
    delta_ref[tiles] = jnp.zeros((1, width), jnp.float32)
    kv_ref[:, count * TILE :, :] = jnp.zeros((2, TILE, HD), jnp.bfloat16)
    low_b[...] = jnp.zeros_like(low_b)
    grad_b[...] = jnp.zeros_like(grad_b)

    for copy in heads_in:
        copy.wait()

    @pl.loop(0, tiles, unroll=tiles)
    def _(tile):
        for h in range(heads):
            lanes = slice(h * HD, (h + 1) * HD)
            q_cols[tile, :, lanes] = q_rows[tile, h].T
            g_cols[tile, :, lanes] = g_rows[tile, h].T

    delta_in.wait()
    pltpu.make_async_copy(kv_hbm, kv_ref.at[:, 0 : count * TILE], sems.at[1]).wait()

    def groups(value):
        return value.reshape(value.shape[0] // 8, 8, width)

    def area(index):
        return pl.ds(pl.multiple_of(item_first[index] * TILE, TILE), pair)

    def score(index, into):
        into[...] = jnp.dot(
            kv_ref[0, area(index), :],
            q_cols[item_tile[index]],
            preferred_element_type=jnp.float32,
        )

    def weigh(index, source, edge):
        tile = item_tile[index]
        scores = source[...] * (scale * LOG2E)
        if edge:
            gap = jnp.concatenate([gap_ref[...]] * heads, axis=1)
            scores = jnp.where(gap <= item_bound[index], scores, LOW)
        scores = groups(scores)
        old = top_ref[tile]
        top = jnp.maximum(old, jnp.max(scores, axis=0))
        probs = jnp.exp2(scores - top[None])
        probs_buf[index] = probs.reshape(pair, width)
        top_buf[index] = top
        top_ref[tile] = top
        total_ref[tile] = total_ref[tile] * jnp.exp2(old - top) + jnp.sum(probs, axis=0)

    score(0, scores_a)

    def weigh_two(index, edge=False):
        score(index + 1, scores_b)
        weigh(index, scores_a, edge)
        score(index + 2, scores_a)
        weigh(index + 1, scores_b, edge)

    edges = (tiles + 1) // 2
    rounds = (items + 1) // 2
    for part in range(edges):
        weigh_two(2 * part, edge=True)
    deep = edges + (rounds - edges) // DEEP * DEEP

    @pl.loop(0, (rounds - edges) // DEEP)
    def _(step):
        for part in range(DEEP):
            weigh_two(2 * (edges + DEEP * step + part))

    @pl.loop(deep, rounds)
    def _(step):
        weigh_two(2 * step)

    for tile in range(tiles):
        top = top_ref[tile]
        peak = jnp.broadcast_to(jnp.max(top, axis=0, keepdims=True), (8, width))
        total = jnp.sum(total_ref[tile] * jnp.exp2(top - peak), axis=0, keepdims=True)
        top_ref[tile] = peak
        share_ref[tile] = 1.0 / jnp.broadcast_to(total, (8, width))
    top_ref[tiles] = jnp.zeros((8, width), jnp.float32)
    share_ref[tiles] = jnp.zeros((8, width), jnp.float32)
    for extra in range(2):
        probs_buf[items + extra] = jnp.zeros((pair, width), jnp.float32)
        top_buf[items + extra] = jnp.zeros((8, width), jnp.float32)

    def value_scores(index, into):
        into[...] = jnp.dot(
            kv_ref[1, area(index), :],
            g_cols[item_tile[index]],
            preferred_element_type=jnp.float32,
        )

    def combine(index, source, low, grad):
        tile = item_tile[index]
        factor = jnp.exp2(top_buf[index] - top_ref[tile]) * share_ref[tile]
        probs = groups(probs_buf[index]) * factor[None]
        low[...] = probs.reshape(pair, width).astype(jnp.bfloat16)
        grad[...] = (
            (probs * (groups(source[...]) - delta_ref[tile][None]) * scale)
            .reshape(pair, width)
            .astype(jnp.bfloat16)
        )

    def add(index, low, grad):
        tile = item_tile[index]
        spot = area(index)
        dkv_acc[1, spot, :] += jnp.dot(
            low[...], g_rows[tile].reshape(width, HD), preferred_element_type=jnp.float32
        )
        dkv_acc[0, spot, :] += jnp.dot(
            grad[...], q_rows[tile].reshape(width, HD), preferred_element_type=jnp.float32
        )
        dq_acc[tile] += lax.dot_general(
            kv_ref[0, spot, :],
            grad[...],
            (((0,), (0,)), ((), ())),
            preferred_element_type=jnp.float32,
        )

    value_scores(0, scores_a)

    def add_two(index):
        value_scores(index + 1, scores_b)
        add(jnp.where(index == 0, items, index - 1), low_b, grad_b)
        combine(index, scores_a, low_a, grad_a)
        value_scores(index + 2, scores_a)
        add(index, low_a, grad_a)
        combine(index + 1, scores_b, low_b, grad_b)

    turns = (items + 2) // 2

    @pl.loop(0, turns // DEEP)
    def _(step):
        for part in range(DEEP):
            add_two(2 * (DEEP * step + part))

    @pl.loop(turns // DEEP * DEEP, turns)
    def _(step):
        add_two(2 * step)

    outs = [pltpu.make_async_copy(dkv_own.at[w], dkv_ref.at[w], sems.at[w]) for w in range(2)]
    for which in range(2):
        @pl.loop(0, count, unroll=4)
        def _(spot):
            place = position_ref[spot]
            dkv_own[which, tile_at(spot), :] = dkv_acc[which, tile_at(place), :].astype(
                jnp.bfloat16
            )

        outs[which].start()

    for tile in range(tiles):
        rows = slice(tile * TILE, (tile + 1) * TILE)
        for h in range(heads):
            lanes = slice(h * HD, (h + 1) * HD)
            dq_own[rows, lanes] = dq_acc[tile, :, lanes].T.astype(jnp.bfloat16)
        copy = pltpu.make_async_copy(dq_own.at[rows], dq_ref.at[rows], sems.at[2 + tile])
        copy.start()
        outs.append(copy)
    for copy in outs:
        copy.wait()


def attention_backward(positions, docs, team, q, g, delta, kv):
    rows, width = q.shape
    heads = width // HD
    tokens = kv.shape[1]
    tiles = rows // TILE
    count = tokens // TILE
    longest = count // 2
    most = sum((longest - i + 1) // 2 for i in range(min(tiles, longest)))
    most = max(most, tiles) + 4
    pair = SPAN * TILE
    smem = pl.BlockSpec(memory_space=pltpu.SMEM)
    hbm = pl.BlockSpec(memory_space=pl.ANY)
    slots = tiles + 1
    stat = pltpu.VMEM((slots, 8, width), jnp.float32)
    return pl.pallas_call(
        functools.partial(attention_kernel, heads, tiles, team),
        out_shape=(
            jax.ShapeDtypeStruct((rows, width), jnp.bfloat16),
            jax.ShapeDtypeStruct((2, tokens, HD), jnp.bfloat16),
        ),
        in_specs=[smem, smem, hbm, hbm, hbm, hbm],
        out_specs=(hbm, hbm),
        scratch_shapes=[
            pltpu.SMEM((count,), jnp.int32),
            pltpu.SMEM((most,), jnp.int32),
            pltpu.SMEM((most,), jnp.int32),
            pltpu.SMEM((most,), jnp.int32),
            pltpu.VMEM((slots, heads, TILE, HD), jnp.bfloat16),
            pltpu.VMEM((slots, heads, TILE, HD), jnp.bfloat16),
            pltpu.VMEM((slots, HD, width), jnp.bfloat16),
            pltpu.VMEM((slots, HD, width), jnp.bfloat16),
            pltpu.VMEM((slots, 1, width), jnp.float32),
            pltpu.VMEM((2, tokens + TILE, HD), jnp.bfloat16),
            pltpu.VMEM((pair, TILE), jnp.int32),
            pltpu.VMEM((pair, width), jnp.float32),
            pltpu.VMEM((pair, width), jnp.float32),
            pltpu.VMEM((pair, width), jnp.bfloat16),
            pltpu.VMEM((pair, width), jnp.bfloat16),
            pltpu.VMEM((pair, width), jnp.bfloat16),
            pltpu.VMEM((pair, width), jnp.bfloat16),
            pltpu.VMEM((most, pair, width), jnp.float32),
            pltpu.VMEM((most, 8, width), jnp.float32),
            stat,
            stat,
            stat,
            pltpu.VMEM((slots, HD, width), jnp.float32),
            pltpu.VMEM((2, tokens + TILE, HD), jnp.float32),
            pltpu.VMEM((rows, width), jnp.bfloat16),
            pltpu.VMEM((2, tokens, HD), jnp.bfloat16),
            pltpu.SemaphoreType.DMA((2 + max(2 * heads, tiles),)),
        ],
        compiler_params=pltpu.CompilerParams(vmem_limit_bytes=ATTENTION_LIMIT),
        cost_estimate=pl.CostEstimate(
            flops=rows * width * tokens * 3, bytes_accessed=12 << 20, transcendentals=0
        ),
    )(positions, docs, q.reshape(tiles, TILE, width), g.reshape(tiles, TILE, width), delta, kv)


def bring_kernel(
    team,
    planes,
    q_ref,
    g_ref,
    k_ref,
    v_ref,
    o_ref,
    q_out,
    g_out,
    delta_out,
    kv_out,
    kv_own,
    g_own,
    o_own,
    delta_own,
    load_sem,
    local_sem,
    flat_send,
    flat_recv,
    chain_send,
    chain_recv,
    core_send,
    core_recv,
):
    me = lax.axis_index("ctx")
    slot = me % team
    plane = me // team
    core = slot % 2
    mate = me + 1 - 2 * core
    width = q_out.shape[1]
    span = team * TILE
    tall = pl.ds(pl.multiple_of(slot * TILE, TILE), TILE)
    wide = pl.ds(pl.multiple_of(slot * width, HD), width)

    loads = [
        pltpu.make_async_copy(k_ref, kv_own.at[0], load_sem.at[0]),
        pltpu.make_async_copy(v_ref, kv_own.at[1], load_sem.at[1]),
        pltpu.make_async_copy(g_ref, g_own, load_sem.at[2]),
        pltpu.make_async_copy(o_ref, o_own, load_sem.at[3]),
    ]
    for load in loads:
        load.start()

    barrier = pltpu.get_barrier_semaphore()
    for shift in range(1, team):
        pl.semaphore_signal(
            barrier,
            inc=1,
            device_id=(plane * team + (slot + shift) % team, 0),
            device_id_type=MESH,
        )

    @pl.when(plane < planes - 1)
    def _():
        pl.semaphore_signal(barrier, inc=1, device_id=(me + team, 0), device_id_type=MESH)

    @pl.when(plane > 0)
    def _():
        pl.semaphore_signal(barrier, inc=1, device_id=(me - team, 0), device_id_type=MESH)

    near = jnp.where(plane < planes - 1, 1, 0) + jnp.where(plane > 0, 1, 0)
    pl.semaphore_wait(barrier, team - 1 + near)

    def flat(kind, shift, src, dst):
        return pltpu.make_async_remote_copy(
            src_ref=src,
            dst_ref=dst,
            send_sem=flat_send.at[kind, shift - 1],
            recv_sem=flat_recv.at[kind, slot],
            device_id=(plane * team + (slot + shift) % team, 0),
            device_id_type=MESH,
        )

    loads[0].wait()
    loads[1].wait()
    home = pl.ds(pl.multiple_of(me * TILE, TILE), TILE)
    flats = []
    for shift in range(1, team):
        other = (slot + shift) % team
        lanes = pl.ds(pl.multiple_of(other // 2 * HD, HD), HD)
        copy = flat(
            0, shift, kv_own.at[other % 2, :, lanes], kv_out.at[other % 2, home, :]
        )
        copy.start()
        flats.append(copy)
    locals_ = [
        pltpu.make_async_copy(
            kv_own.at[core, :, pl.ds(pl.multiple_of(slot // 2 * HD, HD), HD)],
            kv_out.at[core, home, :],
            local_sem.at[0],
        ),
        pltpu.make_async_copy(q_ref.at[:, wide], q_out.at[tall, :], local_sem.at[1]),
        pltpu.make_async_copy(g_ref.at[:, wide], g_out.at[tall, :], local_sem.at[2]),
    ]
    for copy in locals_:
        copy.start()
    rest = []
    for kind, (src, dst) in enumerate(((q_ref, q_out), (g_ref, g_out))):
        for shift in range(1, team):
            other = (slot + shift) % team
            lanes = pl.ds(pl.multiple_of(other * width, HD), width)
            copy = flat(1 + kind, shift, src.at[:, lanes], dst.at[tall, :])
            copy.start()
            rest.append(copy)
    locals_[0].wait()
    part_rows = span // SUB
    per_part = team // SUB

    def arrived(kind, source, dst):
        return pltpu.make_async_remote_copy(
            src_ref=dst,
            dst_ref=dst,
            send_sem=flat_send.at[kind, 0],
            recv_sem=flat_recv.at[kind, source],
            device_id=(mate, 0),
            device_id_type=MESH,
        )

    def part(which, sub):
        first = pl.multiple_of(which * span + sub * part_rows, TILE)
        return kv_out.at[core, pl.ds(first, part_rows), :]

    def chain(way, step, which, sub):
        return pltpu.make_async_remote_copy(
            src_ref=part(which, sub),
            dst_ref=part(which, sub),
            send_sem=chain_send.at[way, step, sub],
            recv_sem=chain_recv.at[way, step, sub],
            device_id=(me + team - 2 * way * team, 0),
            device_id_type=MESH,
        )

    def share(index, which, sub):
        return pltpu.make_async_remote_copy(
            src_ref=part(which, sub),
            dst_ref=part(which, sub),
            send_sem=core_send.at[index, sub],
            recv_sem=core_recv.at[index, sub],
            device_id=(mate, 0),
            device_id_type=MESH,
        )

    def up_ok(step):
        return (plane < planes - 1) & (plane - step >= 0)

    def down_ok(step):
        return (plane > 0) & (plane + step <= planes - 1)

    def up_come(step):
        return plane - 1 - step >= 0

    def down_come(step):
        return plane + 1 + step <= planes - 1

    for sub in range(SUB):
        for source in range(sub * per_part, (sub + 1) * per_part):
            @pl.when(slot != source)
            def _():
                arrived(0, source, kv_out.at[core, home, :]).wait_recv()

        @pl.when(up_ok(0))
        def _():
            chain(0, 0, plane, sub).start()

        @pl.when(down_ok(0))
        def _():
            chain(1, 0, plane, sub).start()

        share(0, plane, sub).start()

    loads[2].wait()
    loads[3].wait()
    for index in range(team):
        for head in range(width // HD):
            lanes = slice(index * width + head * HD, index * width + (head + 1) * HD)
            product = g_own[:, lanes].astype(jnp.float32) * o_own[:, lanes].astype(jnp.float32)
            row = jnp.sum(product.T, axis=0, keepdims=True)
            delta_own[index, :, head * HD : (head + 1) * HD] = row
    for shift in range(1, team):
        other = (slot + shift) % team
        copy = flat(3, shift, delta_own.at[other], delta_out.at[slot])
        copy.start()
        rest.append(copy)
    own_delta = pltpu.make_async_copy(delta_own.at[slot], delta_out.at[slot], local_sem.at[3])
    own_delta.start()

    for step in range(planes - 1):
        for sub in range(SUB):
            @pl.when(up_come(step))
            def _():
                chain(0, step, plane - 1 - step, sub).wait_recv()
                if step < planes - 2:
                    @pl.when(up_ok(step + 1))
                    def _():
                        chain(0, step + 1, plane - 1 - step, sub).start()
                share(1 + step, plane - 1 - step, sub).start()

            @pl.when(down_come(step))
            def _():
                chain(1, step, plane + 1 + step, sub).wait_recv()
                if step < planes - 2:
                    @pl.when(down_ok(step + 1))
                    def _():
                        chain(1, step + 1, plane + 1 + step, sub).start()
                share(planes + step, plane + 1 + step, sub).start()

    for sub in range(SUB):
        share(0, plane, sub).wait()
        for step in range(planes - 1):
            @pl.when(up_come(step))
            def _():
                share(1 + step, plane - 1 - step, sub).wait()

            @pl.when(down_come(step))
            def _():
                share(planes + step, plane + 1 + step, sub).wait()

            @pl.when(up_ok(step))
            def _():
                chain(0, step, plane - step, sub).wait_send()

            @pl.when(down_ok(step))
            def _():
                chain(1, step, plane + step, sub).wait_send()

    for copy in locals_[1:] + [own_delta]:
        copy.wait()
    for copy in rest + flats:
        copy.wait_send()
    for source in range(team):
        @pl.when(slot != source)
        def _():
            arrived(1, source, q_out.at[tall, :]).wait_recv()
            arrived(2, source, g_out.at[tall, :]).wait_recv()
            arrived(3, source, delta_out.at[slot]).wait_recv()


def bring(team, planes, queries, out_grad, key_states, value_states, outputs):
    rows, columns = queries.shape
    width = columns // team
    tokens = rows * team * planes
    vmem = pl.BlockSpec(memory_space=pltpu.VMEM)
    hbm = pl.BlockSpec(memory_space=pltpu.HBM)
    dma = pltpu.SemaphoreType.DMA
    return pl.pallas_call(
        functools.partial(bring_kernel, team, planes),
        out_shape=(
            jax.ShapeDtypeStruct((rows * team, width), jnp.bfloat16),
            jax.ShapeDtypeStruct((rows * team, width), jnp.bfloat16),
            jax.ShapeDtypeStruct((team, 1, width), jnp.float32),
            jax.ShapeDtypeStruct((2, tokens, HD), jnp.bfloat16),
        ),
        in_specs=[hbm, hbm, hbm, hbm, hbm],
        out_specs=(hbm, hbm, hbm, hbm),
        scratch_shapes=[
            pltpu.VMEM((2, rows, key_states.shape[1]), jnp.bfloat16),
            pltpu.VMEM((rows, columns), jnp.bfloat16),
            pltpu.VMEM((rows, columns), jnp.bfloat16),
            pltpu.VMEM((team, 1, width), jnp.float32),
            dma((4,)),
            dma((4,)),
            dma((4, team - 1)),
            dma((4, team)),
            dma((2, planes - 1, SUB)),
            dma((2, planes - 1, SUB)),
            dma((2 * planes - 1, SUB)),
            dma((2 * planes - 1, SUB)),
        ],
        compiler_params=pltpu.CompilerParams(
            collective_id=0, has_side_effects=True, vmem_limit_bytes=60 * 1024 * 1024
        ),
        cost_estimate=pl.CostEstimate(flops=0, bytes_accessed=60 << 20, transcendentals=0),
    )(queries, out_grad, key_states, value_states, outputs)


def return_kernel(
    team,
    planes,
    dq_ref,
    dkv_ref,
    dq_out,
    dkv_out,
    own,
    mate_in,
    chain_in,
    chain_own,
    total,
    local_sem,
    dq_send,
    dq_recv,
    flat_send,
    flat_recv,
    chain_send,
    chain_recv,
    core_send,
    core_recv,
):
    me = lax.axis_index("ctx")
    slot = me % team
    plane = me // team
    core = slot % 2
    mate = me + 1 - 2 * core
    width = dq_ref.shape[1]
    part_rows = TILE // FINE

    load = pltpu.make_async_copy(dkv_ref.at[core], own, local_sem.at[2])
    load.start()
    barrier = pltpu.get_barrier_semaphore()
    for shift in range(1, team):
        pl.semaphore_signal(
            barrier,
            inc=1,
            device_id=(plane * team + (slot + shift) % team, 0),
            device_id_type=MESH,
        )

    @pl.when(plane < planes - 1)
    def _():
        pl.semaphore_signal(barrier, inc=1, device_id=(me + team, 0), device_id_type=MESH)

    @pl.when(plane > 0)
    def _():
        pl.semaphore_signal(barrier, inc=1, device_id=(me - team, 0), device_id_type=MESH)

    near = jnp.where(plane < planes - 1, 1, 0) + jnp.where(plane > 0, 1, 0)
    pl.semaphore_wait(barrier, team - 1 + near)

    def inner(sub):
        return pl.ds(sub * part_rows, part_rows)

    def tile_rows(which):
        return pl.ds(pl.multiple_of(which * TILE, TILE), TILE)

    half = plane // (planes // 2)
    depth = plane * (1 - half) + (planes - 1 - plane) * half
    ahead = me + team * (1 - 2 * half)
    behind = me - team * (1 - 2 * half)

    def target_plane(index):
        return (planes - 1 - index) * (1 - half) + index * half

    shares = {}
    for index in range(planes):
        for sub in range(FINE):
            copy = pltpu.make_async_remote_copy(
                src_ref=dkv_ref.at[1 - core, target_plane(index), :, inner(sub), :],
                dst_ref=mate_in.at[index, :, inner(sub), :],
                send_sem=core_send.at[index, sub],
                recv_sem=core_recv.at[index, sub],
                device_id=(mate, 0),
                device_id_type=MESH,
            )
            shares[index, sub] = copy
    for sub in range(FINE):
        shares[0, sub].start()

    wide = pl.ds(pl.multiple_of(slot * width, HD), width)
    rest = []
    own_dq = pltpu.make_async_copy(
        dq_ref.at[tile_rows(slot), :], dq_out.at[:, wide], local_sem.at[0]
    )
    own_dq.start()
    for shift in range(1, team):
        other = (slot + shift) % team
        copy = pltpu.make_async_remote_copy(
            src_ref=dq_ref.at[tile_rows(other), :],
            dst_ref=dq_out.at[:, wide],
            send_sem=dq_send.at[shift - 1],
            recv_sem=dq_recv.at[shift - 1],
            device_id=(plane * team + other, 0),
            device_id_type=MESH,
        )
        copy.start()
        rest.append(copy)

    def chain(source, into, index, sub, device):
        return pltpu.make_async_remote_copy(
            src_ref=chain_own.at[source, index, :, inner(sub), :],
            dst_ref=chain_in.at[into, index, :, inner(sub), :],
            send_sem=chain_send.at[source, index, sub],
            recv_sem=chain_recv.at[into, index, sub],
            device_id=(device, 0),
            device_id_type=MESH,
        )

    def local_sum(index, sub):
        shares[index, sub].wait_recv()
        return own[target_plane(index), :, inner(sub), :].astype(jnp.float32) + mate_in[
            index, :, inner(sub), :
        ].astype(jnp.float32)

    def come(way, index, sub):
        chain(0, way, index, sub, mate).wait_recv()
        return chain_in[way, index, :, inner(sub), :].astype(jnp.float32)

    load.wait()
    for sub in range(FINE):
        shares[0, sub].wait_send()
    for index in (planes - 1, *range(1, planes - 1)):
        for sub in range(FINE):
            shares[index, sub].start()
    lanes = pl.ds(pl.multiple_of(slot // 2 * HD, HD), HD)
    def flat(shift, sub):
        target = (slot + shift) % team
        return pltpu.make_async_remote_copy(
            src_ref=total.at[target, inner(sub), :],
            dst_ref=dkv_out.at[core, inner(sub), lanes],
            send_sem=flat_send.at[shift - 1, sub],
            recv_sem=flat_recv.at[shift - 1, sub],
            device_id=(plane * team + target, 0),
            device_id_type=MESH,
        )

    def finish(value, sub):
        total[:, inner(sub), :] = value.astype(jnp.bfloat16)
        for shift in range(1, team):
            flat(shift, sub).start()

    pieces = [(index, sub) for index in range(planes - 1) for sub in range(FINE)]

    @pl.when(depth == 0)
    def _():
        moves = []
        for index, sub in pieces:
            chain_own[0, index, :, inner(sub), :] = local_sum(index, sub).astype(jnp.bfloat16)
            if len(moves) >= FLIGHT:
                moves[-FLIGHT].wait_send()
            move = chain(0, 0, index, sub, ahead)
            move.start()
            moves.append(move)
        for sub in range(FINE):
            finish(local_sum(planes - 1, sub) + come(1, 0, sub), sub)
        for move in moves[-FLIGHT:]:
            move.wait_send()

    @pl.when(depth == 1)
    def _():
        moves = []
        near = [(0, 0, index, sub) for index in range(2) for sub in range(FINE)]
        far = [(1, 1, 0, sub) for sub in range(FINE)]
        line = near[:FINE]
        for step in range(FINE):
            line.extend((far[step], near[FINE + step]))
        for way, source, index, sub in line:
            share = planes - 1 if way else index
            chain_own[source, index, :, inner(sub), :] = (
                local_sum(share, sub) + come(way, index, sub)
            ).astype(jnp.bfloat16)
            move = chain(source, 1, index, sub, behind if way else ahead)
            move.start()
            moves.append(move)
        for sub in range(FINE):
            finish(local_sum(2, sub) + come(1, 1, sub) + come(0, 2, sub), sub)
        for move in moves:
            move.wait_send()

    own_dkv = pltpu.make_async_copy(
        total.at[slot], dkv_out.at[core, :, lanes], local_sem.at[1]
    )
    own_dkv.start()
    own_dq.wait()
    own_dkv.wait()
    for index in range(1, planes):
        for sub in range(FINE):
            shares[index, sub].wait_send()
    for copy in rest:
        copy.wait()
    for sub in range(FINE):
        for shift in range(1, team):
            flat(shift, sub).wait()


def give_back(team, planes, dq, dkv):
    tall, width = dq.shape
    rows = tall // team
    heads = team // 2
    hbm = pl.BlockSpec(memory_space=pl.ANY)
    dma = pltpu.SemaphoreType.DMA
    part = pltpu.VMEM((2, planes - 1, team, rows, HD), jnp.bfloat16)
    return pl.pallas_call(
        functools.partial(return_kernel, team, planes),
        out_shape=(
            jax.ShapeDtypeStruct((rows, width * team), jnp.bfloat16),
            jax.ShapeDtypeStruct((2, rows, heads * HD), jnp.bfloat16),
        ),
        in_specs=[hbm, hbm],
        out_specs=(hbm, hbm),
        scratch_shapes=[
            pltpu.VMEM((planes, team, rows, HD), jnp.bfloat16),
            pltpu.VMEM((planes, team, rows, HD), jnp.bfloat16),
            part,
            part,
            pltpu.VMEM((team, rows, HD), jnp.bfloat16),
            dma((3,)),
            dma((team - 1,)),
            dma((team - 1,)),
            dma((team - 1, FINE)),
            dma((team - 1, FINE)),
            dma((2, planes - 1, FINE)),
            dma((2, planes - 1, FINE)),
            dma((planes, FINE)),
            dma((planes, FINE)),
        ],
        compiler_params=pltpu.CompilerParams(
            collective_id=1, has_side_effects=True, vmem_limit_bytes=GIVE_LIMIT
        ),
        cost_estimate=pl.CostEstimate(flops=0, bytes_accessed=60 << 20, transcendentals=0),
    )(dq, dkv.reshape(2, planes, team, rows, HD))


def local_planes(queries, key_states, value_states, outputs, out_grad, doc_of_tile, tile_position):
    team = 2 * (key_states.shape[1] // HD)
    planes = lax.axis_size("ctx") // team
    q, g, delta, kv = bring(team, planes, queries, out_grad, key_states, value_states, outputs)
    dq, dkv = attention_backward(tile_position, doc_of_tile, team, q, g, delta, kv)
    dq, dkv = give_back(team, planes, dq, dkv)
    return dq, dkv[0], dkv[1]


def local_any(queries, key_states, value_states, outputs, out_grad, doc_of_tile, tile_position):
    rows = queries.shape[0]
    kv_heads = key_states.shape[1] // HD
    head_count = lax.axis_size("head")
    ctx_count = lax.axis_size("ctx")
    ctx_index = lax.axis_index("ctx")
    split = kv_heads * head_count
    team = kv_heads
    parts = ctx_count // team
    near = [[b * team + s for s in range(team)] for b in range(parts)]
    far = [[b * team + s for b in range(parts)] for s in range(team)]

    def swap(value, split_axis, concat_axis):
        if head_count > 1:
            return lax.all_to_all(value, "head", split_axis, concat_axis, tiled=True)
        return lax.all_to_all(
            value, "ctx", split_axis, concat_axis, axis_index_groups=near, tiled=True
        )

    heads = queries.shape[1] // split // HD
    products = out_grad.astype(jnp.float32) * outputs.astype(jnp.float32)
    delta = jnp.sum(products.reshape(rows, split * heads, HD), axis=-1)
    kv = jnp.concatenate([key_states, value_states], axis=1)
    if head_count == 1:
        kv = kv.reshape(rows, 2, team, HD).transpose(0, 2, 1, 3).reshape(rows, team * 2 * HD)
        kv = swap(kv, 1, 0)
    kv = lax.all_gather(kv, "ctx", axis=0, tiled=True, axis_index_groups=far)
    kv = kv.reshape(-1, 2, HD).transpose(1, 0, 2)
    qd = jnp.concatenate(
        [
            queries.reshape(rows, split, heads * HD),
            out_grad.reshape(rows, split, heads * HD),
        ],
        axis=2,
    ).reshape(rows, split * 2 * heads * HD)
    qd = swap(qd, 1, 0)
    delta = swap(delta, 1, 0)
    tiles = qd.shape[0] // TILE
    delta = jnp.transpose(delta.reshape(tiles, TILE, heads), (0, 2, 1)).reshape(
        tiles, 1, heads * TILE
    )
    width = heads * HD
    dq, dkv = attention_backward(
        tile_position, doc_of_tile, team, qd[:, :width], qd[:, width:], delta, kv
    )
    if head_count == 1:
        dq = swap(dq, 0, 1)
    dkv = dkv.transpose(1, 0, 2).reshape(-1, 2 * HD)
    dkv = lax.all_to_all(dkv, "ctx", 0, 0, axis_index_groups=far, tiled=True)
    dkv = jnp.sum(dkv.reshape(parts, -1, 2 * HD).astype(jnp.float32), axis=0).astype(jnp.bfloat16)
    if head_count == 1:
        dkv = swap(dkv, 0, 1)
    dkv = dkv.reshape(dkv.shape[0], kv_heads, 2, HD)
    return (
        dq,
        dkv[:, :, 0].reshape(-1, kv_heads * HD),
        dkv[:, :, 1].reshape(-1, kv_heads * HD),
    )


def solution(mesh):
    placed = (
        P(("ctx", "head"), None),
        P("ctx", "head"),
        P("ctx", "head"),
        P(("ctx", "head"), None),
        P(("ctx", "head"), None),
        P(),
        P(),
    )
    slabs = mesh.shape["head"] == 1 and mesh.shape["ctx"] == 32
    return jax.shard_map(
        local_planes if slabs else local_any,
        mesh=mesh,
        in_specs=placed,
        out_specs=(P("ctx", "head"), P("ctx", "head"), P("ctx", "head")),
        check_vma=False,
    )
```

```python
import functools

import jax
import jax.numpy as jnp
from jax import lax
from jax.experimental import pallas as pl
from jax.experimental.pallas import tpu as pltpu
from jax.sharding import PartitionSpec as P

HD = 128
TILE = 128
SPAN = 2
LOW = -1e30
LOG2E = 1.4426950408889634
DEEP = 4
SUB = 2
FINE = 2
FLIGHT = 2
GIVE_LIMIT = 52 * 1024 * 1024
ATTENTION_LIMIT = 56 * 1024 * 1024
MESH = pl.DeviceIdType.MESH


def attention_kernel(
    heads,
    tiles,
    team,
    position_ref,
    doc_ref,
    q_hbm,
    g_hbm,
    delta_hbm,
    kv_hbm,
    dq_ref,
    dkv_ref,
    start_ref,
    item_tile,
    item_first,
    item_bound,
    q_rows,
    g_rows,
    q_cols,
    g_cols,
    delta_ref,
    kv_ref,
    gap_ref,
    scores_a,
    scores_b,
    low_a,
    low_b,
    grad_a,
    grad_b,
    probs_buf,
    top_buf,
    top_ref,
    total_ref,
    share_ref,
    dq_acc,
    dkv_acc,
    dq_own,
    dkv_own,
    sems,
):
    width = heads * HD
    scale = HD ** (-0.5)
    pair = SPAN * TILE
    count = position_ref.shape[0]
    block = lax.axis_index("ctx") // team

    def tile_at(index):
        return pl.ds(pl.multiple_of(index * TILE, TILE), TILE)

    heads_in = []
    for h in range(heads):
        lanes = slice(h * HD, (h + 1) * HD)
        for which, (src, dst) in enumerate(((q_hbm, q_rows), (g_hbm, g_rows))):
            copy = pltpu.make_async_copy(
                src.at[:, :, lanes], dst.at[0:tiles, h], sems.at[2 + 2 * h + which]
            )
            copy.start()
            heads_in.append(copy)
    delta_in = pltpu.make_async_copy(delta_hbm, delta_ref.at[0:tiles], sems.at[0])
    delta_in.start()

    @pl.loop(0, count)
    def _(spot):
        place = position_ref[spot]
        for which in range(2):
            pltpu.make_async_copy(
                kv_hbm.at[which, tile_at(spot), :],
                kv_ref.at[which, tile_at(place), :],
                sems.at[1],
            ).start()

    def find(index, start):
        fresh = doc_ref[index] != doc_ref[jnp.maximum(index - 1, 0)]
        start = jnp.where(fresh, index, start)
        start_ref[index] = start
        return start

    lax.fori_loop(0, count, find, jnp.int32(0))

    def put(index, tile, first, bound):
        item_tile[index] = tile
        item_first[index] = first
        item_bound[index] = bound

    def listed(tile, total):
        place = position_ref[block * tiles + tile]
        start = start_ref[place]
        full = (place - start) // 2
        put(tile, tile, start + 2 * full, (place - start - 2 * full) * TILE)

        @pl.loop(0, full)
        def _(step):
            put(total + step, tile, start + 2 * step, pair)

        return total + full

    items = lax.fori_loop(0, tiles, listed, jnp.int32(tiles))
    for extra in range(4):
        put(items + extra, tiles, 0, pair)

    gap_ref[...] = lax.broadcasted_iota(jnp.int32, (pair, TILE), 0) - lax.broadcasted_iota(
        jnp.int32, (pair, TILE), 1
    )
    dkv_acc[...] = jnp.zeros_like(dkv_acc)
    dq_acc[...] = jnp.zeros_like(dq_acc)
    top_ref[...] = jnp.full_like(top_ref, LOW)
    total_ref[...] = jnp.zeros_like(total_ref)
    q_cols[tiles] = jnp.zeros((HD, width), jnp.bfloat16)
    g_cols[tiles] = jnp.zeros((HD, width), jnp.bfloat16)
    q_rows[tiles] = jnp.zeros((heads, TILE, HD), jnp.bfloat16)
    g_rows[tiles] = jnp.zeros((heads, TILE, HD), jnp.bfloat16)
    delta_ref[tiles] = jnp.zeros((1, width), jnp.float32)
    kv_ref[:, count * TILE :, :] = jnp.zeros((2, TILE, HD), jnp.bfloat16)
    low_b[...] = jnp.zeros_like(low_b)
    grad_b[...] = jnp.zeros_like(grad_b)

    for copy in heads_in:
        copy.wait()

    @pl.loop(0, tiles, unroll=tiles)
    def _(tile):
        for h in range(heads):
            lanes = slice(h * HD, (h + 1) * HD)
            q_cols[tile, :, lanes] = q_rows[tile, h].T
            g_cols[tile, :, lanes] = g_rows[tile, h].T

    delta_in.wait()
    pltpu.make_async_copy(kv_hbm, kv_ref.at[:, 0 : count * TILE], sems.at[1]).wait()

    def groups(value):
        return value.reshape(value.shape[0] // 8, 8, width)

    def area(index):
        return pl.ds(pl.multiple_of(item_first[index] * TILE, TILE), pair)

    def score(index, into):
        into[...] = jnp.dot(
            kv_ref[0, area(index), :],
            q_cols[item_tile[index]],
            preferred_element_type=jnp.float32,
        )

    def weigh(index, source, edge):
        tile = item_tile[index]
        scores = source[...] * (scale * LOG2E)
        if edge:
            gap = jnp.concatenate([gap_ref[...]] * heads, axis=1)
            scores = jnp.where(gap <= item_bound[index], scores, LOW)
        scores = groups(scores)
        old = top_ref[tile]
        top = jnp.maximum(old, jnp.max(scores, axis=0))
        probs = jnp.exp2(scores - top[None])
        probs_buf[index] = probs.reshape(pair, width)
        top_buf[index] = top
        top_ref[tile] = top
        total_ref[tile] = total_ref[tile] * jnp.exp2(old - top) + jnp.sum(probs, axis=0)

    score(0, scores_a)

    def weigh_two(index, edge=False):
        score(index + 1, scores_b)
        weigh(index, scores_a, edge)
        score(index + 2, scores_a)
        weigh(index + 1, scores_b, edge)

    edges = (tiles + 1) // 2
    rounds = (items + 1) // 2
    for part in range(edges):
        weigh_two(2 * part, edge=True)
    deep = edges + (rounds - edges) // DEEP * DEEP

    @pl.loop(0, (rounds - edges) // DEEP)
    def _(step):
        for part in range(DEEP):
            weigh_two(2 * (edges + DEEP * step + part))

    @pl.loop(deep, rounds)
    def _(step):
        weigh_two(2 * step)

    for tile in range(tiles):
        top = top_ref[tile]
        peak = jnp.broadcast_to(jnp.max(top, axis=0, keepdims=True), (8, width))
        total = jnp.sum(total_ref[tile] * jnp.exp2(top - peak), axis=0, keepdims=True)
        top_ref[tile] = peak
        share_ref[tile] = 1.0 / jnp.broadcast_to(total, (8, width))
    top_ref[tiles] = jnp.zeros((8, width), jnp.float32)
    share_ref[tiles] = jnp.zeros((8, width), jnp.float32)
    for extra in range(2):
        probs_buf[items + extra] = jnp.zeros((pair, width), jnp.float32)
        top_buf[items + extra] = jnp.zeros((8, width), jnp.float32)

    def value_scores(index, into):
        into[...] = jnp.dot(
            kv_ref[1, area(index), :],
            g_cols[item_tile[index]],
            preferred_element_type=jnp.float32,
        )

    def combine(index, source, low, grad):
        tile = item_tile[index]
        factor = jnp.exp2(top_buf[index] - top_ref[tile]) * share_ref[tile]
        probs = groups(probs_buf[index]) * factor[None]
        low[...] = probs.reshape(pair, width).astype(jnp.bfloat16)
        grad[...] = (
            (probs * (groups(source[...]) - delta_ref[tile][None]) * scale)
            .reshape(pair, width)
            .astype(jnp.bfloat16)
        )

    def add(index, low, grad):
        tile = item_tile[index]
        spot = area(index)
        dkv_acc[1, spot, :] += jnp.dot(
            low[...], g_rows[tile].reshape(width, HD), preferred_element_type=jnp.float32
        )
        dkv_acc[0, spot, :] += jnp.dot(
            grad[...], q_rows[tile].reshape(width, HD), preferred_element_type=jnp.float32
        )
        dq_acc[tile] += lax.dot_general(
            kv_ref[0, spot, :],
            grad[...],
            (((0,), (0,)), ((), ())),
            preferred_element_type=jnp.float32,
        )

    value_scores(0, scores_a)

    def add_two(index):
        value_scores(index + 1, scores_b)
        add(jnp.where(index == 0, items, index - 1), low_b, grad_b)
        combine(index, scores_a, low_a, grad_a)
        value_scores(index + 2, scores_a)
        add(index, low_a, grad_a)
        combine(index + 1, scores_b, low_b, grad_b)

    turns = (items + 1) // 2

    @pl.loop(0, turns // DEEP)
    def _(step):
        for part in range(DEEP):
            add_two(2 * (DEEP * step + part))

    @pl.loop(turns // DEEP * DEEP, turns)
    def _(step):
        add_two(2 * step)

    @pl.when(items % 2 == 0)
    def _():
        add(items - 1, low_b, grad_b)

    outs = [pltpu.make_async_copy(dkv_own.at[w], dkv_ref.at[w], sems.at[w]) for w in range(2)]
    for which in range(2):
        @pl.loop(0, count, unroll=4)
        def _(spot):
            place = position_ref[spot]
            dkv_own[which, tile_at(spot), :] = dkv_acc[which, tile_at(place), :].astype(
                jnp.bfloat16
            )

        outs[which].start()

    for tile in range(tiles):
        rows = slice(tile * TILE, (tile + 1) * TILE)
        for h in range(heads):
            lanes = slice(h * HD, (h + 1) * HD)
            dq_own[rows, lanes] = dq_acc[tile, :, lanes].T.astype(jnp.bfloat16)
        copy = pltpu.make_async_copy(dq_own.at[rows], dq_ref.at[rows], sems.at[2 + tile])
        copy.start()
        outs.append(copy)
    for copy in outs:
        copy.wait()


def attention_backward(positions, docs, team, q, g, delta, kv):
    rows, width = q.shape
    heads = width // HD
    tokens = kv.shape[1]
    tiles = rows // TILE
    count = tokens // TILE
    longest = count // 2
    most = sum(max(longest - i // 2 + 1, 2) // 2 for i in range(tiles)) + 4
    pair = SPAN * TILE
    smem = pl.BlockSpec(memory_space=pltpu.SMEM)
    hbm = pl.BlockSpec(memory_space=pl.ANY)
    slots = tiles + 1
    stat = pltpu.VMEM((slots, 8, width), jnp.float32)
    return pl.pallas_call(
        functools.partial(attention_kernel, heads, tiles, team),
        out_shape=(
            jax.ShapeDtypeStruct((rows, width), jnp.bfloat16),
            jax.ShapeDtypeStruct((2, tokens, HD), jnp.bfloat16),
        ),
        in_specs=[smem, smem, hbm, hbm, hbm, hbm],
        out_specs=(hbm, hbm),
        scratch_shapes=[
            pltpu.SMEM((count,), jnp.int32),
            pltpu.SMEM((most,), jnp.int32),
            pltpu.SMEM((most,), jnp.int32),
            pltpu.SMEM((most,), jnp.int32),
            pltpu.VMEM((slots, heads, TILE, HD), jnp.bfloat16),
            pltpu.VMEM((slots, heads, TILE, HD), jnp.bfloat16),
            pltpu.VMEM((slots, HD, width), jnp.bfloat16),
            pltpu.VMEM((slots, HD, width), jnp.bfloat16),
            pltpu.VMEM((slots, 1, width), jnp.float32),
            pltpu.VMEM((2, tokens + TILE, HD), jnp.bfloat16),
            pltpu.VMEM((pair, TILE), jnp.int32),
            pltpu.VMEM((pair, width), jnp.float32),
            pltpu.VMEM((pair, width), jnp.float32),
            pltpu.VMEM((pair, width), jnp.bfloat16),
            pltpu.VMEM((pair, width), jnp.bfloat16),
            pltpu.VMEM((pair, width), jnp.bfloat16),
            pltpu.VMEM((pair, width), jnp.bfloat16),
            pltpu.VMEM((most, pair, width), jnp.float32),
            pltpu.VMEM((most, 8, width), jnp.float32),
            stat,
            stat,
            stat,
            pltpu.VMEM((slots, HD, width), jnp.float32),
            pltpu.VMEM((2, tokens + TILE, HD), jnp.float32),
            pltpu.VMEM((rows, width), jnp.bfloat16),
            pltpu.VMEM((2, tokens, HD), jnp.bfloat16),
            pltpu.SemaphoreType.DMA((2 + max(2 * heads, tiles),)),
        ],
        compiler_params=pltpu.CompilerParams(vmem_limit_bytes=ATTENTION_LIMIT),
        cost_estimate=pl.CostEstimate(
            flops=rows * width * tokens * 3, bytes_accessed=12 << 20, transcendentals=0
        ),
    )(positions, docs, q.reshape(tiles, TILE, width), g.reshape(tiles, TILE, width), delta, kv)


def bring_kernel(
    team,
    planes,
    q_ref,
    g_ref,
    k_ref,
    v_ref,
    o_ref,
    q_out,
    g_out,
    delta_out,
    kv_out,
    kv_own,
    g_own,
    o_own,
    delta_own,
    load_sem,
    local_sem,
    flat_send,
    flat_recv,
    chain_send,
    chain_recv,
    core_send,
    core_recv,
):
    me = lax.axis_index("ctx")
    slot = me % team
    plane = me // team
    core = slot % 2
    mate = me + 1 - 2 * core
    width = q_out.shape[1]
    span = team * TILE
    tall = pl.ds(pl.multiple_of(slot * TILE, TILE), TILE)
    wide = pl.ds(pl.multiple_of(slot * width, HD), width)

    loads = [
        pltpu.make_async_copy(k_ref, kv_own.at[0], load_sem.at[0]),
        pltpu.make_async_copy(v_ref, kv_own.at[1], load_sem.at[1]),
        pltpu.make_async_copy(g_ref, g_own, load_sem.at[2]),
        pltpu.make_async_copy(o_ref, o_own, load_sem.at[3]),
    ]
    for load in loads:
        load.start()

    barrier = pltpu.get_barrier_semaphore()
    for shift in range(1, team):
        pl.semaphore_signal(
            barrier,
            inc=1,
            device_id=(plane * team + (slot + shift) % team, 0),
            device_id_type=MESH,
        )

    @pl.when(plane < planes - 1)
    def _():
        pl.semaphore_signal(barrier, inc=1, device_id=(me + team, 0), device_id_type=MESH)

    @pl.when(plane > 0)
    def _():
        pl.semaphore_signal(barrier, inc=1, device_id=(me - team, 0), device_id_type=MESH)

    near = jnp.where(plane < planes - 1, 1, 0) + jnp.where(plane > 0, 1, 0)
    pl.semaphore_wait(barrier, team - 1 + near)

    def flat(kind, shift, src, dst):
        return pltpu.make_async_remote_copy(
            src_ref=src,
            dst_ref=dst,
            send_sem=flat_send.at[kind, shift - 1],
            recv_sem=flat_recv.at[kind, slot],
            device_id=(plane * team + (slot + shift) % team, 0),
            device_id_type=MESH,
        )

    loads[0].wait()
    loads[1].wait()
    home = pl.ds(pl.multiple_of(me * TILE, TILE), TILE)
    flats = []
    for shift in range(1, team):
        other = (slot + shift) % team
        lanes = pl.ds(pl.multiple_of(other // 2 * HD, HD), HD)
        copy = flat(
            0, shift, kv_own.at[other % 2, :, lanes], kv_out.at[other % 2, home, :]
        )
        copy.start()
        flats.append(copy)
    locals_ = [
        pltpu.make_async_copy(
            kv_own.at[core, :, pl.ds(pl.multiple_of(slot // 2 * HD, HD), HD)],
            kv_out.at[core, home, :],
            local_sem.at[0],
        ),
        pltpu.make_async_copy(q_ref.at[:, wide], q_out.at[tall, :], local_sem.at[1]),
        pltpu.make_async_copy(g_ref.at[:, wide], g_out.at[tall, :], local_sem.at[2]),
    ]
    for copy in locals_:
        copy.start()
    rest = []
    for kind, (src, dst) in enumerate(((q_ref, q_out), (g_ref, g_out))):
        for shift in range(1, team):
            other = (slot + shift) % team
            lanes = pl.ds(pl.multiple_of(other * width, HD), width)
            copy = flat(1 + kind, shift, src.at[:, lanes], dst.at[tall, :])
            copy.start()
            rest.append(copy)
    locals_[0].wait()
    part_rows = span // SUB
    per_part = team // SUB

    def arrived(kind, source, dst):
        return pltpu.make_async_remote_copy(
            src_ref=dst,
            dst_ref=dst,
            send_sem=flat_send.at[kind, 0],
            recv_sem=flat_recv.at[kind, source],
            device_id=(mate, 0),
            device_id_type=MESH,
        )

    def part(which, sub):
        first = pl.multiple_of(which * span + sub * part_rows, TILE)
        return kv_out.at[core, pl.ds(first, part_rows), :]

    def chain(way, step, which, sub):
        return pltpu.make_async_remote_copy(
            src_ref=part(which, sub),
            dst_ref=part(which, sub),
            send_sem=chain_send.at[way, step, sub],
            recv_sem=chain_recv.at[way, step, sub],
            device_id=(me + team - 2 * way * team, 0),
            device_id_type=MESH,
        )

    def share(index, which, sub):
        return pltpu.make_async_remote_copy(
            src_ref=part(which, sub),
            dst_ref=part(which, sub),
            send_sem=core_send.at[index, sub],
            recv_sem=core_recv.at[index, sub],
            device_id=(mate, 0),
            device_id_type=MESH,
        )

    def up_ok(step):
        return (plane < planes - 1) & (plane - step >= 0)

    def down_ok(step):
        return (plane > 0) & (plane + step <= planes - 1)

    def up_come(step):
        return plane - 1 - step >= 0

    def down_come(step):
        return plane + 1 + step <= planes - 1

    for sub in range(SUB):
        for source in range(sub * per_part, (sub + 1) * per_part):
            @pl.when(slot != source)
            def _():
                arrived(0, source, kv_out.at[core, home, :]).wait_recv()

        @pl.when(up_ok(0))
        def _():
            chain(0, 0, plane, sub).start()

        @pl.when(down_ok(0))
        def _():
            chain(1, 0, plane, sub).start()

        share(0, plane, sub).start()

    loads[2].wait()
    loads[3].wait()
    for index in range(team):
        for head in range(width // HD):
            lanes = slice(index * width + head * HD, index * width + (head + 1) * HD)
            product = g_own[:, lanes].astype(jnp.float32) * o_own[:, lanes].astype(jnp.float32)
            row = jnp.sum(product.T, axis=0, keepdims=True)
            delta_own[index, :, head * HD : (head + 1) * HD] = row
    for shift in range(1, team):
        other = (slot + shift) % team
        copy = flat(3, shift, delta_own.at[other], delta_out.at[slot])
        copy.start()
        rest.append(copy)
    own_delta = pltpu.make_async_copy(delta_own.at[slot], delta_out.at[slot], local_sem.at[3])
    own_delta.start()

    for step in range(planes - 1):
        for sub in range(SUB):
            @pl.when(up_come(step))
            def _():
                chain(0, step, plane - 1 - step, sub).wait_recv()
                if step < planes - 2:
                    @pl.when(up_ok(step + 1))
                    def _():
                        chain(0, step + 1, plane - 1 - step, sub).start()
                share(1 + step, plane - 1 - step, sub).start()

            @pl.when(down_come(step))
            def _():
                chain(1, step, plane + 1 + step, sub).wait_recv()
                if step < planes - 2:
                    @pl.when(down_ok(step + 1))
                    def _():
                        chain(1, step + 1, plane + 1 + step, sub).start()
                share(planes + step, plane + 1 + step, sub).start()

    for sub in range(SUB):
        share(0, plane, sub).wait()
        for step in range(planes - 1):
            @pl.when(up_come(step))
            def _():
                share(1 + step, plane - 1 - step, sub).wait()

            @pl.when(down_come(step))
            def _():
                share(planes + step, plane + 1 + step, sub).wait()

            @pl.when(up_ok(step))
            def _():
                chain(0, step, plane - step, sub).wait_send()

            @pl.when(down_ok(step))
            def _():
                chain(1, step, plane + step, sub).wait_send()

    for copy in locals_[1:] + [own_delta]:
        copy.wait()
    for copy in rest + flats:
        copy.wait_send()
    for source in range(team):
        @pl.when(slot != source)
        def _():
            arrived(1, source, q_out.at[tall, :]).wait_recv()
            arrived(2, source, g_out.at[tall, :]).wait_recv()
            arrived(3, source, delta_out.at[slot]).wait_recv()


def bring(team, planes, queries, out_grad, key_states, value_states, outputs):
    rows, columns = queries.shape
    width = columns // team
    tokens = rows * team * planes
    vmem = pl.BlockSpec(memory_space=pltpu.VMEM)
    hbm = pl.BlockSpec(memory_space=pltpu.HBM)
    dma = pltpu.SemaphoreType.DMA
    return pl.pallas_call(
        functools.partial(bring_kernel, team, planes),
        out_shape=(
            jax.ShapeDtypeStruct((rows * team, width), jnp.bfloat16),
            jax.ShapeDtypeStruct((rows * team, width), jnp.bfloat16),
            jax.ShapeDtypeStruct((team, 1, width), jnp.float32),
            jax.ShapeDtypeStruct((2, tokens, HD), jnp.bfloat16),
        ),
        in_specs=[hbm, hbm, hbm, hbm, hbm],
        out_specs=(hbm, hbm, hbm, hbm),
        scratch_shapes=[
            pltpu.VMEM((2, rows, key_states.shape[1]), jnp.bfloat16),
            pltpu.VMEM((rows, columns), jnp.bfloat16),
            pltpu.VMEM((rows, columns), jnp.bfloat16),
            pltpu.VMEM((team, 1, width), jnp.float32),
            dma((4,)),
            dma((4,)),
            dma((4, team - 1)),
            dma((4, team)),
            dma((2, planes - 1, SUB)),
            dma((2, planes - 1, SUB)),
            dma((2 * planes - 1, SUB)),
            dma((2 * planes - 1, SUB)),
        ],
        compiler_params=pltpu.CompilerParams(
            collective_id=0, has_side_effects=True, vmem_limit_bytes=60 * 1024 * 1024
        ),
        cost_estimate=pl.CostEstimate(flops=0, bytes_accessed=60 << 20, transcendentals=0),
    )(queries, out_grad, key_states, value_states, outputs)


def return_kernel(
    team,
    planes,
    dq_ref,
    dkv_ref,
    dq_out,
    dkv_out,
    own,
    mate_in,
    chain_in,
    chain_own,
    total,
    local_sem,
    dq_send,
    dq_recv,
    flat_send,
    flat_recv,
    chain_send,
    chain_recv,
    core_send,
    core_recv,
):
    me = lax.axis_index("ctx")
    slot = me % team
    plane = me // team
    core = slot % 2
    mate = me + 1 - 2 * core
    width = dq_ref.shape[1]
    part_rows = TILE // FINE

    load = pltpu.make_async_copy(dkv_ref.at[core], own, local_sem.at[2])
    load.start()
    barrier = pltpu.get_barrier_semaphore()
    for shift in range(1, team):
        pl.semaphore_signal(
            barrier,
            inc=1,
            device_id=(plane * team + (slot + shift) % team, 0),
            device_id_type=MESH,
        )

    @pl.when(plane < planes - 1)
    def _():
        pl.semaphore_signal(barrier, inc=1, device_id=(me + team, 0), device_id_type=MESH)

    @pl.when(plane > 0)
    def _():
        pl.semaphore_signal(barrier, inc=1, device_id=(me - team, 0), device_id_type=MESH)

    near = jnp.where(plane < planes - 1, 1, 0) + jnp.where(plane > 0, 1, 0)
    pl.semaphore_wait(barrier, team - 1 + near)

    def inner(sub):
        return pl.ds(sub * part_rows, part_rows)

    def tile_rows(which):
        return pl.ds(pl.multiple_of(which * TILE, TILE), TILE)

    half = plane // (planes // 2)
    depth = plane * (1 - half) + (planes - 1 - plane) * half
    ahead = me + team * (1 - 2 * half)
    behind = me - team * (1 - 2 * half)

    def target_plane(index):
        return (planes - 1 - index) * (1 - half) + index * half

    shares = {}
    for index in range(planes):
        for sub in range(FINE):
            copy = pltpu.make_async_remote_copy(
                src_ref=dkv_ref.at[1 - core, target_plane(index), :, inner(sub), :],
                dst_ref=mate_in.at[index, :, inner(sub), :],
                send_sem=core_send.at[index, sub],
                recv_sem=core_recv.at[index, sub],
                device_id=(mate, 0),
                device_id_type=MESH,
            )
            shares[index, sub] = copy
    for sub in range(FINE):
        shares[0, sub].start()

    wide = pl.ds(pl.multiple_of(slot * width, HD), width)
    rest = []
    own_dq = pltpu.make_async_copy(
        dq_ref.at[tile_rows(slot), :], dq_out.at[:, wide], local_sem.at[0]
    )
    own_dq.start()
    for shift in range(1, team):
        other = (slot + shift) % team
        copy = pltpu.make_async_remote_copy(
            src_ref=dq_ref.at[tile_rows(other), :],
            dst_ref=dq_out.at[:, wide],
            send_sem=dq_send.at[shift - 1],
            recv_sem=dq_recv.at[shift - 1],
            device_id=(plane * team + other, 0),
            device_id_type=MESH,
        )
        copy.start()
        rest.append(copy)

    def chain(source, into, index, sub, device):
        return pltpu.make_async_remote_copy(
            src_ref=chain_own.at[source, index, :, inner(sub), :],
            dst_ref=chain_in.at[into, index, :, inner(sub), :],
            send_sem=chain_send.at[source, index, sub],
            recv_sem=chain_recv.at[into, index, sub],
            device_id=(device, 0),
            device_id_type=MESH,
        )

    def local_sum(index, sub):
        shares[index, sub].wait_recv()
        return own[target_plane(index), :, inner(sub), :].astype(jnp.float32) + mate_in[
            index, :, inner(sub), :
        ].astype(jnp.float32)

    def come(way, index, sub):
        chain(0, way, index, sub, mate).wait_recv()
        return chain_in[way, index, :, inner(sub), :].astype(jnp.float32)

    load.wait()
    for sub in range(FINE):
        shares[0, sub].wait_send()
    for index in (planes - 1, *range(1, planes - 1)):
        for sub in range(FINE):
            shares[index, sub].start()
    lanes = pl.ds(pl.multiple_of(slot // 2 * HD, HD), HD)
    def flat(shift, sub):
        target = (slot + shift) % team
        return pltpu.make_async_remote_copy(
            src_ref=total.at[target, inner(sub), :],
            dst_ref=dkv_out.at[core, inner(sub), lanes],
            send_sem=flat_send.at[shift - 1, sub],
            recv_sem=flat_recv.at[shift - 1, sub],
            device_id=(plane * team + target, 0),
            device_id_type=MESH,
        )

    def finish(value, sub):
        total[:, inner(sub), :] = value.astype(jnp.bfloat16)
        for shift in range(1, team):
            flat(shift, sub).start()

    pieces = [(index, sub) for index in range(planes - 1) for sub in range(FINE)]

    @pl.when(depth == 0)
    def _():
        moves = []
        for index, sub in pieces:
            chain_own[0, index, :, inner(sub), :] = local_sum(index, sub).astype(jnp.bfloat16)
            if len(moves) >= FLIGHT:
                moves[-FLIGHT].wait_send()
            move = chain(0, 0, index, sub, ahead)
            move.start()
            moves.append(move)
        for sub in range(FINE):
            finish(local_sum(planes - 1, sub) + come(1, 0, sub), sub)
        for move in moves[-FLIGHT:]:
            move.wait_send()

    @pl.when(depth == 1)
    def _():
        moves = []
        near = [(0, 0, index, sub) for index in range(2) for sub in range(FINE)]
        far = [(1, 1, 0, sub) for sub in range(FINE)]
        line = near[:FINE]
        for step in range(FINE):
            line.extend((far[step], near[FINE + step]))
        for way, source, index, sub in line:
            share = planes - 1 if way else index
            chain_own[source, index, :, inner(sub), :] = (
                local_sum(share, sub) + come(way, index, sub)
            ).astype(jnp.bfloat16)
            move = chain(source, 1, index, sub, behind if way else ahead)
            move.start()
            moves.append(move)
        for sub in range(FINE):
            finish(local_sum(2, sub) + come(1, 1, sub) + come(0, 2, sub), sub)
        for move in moves:
            move.wait_send()

    own_dkv = pltpu.make_async_copy(
        total.at[slot], dkv_out.at[core, :, lanes], local_sem.at[1]
    )
    own_dkv.start()
    own_dq.wait()
    own_dkv.wait()
    for index in range(1, planes):
        for sub in range(FINE):
            shares[index, sub].wait_send()
    for copy in rest:
        copy.wait()
    for sub in range(FINE):
        for shift in range(1, team):
            flat(shift, sub).wait()


def give_back(team, planes, dq, dkv):
    tall, width = dq.shape
    rows = tall // team
    heads = team // 2
    hbm = pl.BlockSpec(memory_space=pl.ANY)
    dma = pltpu.SemaphoreType.DMA
    part = pltpu.VMEM((2, planes - 1, team, rows, HD), jnp.bfloat16)
    return pl.pallas_call(
        functools.partial(return_kernel, team, planes),
        out_shape=(
            jax.ShapeDtypeStruct((rows, width * team), jnp.bfloat16),
            jax.ShapeDtypeStruct((2, rows, heads * HD), jnp.bfloat16),
        ),
        in_specs=[hbm, hbm],
        out_specs=(hbm, hbm),
        scratch_shapes=[
            pltpu.VMEM((planes, team, rows, HD), jnp.bfloat16),
            pltpu.VMEM((planes, team, rows, HD), jnp.bfloat16),
            part,
            part,
            pltpu.VMEM((team, rows, HD), jnp.bfloat16),
            dma((3,)),
            dma((team - 1,)),
            dma((team - 1,)),
            dma((team - 1, FINE)),
            dma((team - 1, FINE)),
            dma((2, planes - 1, FINE)),
            dma((2, planes - 1, FINE)),
            dma((planes, FINE)),
            dma((planes, FINE)),
        ],
        compiler_params=pltpu.CompilerParams(
            collective_id=1, has_side_effects=True, vmem_limit_bytes=GIVE_LIMIT
        ),
        cost_estimate=pl.CostEstimate(flops=0, bytes_accessed=60 << 20, transcendentals=0),
    )(dq, dkv.reshape(2, planes, team, rows, HD))


def local_planes(queries, key_states, value_states, outputs, out_grad, doc_of_tile, tile_position):
    team = 2 * (key_states.shape[1] // HD)
    planes = lax.axis_size("ctx") // team
    q, g, delta, kv = bring(team, planes, queries, out_grad, key_states, value_states, outputs)
    dq, dkv = attention_backward(tile_position, doc_of_tile, team, q, g, delta, kv)
    dq, dkv = give_back(team, planes, dq, dkv)
    return dq, dkv[0], dkv[1]


def local_any(queries, key_states, value_states, outputs, out_grad, doc_of_tile, tile_position):
    rows = queries.shape[0]
    kv_heads = key_states.shape[1] // HD
    head_count = lax.axis_size("head")
    ctx_count = lax.axis_size("ctx")
    ctx_index = lax.axis_index("ctx")
    split = kv_heads * head_count
    team = kv_heads
    parts = ctx_count // team
    near = [[b * team + s for s in range(team)] for b in range(parts)]
    far = [[b * team + s for b in range(parts)] for s in range(team)]

    def swap(value, split_axis, concat_axis):
        if head_count > 1:
            return lax.all_to_all(value, "head", split_axis, concat_axis, tiled=True)
        return lax.all_to_all(
            value, "ctx", split_axis, concat_axis, axis_index_groups=near, tiled=True
        )

    heads = queries.shape[1] // split // HD
    products = out_grad.astype(jnp.float32) * outputs.astype(jnp.float32)
    delta = jnp.sum(products.reshape(rows, split * heads, HD), axis=-1)
    kv = jnp.concatenate([key_states, value_states], axis=1)
    if head_count == 1:
        kv = kv.reshape(rows, 2, team, HD).transpose(0, 2, 1, 3).reshape(rows, team * 2 * HD)
        kv = swap(kv, 1, 0)
    kv = lax.all_gather(kv, "ctx", axis=0, tiled=True, axis_index_groups=far)
    kv = kv.reshape(-1, 2, HD).transpose(1, 0, 2)
    qd = jnp.concatenate(
        [
            queries.reshape(rows, split, heads * HD),
            out_grad.reshape(rows, split, heads * HD),
        ],
        axis=2,
    ).reshape(rows, split * 2 * heads * HD)
    qd = swap(qd, 1, 0)
    delta = swap(delta, 1, 0)
    tiles = qd.shape[0] // TILE
    delta = jnp.transpose(delta.reshape(tiles, TILE, heads), (0, 2, 1)).reshape(
        tiles, 1, heads * TILE
    )
    width = heads * HD
    dq, dkv = attention_backward(
        tile_position, doc_of_tile, team, qd[:, :width], qd[:, width:], delta, kv
    )
    if head_count == 1:
        dq = swap(dq, 0, 1)
    dkv = dkv.transpose(1, 0, 2).reshape(-1, 2 * HD)
    dkv = lax.all_to_all(dkv, "ctx", 0, 0, axis_index_groups=far, tiled=True)
    dkv = jnp.sum(dkv.reshape(parts, -1, 2 * HD).astype(jnp.float32), axis=0).astype(jnp.bfloat16)
    if head_count == 1:
        dkv = swap(dkv, 0, 1)
    dkv = dkv.reshape(dkv.shape[0], kv_heads, 2, HD)
    return (
        dq,
        dkv[:, :, 0].reshape(-1, kv_heads * HD),
        dkv[:, :, 1].reshape(-1, kv_heads * HD),
    )


def solution(mesh):
    placed = (
        P(("ctx", "head"), None),
        P("ctx", "head"),
        P("ctx", "head"),
        P(("ctx", "head"), None),
        P(("ctx", "head"), None),
        P(),
        P(),
    )
    slabs = mesh.shape["head"] == 1 and mesh.shape["ctx"] == 32
    return jax.shard_map(
        local_planes if slabs else local_any,
        mesh=mesh,
        in_specs=placed,
        out_specs=(P("ctx", "head"), P("ctx", "head"), P("ctx", "head")),
        check_vma=False,
    )
```

```python
import functools

import jax
import jax.numpy as jnp
from jax import lax
from jax.experimental import pallas as pl
from jax.experimental.pallas import tpu as pltpu
from jax.sharding import PartitionSpec as P

HD = 128
TILE = 128
SPAN = 2
LOW = -1e30
LOG2E = 1.4426950408889634
DEEP = 4
SUB = 2
FINE = 2
FLIGHT = 2
GIVE_LIMIT = 52 * 1024 * 1024
ATTENTION_LIMIT = 56 * 1024 * 1024
MESH = pl.DeviceIdType.MESH


def attention_kernel(
    heads,
    tiles,
    team,
    position_ref,
    doc_ref,
    q_hbm,
    g_hbm,
    delta_hbm,
    kv_hbm,
    dq_ref,
    dkv_ref,
    start_ref,
    item_tile,
    item_first,
    item_bound,
    q_rows,
    g_rows,
    q_cols,
    g_cols,
    delta_ref,
    kv_ref,
    gap_ref,
    scores_a,
    scores_b,
    low_a,
    low_b,
    grad_a,
    grad_b,
    probs_buf,
    top_buf,
    top_ref,
    total_ref,
    share_ref,
    dq_acc,
    dkv_acc,
    dq_own,
    dkv_own,
    sems,
):
    width = heads * HD
    scale = HD ** (-0.5)
    pair = SPAN * TILE
    count = position_ref.shape[0]
    block = lax.axis_index("ctx") // team

    def tile_at(index):
        return pl.ds(pl.multiple_of(index * TILE, TILE), TILE)

    heads_in = []
    for h in range(heads):
        lanes = slice(h * HD, (h + 1) * HD)
        for which, (src, dst) in enumerate(((q_hbm, q_rows), (g_hbm, g_rows))):
            copy = pltpu.make_async_copy(
                src.at[:, :, lanes], dst.at[0:tiles, h], sems.at[2 + 2 * h + which]
            )
            copy.start()
            heads_in.append(copy)
    delta_in = pltpu.make_async_copy(delta_hbm, delta_ref.at[0:tiles], sems.at[0])
    delta_in.start()

    @pl.loop(0, count)
    def _(spot):
        place = position_ref[spot]
        for which in range(2):
            pltpu.make_async_copy(
                kv_hbm.at[which, tile_at(spot), :],
                kv_ref.at[which, tile_at(place), :],
                sems.at[1],
            ).start()

    def find(index, start):
        fresh = doc_ref[index] != doc_ref[jnp.maximum(index - 1, 0)]
        start = jnp.where(fresh, index, start)
        start_ref[index] = start
        return start

    lax.fori_loop(0, count, find, jnp.int32(0))

    def put(index, tile, first, bound):
        item_tile[index] = tile
        item_first[index] = first
        item_bound[index] = bound

    def listed(tile, total):
        place = position_ref[block * tiles + tile]
        start = start_ref[place]
        full = (place - start) // 2
        put(tile, tile, start + 2 * full, (place - start - 2 * full) * TILE)

        @pl.loop(0, full)
        def _(step):
            put(total + step, tile, start + 2 * step, pair)

        return total + full

    items = lax.fori_loop(0, tiles, listed, jnp.int32(tiles))
    for extra in range(4):
        put(items + extra, tiles, 0, pair)

    gap_ref[...] = lax.broadcasted_iota(jnp.int32, (pair, TILE), 0) - lax.broadcasted_iota(
        jnp.int32, (pair, TILE), 1
    )
    dkv_acc[...] = jnp.zeros_like(dkv_acc)
    dq_acc[...] = jnp.zeros_like(dq_acc)
    top_ref[...] = jnp.full_like(top_ref, LOW)
    total_ref[...] = jnp.zeros_like(total_ref)
    q_cols[tiles] = jnp.zeros((HD, width), jnp.bfloat16)
    g_cols[tiles] = jnp.zeros((HD, width), jnp.bfloat16)
    q_rows[tiles] = jnp.zeros((heads, TILE, HD), jnp.bfloat16)
    g_rows[tiles] = jnp.zeros((heads, TILE, HD), jnp.bfloat16)
    delta_ref[tiles] = jnp.zeros((1, width), jnp.float32)
    kv_ref[:, count * TILE :, :] = jnp.zeros((2, TILE, HD), jnp.bfloat16)
    low_b[...] = jnp.zeros_like(low_b)
    grad_b[...] = jnp.zeros_like(grad_b)

    for copy in heads_in:
        copy.wait()

    @pl.loop(0, tiles, unroll=tiles)
    def _(tile):
        for h in range(heads):
            lanes = slice(h * HD, (h + 1) * HD)
            q_cols[tile, :, lanes] = q_rows[tile, h].T
            g_cols[tile, :, lanes] = g_rows[tile, h].T

    delta_in.wait()
    pltpu.make_async_copy(kv_hbm, kv_ref.at[:, 0 : count * TILE], sems.at[1]).wait()

    def groups(value):
        return value.reshape(value.shape[0] // 8, 8, width)

    def area(index):
        return pl.ds(pl.multiple_of(item_first[index] * TILE, TILE), pair)

    def score(index, into):
        into[...] = jnp.dot(
            kv_ref[0, area(index), :],
            q_cols[item_tile[index]],
            preferred_element_type=jnp.float32,
        )

    def weigh(index, source, edge):
        tile = item_tile[index]
        scores = source[...] * (scale * LOG2E)
        if edge:
            gap = jnp.concatenate([gap_ref[...]] * heads, axis=1)
            scores = jnp.where(gap <= item_bound[index], scores, LOW)
        scores = groups(scores)
        old = top_ref[tile]
        top = jnp.maximum(old, jnp.max(scores, axis=0))
        probs = jnp.exp2(scores - top[None])
        probs_buf[index] = probs.reshape(pair, width)
        top_buf[index] = top
        top_ref[tile] = top
        total_ref[tile] = total_ref[tile] * jnp.exp2(old - top) + jnp.sum(probs, axis=0)

    score(0, scores_a)

    def weigh_two(index, edge=False):
        score(index + 1, scores_b)
        weigh(index, scores_a, edge)
        score(index + 2, scores_a)
        weigh(index + 1, scores_b, edge)

    edges = (tiles + 1) // 2
    rounds = (items + 1) // 2
    for part in range(edges):
        weigh_two(2 * part, edge=True)
    deep = edges + (rounds - edges) // DEEP * DEEP

    @pl.loop(0, (rounds - edges) // DEEP)
    def _(step):
        for part in range(DEEP):
            weigh_two(2 * (edges + DEEP * step + part))

    @pl.loop(deep, rounds)
    def _(step):
        weigh_two(2 * step)

    for tile in range(tiles):
        top = top_ref[tile]
        peak = jnp.broadcast_to(jnp.max(top, axis=0, keepdims=True), (8, width))
        total = jnp.sum(total_ref[tile] * jnp.exp2(top - peak), axis=0, keepdims=True)
        top_ref[tile] = peak
        share_ref[tile] = 1.0 / jnp.broadcast_to(total, (8, width))
    top_ref[tiles] = jnp.zeros((8, width), jnp.float32)
    share_ref[tiles] = jnp.zeros((8, width), jnp.float32)
    for extra in range(2):
        probs_buf[items + extra] = jnp.zeros((pair, width), jnp.float32)
        top_buf[items + extra] = jnp.zeros((8, width), jnp.float32)

    def value_scores(index, into):
        into[...] = jnp.dot(
            kv_ref[1, area(index), :],
            g_cols[item_tile[index]],
            preferred_element_type=jnp.float32,
        )

    def combine(index, source, low, grad):
        tile = item_tile[index]
        factor = jnp.exp2(top_buf[index] - top_ref[tile]) * share_ref[tile]
        probs = groups(probs_buf[index]) * factor[None]
        low[...] = probs.reshape(pair, width).astype(jnp.bfloat16)
        grad[...] = (
            (probs * (groups(source[...]) - delta_ref[tile][None]) * scale)
            .reshape(pair, width)
            .astype(jnp.bfloat16)
        )

    def add(index, low, grad):
        tile = item_tile[index]
        spot = area(index)
        dkv_acc[1, spot, :] += jnp.dot(
            low[...], g_rows[tile].reshape(width, HD), preferred_element_type=jnp.float32
        )
        dkv_acc[0, spot, :] += jnp.dot(
            grad[...], q_rows[tile].reshape(width, HD), preferred_element_type=jnp.float32
        )
        dq_acc[tile] += lax.dot_general(
            kv_ref[0, spot, :],
            grad[...],
            (((0,), (0,)), ((), ())),
            preferred_element_type=jnp.float32,
        )

    value_scores(0, scores_a)

    def add_two(index):
        value_scores(index + 1, scores_b)
        add(jnp.where(index == 0, items, index - 1), low_b, grad_b)
        combine(index, scores_a, low_a, grad_a)
        value_scores(index + 2, scores_a)
        add(index, low_a, grad_a)
        combine(index + 1, scores_b, low_b, grad_b)

    turns = (items + 1) // 2

    @pl.loop(0, turns // DEEP)
    def _(step):
        for part in range(DEEP):
            add_two(2 * (DEEP * step + part))

    @pl.loop(turns // DEEP * DEEP, turns)
    def _(step):
        add_two(2 * step)

    @pl.when(items % 2 == 0)
    def _():
        add(items - 1, low_b, grad_b)

    outs = [pltpu.make_async_copy(dkv_own.at[w], dkv_ref.at[w], sems.at[w]) for w in range(2)]
    for which in range(2):
        @pl.loop(0, count, unroll=4)
        def _(spot):
            place = position_ref[spot]
            dkv_own[which, tile_at(spot), :] = dkv_acc[which, tile_at(place), :].astype(
                jnp.bfloat16
            )

        outs[which].start()

    for tile in range(tiles):
        rows = slice(tile * TILE, (tile + 1) * TILE)
        for h in range(heads):
            lanes = slice(h * HD, (h + 1) * HD)
            dq_own[rows, lanes] = dq_acc[tile, :, lanes].T.astype(jnp.bfloat16)
        copy = pltpu.make_async_copy(dq_own.at[rows], dq_ref.at[rows], sems.at[2 + tile])
        copy.start()
        outs.append(copy)
    for copy in outs:
        copy.wait()


def attention_backward(positions, docs, team, q, g, delta, kv):
    rows, width = q.shape
    heads = width // HD
    tokens = kv.shape[1]
    tiles = rows // TILE
    count = tokens // TILE
    longest = count // 2
    most = sum(max(longest - i // 2 + 1, 2) // 2 for i in range(tiles)) + 4
    pair = SPAN * TILE
    smem = pl.BlockSpec(memory_space=pltpu.SMEM)
    hbm = pl.BlockSpec(memory_space=pl.ANY)
    slots = tiles + 1
    stat = pltpu.VMEM((slots, 8, width), jnp.float32)
    return pl.pallas_call(
        functools.partial(attention_kernel, heads, tiles, team),
        out_shape=(
            jax.ShapeDtypeStruct((rows, width), jnp.bfloat16),
            jax.ShapeDtypeStruct((2, tokens, HD), jnp.bfloat16),
        ),
        in_specs=[smem, smem, hbm, hbm, hbm, hbm],
        out_specs=(hbm, hbm),
        scratch_shapes=[
            pltpu.SMEM((count,), jnp.int32),
            pltpu.SMEM((most,), jnp.int32),
            pltpu.SMEM((most,), jnp.int32),
            pltpu.SMEM((most,), jnp.int32),
            pltpu.VMEM((slots, heads, TILE, HD), jnp.bfloat16),
            pltpu.VMEM((slots, heads, TILE, HD), jnp.bfloat16),
            pltpu.VMEM((slots, HD, width), jnp.bfloat16),
            pltpu.VMEM((slots, HD, width), jnp.bfloat16),
            pltpu.VMEM((slots, 1, width), jnp.float32),
            pltpu.VMEM((2, tokens + TILE, HD), jnp.bfloat16),
            pltpu.VMEM((pair, TILE), jnp.int32),
            pltpu.VMEM((pair, width), jnp.float32),
            pltpu.VMEM((pair, width), jnp.float32),
            pltpu.VMEM((pair, width), jnp.bfloat16),
            pltpu.VMEM((pair, width), jnp.bfloat16),
            pltpu.VMEM((pair, width), jnp.bfloat16),
            pltpu.VMEM((pair, width), jnp.bfloat16),
            pltpu.VMEM((most, pair, width), jnp.float32),
            pltpu.VMEM((most, 8, width), jnp.float32),
            stat,
            stat,
            stat,
            pltpu.VMEM((slots, HD, width), jnp.float32),
            pltpu.VMEM((2, tokens + TILE, HD), jnp.float32),
            pltpu.VMEM((rows, width), jnp.bfloat16),
            pltpu.VMEM((2, tokens, HD), jnp.bfloat16),
            pltpu.SemaphoreType.DMA((2 + max(2 * heads, tiles),)),
        ],
        compiler_params=pltpu.CompilerParams(vmem_limit_bytes=ATTENTION_LIMIT),
        cost_estimate=pl.CostEstimate(
            flops=rows * width * tokens * 3, bytes_accessed=12 << 20, transcendentals=0
        ),
    )(positions, docs, q.reshape(tiles, TILE, width), g.reshape(tiles, TILE, width), delta, kv)


def bring_kernel(
    team,
    planes,
    q_ref,
    g_ref,
    k_ref,
    v_ref,
    o_ref,
    q_out,
    g_out,
    delta_out,
    kv_out,
    kv_own,
    g_own,
    o_own,
    delta_own,
    load_sem,
    local_sem,
    flat_send,
    flat_recv,
    chain_send,
    chain_recv,
    core_send,
    core_recv,
):
    me = lax.axis_index("ctx")
    slot = me % team
    plane = me // team
    core = slot % 2
    mate = me + 1 - 2 * core
    width = q_out.shape[1]
    span = team * TILE
    tall = pl.ds(pl.multiple_of(slot * TILE, TILE), TILE)
    wide = pl.ds(pl.multiple_of(slot * width, HD), width)

    loads = [
        pltpu.make_async_copy(k_ref, kv_own.at[0], load_sem.at[0]),
        pltpu.make_async_copy(v_ref, kv_own.at[1], load_sem.at[1]),
        pltpu.make_async_copy(g_ref, g_own, load_sem.at[2]),
        pltpu.make_async_copy(o_ref, o_own, load_sem.at[3]),
    ]
    for load in loads:
        load.start()

    barrier = pltpu.get_barrier_semaphore()
    for shift in range(1, team):
        pl.semaphore_signal(
            barrier,
            inc=1,
            device_id=(plane * team + (slot + shift) % team, 0),
            device_id_type=MESH,
        )

    @pl.when(plane < planes - 1)
    def _():
        pl.semaphore_signal(barrier, inc=1, device_id=(me + team, 0), device_id_type=MESH)

    @pl.when(plane > 0)
    def _():
        pl.semaphore_signal(barrier, inc=1, device_id=(me - team, 0), device_id_type=MESH)

    near = jnp.where(plane < planes - 1, 1, 0) + jnp.where(plane > 0, 1, 0)
    pl.semaphore_wait(barrier, team - 1 + near)

    def flat(kind, shift, src, dst):
        return pltpu.make_async_remote_copy(
            src_ref=src,
            dst_ref=dst,
            send_sem=flat_send.at[kind, shift - 1],
            recv_sem=flat_recv.at[kind, slot],
            device_id=(plane * team + (slot + shift) % team, 0),
            device_id_type=MESH,
        )

    loads[0].wait()
    loads[1].wait()
    home = pl.ds(pl.multiple_of(me * TILE, TILE), TILE)
    flats = []
    for shift in range(1, team):
        other = (slot + shift) % team
        lanes = pl.ds(pl.multiple_of(other // 2 * HD, HD), HD)
        copy = flat(
            0, shift, kv_own.at[other % 2, :, lanes], kv_out.at[other % 2, home, :]
        )
        copy.start()
        flats.append(copy)
    locals_ = [
        pltpu.make_async_copy(
            kv_own.at[core, :, pl.ds(pl.multiple_of(slot // 2 * HD, HD), HD)],
            kv_out.at[core, home, :],
            local_sem.at[0],
        ),
        pltpu.make_async_copy(q_ref.at[:, wide], q_out.at[tall, :], local_sem.at[1]),
        pltpu.make_async_copy(g_ref.at[:, wide], g_out.at[tall, :], local_sem.at[2]),
    ]
    for copy in locals_:
        copy.start()
    rest = []

    def spread(kind, source, dst):
        for shift in range(1, team):
            other = (slot + shift) % team
            lanes = pl.ds(pl.multiple_of(other * width, HD), width)
            copy = flat(kind, shift, source.at[:, lanes], dst.at[tall, :])
            copy.start()
            rest.append(copy)

    spread(1, q_ref, q_out)
    locals_[0].wait()
    part_rows = span // SUB
    per_part = team // SUB

    def arrived(kind, source, dst):
        return pltpu.make_async_remote_copy(
            src_ref=dst,
            dst_ref=dst,
            send_sem=flat_send.at[kind, 0],
            recv_sem=flat_recv.at[kind, source],
            device_id=(mate, 0),
            device_id_type=MESH,
        )

    def part(which, sub):
        first = pl.multiple_of(which * span + sub * part_rows, TILE)
        return kv_out.at[core, pl.ds(first, part_rows), :]

    def chain(way, step, which, sub):
        return pltpu.make_async_remote_copy(
            src_ref=part(which, sub),
            dst_ref=part(which, sub),
            send_sem=chain_send.at[way, step, sub],
            recv_sem=chain_recv.at[way, step, sub],
            device_id=(me + team - 2 * way * team, 0),
            device_id_type=MESH,
        )

    def share(index, which, sub):
        return pltpu.make_async_remote_copy(
            src_ref=part(which, sub),
            dst_ref=part(which, sub),
            send_sem=core_send.at[index, sub],
            recv_sem=core_recv.at[index, sub],
            device_id=(mate, 0),
            device_id_type=MESH,
        )

    def up_ok(step):
        return (plane < planes - 1) & (plane - step >= 0)

    def down_ok(step):
        return (plane > 0) & (plane + step <= planes - 1)

    def up_come(step):
        return plane - 1 - step >= 0

    def down_come(step):
        return plane + 1 + step <= planes - 1

    for sub in range(SUB):
        for source in range(sub * per_part, (sub + 1) * per_part):
            @pl.when(slot != source)
            def _():
                arrived(0, source, kv_out.at[core, home, :]).wait_recv()

        @pl.when(up_ok(0))
        def _():
            chain(0, 0, plane, sub).start()

        @pl.when(down_ok(0))
        def _():
            chain(1, 0, plane, sub).start()

        share(0, plane, sub).start()
        if sub == 0:
            spread(2, g_ref, g_out)

    loads[2].wait()
    loads[3].wait()
    for index in range(team):
        for head in range(width // HD):
            lanes = slice(index * width + head * HD, index * width + (head + 1) * HD)
            product = g_own[:, lanes].astype(jnp.float32) * o_own[:, lanes].astype(jnp.float32)
            row = jnp.sum(product.T, axis=0, keepdims=True)
            delta_own[index, :, head * HD : (head + 1) * HD] = row
    for shift in range(1, team):
        other = (slot + shift) % team
        copy = flat(3, shift, delta_own.at[other], delta_out.at[slot])
        copy.start()
        rest.append(copy)
    own_delta = pltpu.make_async_copy(delta_own.at[slot], delta_out.at[slot], local_sem.at[3])
    own_delta.start()

    for step in range(planes - 1):
        for sub in range(SUB):
            @pl.when(up_come(step))
            def _():
                chain(0, step, plane - 1 - step, sub).wait_recv()
                if step < planes - 2:
                    @pl.when(up_ok(step + 1))
                    def _():
                        chain(0, step + 1, plane - 1 - step, sub).start()
                share(1 + step, plane - 1 - step, sub).start()

            @pl.when(down_come(step))
            def _():
                chain(1, step, plane + 1 + step, sub).wait_recv()
                if step < planes - 2:
                    @pl.when(down_ok(step + 1))
                    def _():
                        chain(1, step + 1, plane + 1 + step, sub).start()
                share(planes + step, plane + 1 + step, sub).start()

    for sub in range(SUB):
        share(0, plane, sub).wait()
        for step in range(planes - 1):
            @pl.when(up_come(step))
            def _():
                share(1 + step, plane - 1 - step, sub).wait()

            @pl.when(down_come(step))
            def _():
                share(planes + step, plane + 1 + step, sub).wait()

            @pl.when(up_ok(step))
            def _():
                chain(0, step, plane - step, sub).wait_send()

            @pl.when(down_ok(step))
            def _():
                chain(1, step, plane + step, sub).wait_send()

    for copy in locals_[1:] + [own_delta]:
        copy.wait()
    for copy in rest + flats:
        copy.wait_send()
    for source in range(team):
        @pl.when(slot != source)
        def _():
            arrived(1, source, q_out.at[tall, :]).wait_recv()
            arrived(2, source, g_out.at[tall, :]).wait_recv()
            arrived(3, source, delta_out.at[slot]).wait_recv()


def bring(team, planes, queries, out_grad, key_states, value_states, outputs):
    rows, columns = queries.shape
    width = columns // team
    tokens = rows * team * planes
    vmem = pl.BlockSpec(memory_space=pltpu.VMEM)
    hbm = pl.BlockSpec(memory_space=pltpu.HBM)
    dma = pltpu.SemaphoreType.DMA
    return pl.pallas_call(
        functools.partial(bring_kernel, team, planes),
        out_shape=(
            jax.ShapeDtypeStruct((rows * team, width), jnp.bfloat16),
            jax.ShapeDtypeStruct((rows * team, width), jnp.bfloat16),
            jax.ShapeDtypeStruct((team, 1, width), jnp.float32),
            jax.ShapeDtypeStruct((2, tokens, HD), jnp.bfloat16),
        ),
        in_specs=[hbm, hbm, hbm, hbm, hbm],
        out_specs=(hbm, hbm, hbm, hbm),
        scratch_shapes=[
            pltpu.VMEM((2, rows, key_states.shape[1]), jnp.bfloat16),
            pltpu.VMEM((rows, columns), jnp.bfloat16),
            pltpu.VMEM((rows, columns), jnp.bfloat16),
            pltpu.VMEM((team, 1, width), jnp.float32),
            dma((4,)),
            dma((4,)),
            dma((4, team - 1)),
            dma((4, team)),
            dma((2, planes - 1, SUB)),
            dma((2, planes - 1, SUB)),
            dma((2 * planes - 1, SUB)),
            dma((2 * planes - 1, SUB)),
        ],
        compiler_params=pltpu.CompilerParams(
            collective_id=0, has_side_effects=True, vmem_limit_bytes=60 * 1024 * 1024
        ),
        cost_estimate=pl.CostEstimate(flops=0, bytes_accessed=60 << 20, transcendentals=0),
    )(queries, out_grad, key_states, value_states, outputs)


def return_kernel(
    team,
    planes,
    dq_ref,
    dkv_ref,
    dq_out,
    dkv_out,
    own,
    mate_in,
    chain_in,
    chain_own,
    total,
    local_sem,
    dq_send,
    dq_recv,
    flat_send,
    flat_recv,
    chain_send,
    chain_recv,
    core_send,
    core_recv,
):
    me = lax.axis_index("ctx")
    slot = me % team
    plane = me // team
    core = slot % 2
    mate = me + 1 - 2 * core
    width = dq_ref.shape[1]
    part_rows = TILE // FINE

    load = pltpu.make_async_copy(dkv_ref.at[core], own, local_sem.at[2])
    load.start()
    barrier = pltpu.get_barrier_semaphore()
    for shift in range(1, team):
        pl.semaphore_signal(
            barrier,
            inc=1,
            device_id=(plane * team + (slot + shift) % team, 0),
            device_id_type=MESH,
        )

    @pl.when(plane < planes - 1)
    def _():
        pl.semaphore_signal(barrier, inc=1, device_id=(me + team, 0), device_id_type=MESH)

    @pl.when(plane > 0)
    def _():
        pl.semaphore_signal(barrier, inc=1, device_id=(me - team, 0), device_id_type=MESH)

    near = jnp.where(plane < planes - 1, 1, 0) + jnp.where(plane > 0, 1, 0)
    pl.semaphore_wait(barrier, team - 1 + near)

    def inner(sub):
        return pl.ds(sub * part_rows, part_rows)

    def tile_rows(which):
        return pl.ds(pl.multiple_of(which * TILE, TILE), TILE)

    half = plane // (planes // 2)
    depth = plane * (1 - half) + (planes - 1 - plane) * half
    ahead = me + team * (1 - 2 * half)
    behind = me - team * (1 - 2 * half)

    def target_plane(index):
        return (planes - 1 - index) * (1 - half) + index * half

    shares = {}
    for index in range(planes):
        for sub in range(FINE):
            copy = pltpu.make_async_remote_copy(
                src_ref=dkv_ref.at[1 - core, target_plane(index), :, inner(sub), :],
                dst_ref=mate_in.at[index, :, inner(sub), :],
                send_sem=core_send.at[index, sub],
                recv_sem=core_recv.at[index, sub],
                device_id=(mate, 0),
                device_id_type=MESH,
            )
            shares[index, sub] = copy
    for sub in range(FINE):
        shares[0, sub].start()

    wide = pl.ds(pl.multiple_of(slot * width, HD), width)
    rest = []
    own_dq = pltpu.make_async_copy(
        dq_ref.at[tile_rows(slot), :], dq_out.at[:, wide], local_sem.at[0]
    )
    own_dq.start()
    for shift in range(1, team):
        other = (slot + shift) % team
        copy = pltpu.make_async_remote_copy(
            src_ref=dq_ref.at[tile_rows(other), :],
            dst_ref=dq_out.at[:, wide],
            send_sem=dq_send.at[shift - 1],
            recv_sem=dq_recv.at[shift - 1],
            device_id=(plane * team + other, 0),
            device_id_type=MESH,
        )
        copy.start()
        rest.append(copy)

    def chain(source, into, index, sub, device):
        return pltpu.make_async_remote_copy(
            src_ref=chain_own.at[source, index, :, inner(sub), :],
            dst_ref=chain_in.at[into, index, :, inner(sub), :],
            send_sem=chain_send.at[source, index, sub],
            recv_sem=chain_recv.at[into, index, sub],
            device_id=(device, 0),
            device_id_type=MESH,
        )

    def local_sum(index, sub):
        shares[index, sub].wait_recv()
        return own[target_plane(index), :, inner(sub), :].astype(jnp.float32) + mate_in[
            index, :, inner(sub), :
        ].astype(jnp.float32)

    def come(way, index, sub):
        chain(0, way, index, sub, mate).wait_recv()
        return chain_in[way, index, :, inner(sub), :].astype(jnp.float32)

    load.wait()
    for sub in range(FINE):
        shares[0, sub].wait_send()
    for index in (planes - 1, *range(1, planes - 1)):
        for sub in range(FINE):
            shares[index, sub].start()
    lanes = pl.ds(pl.multiple_of(slot // 2 * HD, HD), HD)
    def flat(shift, sub):
        target = (slot + shift) % team
        return pltpu.make_async_remote_copy(
            src_ref=total.at[target, inner(sub), :],
            dst_ref=dkv_out.at[core, inner(sub), lanes],
            send_sem=flat_send.at[shift - 1, sub],
            recv_sem=flat_recv.at[shift - 1, sub],
            device_id=(plane * team + target, 0),
            device_id_type=MESH,
        )

    def finish(value, sub):
        total[:, inner(sub), :] = value.astype(jnp.bfloat16)
        for shift in range(1, team):
            flat(shift, sub).start()

    pieces = [(index, sub) for index in range(planes - 1) for sub in range(FINE)]

    @pl.when(depth == 0)
    def _():
        moves = []
        for index, sub in pieces:
            chain_own[0, index, :, inner(sub), :] = local_sum(index, sub).astype(jnp.bfloat16)
            if len(moves) >= FLIGHT:
                moves[-FLIGHT].wait_send()
            move = chain(0, 0, index, sub, ahead)
            move.start()
            moves.append(move)
        for sub in range(FINE):
            finish(local_sum(planes - 1, sub) + come(1, 0, sub), sub)
        for move in moves[-FLIGHT:]:
            move.wait_send()

    @pl.when(depth == 1)
    def _():
        moves = []
        near = [(0, 0, index, sub) for index in range(2) for sub in range(FINE)]
        far = [(1, 1, 0, sub) for sub in range(FINE)]
        line = near[:FINE]
        for step in range(FINE):
            line.extend((far[step], near[FINE + step]))
        for way, source, index, sub in line:
            share = planes - 1 if way else index
            chain_own[source, index, :, inner(sub), :] = (
                local_sum(share, sub) + come(way, index, sub)
            ).astype(jnp.bfloat16)
            move = chain(source, 1, index, sub, behind if way else ahead)
            move.start()
            moves.append(move)
        for sub in range(FINE):
            finish(local_sum(2, sub) + come(1, 1, sub) + come(0, 2, sub), sub)
        for move in moves:
            move.wait_send()

    own_dkv = pltpu.make_async_copy(
        total.at[slot], dkv_out.at[core, :, lanes], local_sem.at[1]
    )
    own_dkv.start()
    own_dq.wait()
    own_dkv.wait()
    for index in range(1, planes):
        for sub in range(FINE):
            shares[index, sub].wait_send()
    for copy in rest:
        copy.wait()
    for sub in range(FINE):
        for shift in range(1, team):
            flat(shift, sub).wait()


def give_back(team, planes, dq, dkv):
    tall, width = dq.shape
    rows = tall // team
    heads = team // 2
    hbm = pl.BlockSpec(memory_space=pl.ANY)
    dma = pltpu.SemaphoreType.DMA
    part = pltpu.VMEM((2, planes - 1, team, rows, HD), jnp.bfloat16)
    return pl.pallas_call(
        functools.partial(return_kernel, team, planes),
        out_shape=(
            jax.ShapeDtypeStruct((rows, width * team), jnp.bfloat16),
            jax.ShapeDtypeStruct((2, rows, heads * HD), jnp.bfloat16),
        ),
        in_specs=[hbm, hbm],
        out_specs=(hbm, hbm),
        scratch_shapes=[
            pltpu.VMEM((planes, team, rows, HD), jnp.bfloat16),
            pltpu.VMEM((planes, team, rows, HD), jnp.bfloat16),
            part,
            part,
            pltpu.VMEM((team, rows, HD), jnp.bfloat16),
            dma((3,)),
            dma((team - 1,)),
            dma((team - 1,)),
            dma((team - 1, FINE)),
            dma((team - 1, FINE)),
            dma((2, planes - 1, FINE)),
            dma((2, planes - 1, FINE)),
            dma((planes, FINE)),
            dma((planes, FINE)),
        ],
        compiler_params=pltpu.CompilerParams(
            collective_id=1, has_side_effects=True, vmem_limit_bytes=GIVE_LIMIT
        ),
        cost_estimate=pl.CostEstimate(flops=0, bytes_accessed=60 << 20, transcendentals=0),
    )(dq, dkv.reshape(2, planes, team, rows, HD))


def local_planes(queries, key_states, value_states, outputs, out_grad, doc_of_tile, tile_position):
    team = 2 * (key_states.shape[1] // HD)
    planes = lax.axis_size("ctx") // team
    q, g, delta, kv = bring(team, planes, queries, out_grad, key_states, value_states, outputs)
    dq, dkv = attention_backward(tile_position, doc_of_tile, team, q, g, delta, kv)
    dq, dkv = give_back(team, planes, dq, dkv)
    return dq, dkv[0], dkv[1]


def local_any(queries, key_states, value_states, outputs, out_grad, doc_of_tile, tile_position):
    rows = queries.shape[0]
    kv_heads = key_states.shape[1] // HD
    head_count = lax.axis_size("head")
    ctx_count = lax.axis_size("ctx")
    ctx_index = lax.axis_index("ctx")
    split = kv_heads * head_count
    team = kv_heads
    parts = ctx_count // team
    near = [[b * team + s for s in range(team)] for b in range(parts)]
    far = [[b * team + s for b in range(parts)] for s in range(team)]

    def swap(value, split_axis, concat_axis):
        if head_count > 1:
            return lax.all_to_all(value, "head", split_axis, concat_axis, tiled=True)
        return lax.all_to_all(
            value, "ctx", split_axis, concat_axis, axis_index_groups=near, tiled=True
        )

    heads = queries.shape[1] // split // HD
    products = out_grad.astype(jnp.float32) * outputs.astype(jnp.float32)
    delta = jnp.sum(products.reshape(rows, split * heads, HD), axis=-1)
    kv = jnp.concatenate([key_states, value_states], axis=1)
    if head_count == 1:
        kv = kv.reshape(rows, 2, team, HD).transpose(0, 2, 1, 3).reshape(rows, team * 2 * HD)
        kv = swap(kv, 1, 0)
    kv = lax.all_gather(kv, "ctx", axis=0, tiled=True, axis_index_groups=far)
    kv = kv.reshape(-1, 2, HD).transpose(1, 0, 2)
    qd = jnp.concatenate(
        [
            queries.reshape(rows, split, heads * HD),
            out_grad.reshape(rows, split, heads * HD),
        ],
        axis=2,
    ).reshape(rows, split * 2 * heads * HD)
    qd = swap(qd, 1, 0)
    delta = swap(delta, 1, 0)
    tiles = qd.shape[0] // TILE
    delta = jnp.transpose(delta.reshape(tiles, TILE, heads), (0, 2, 1)).reshape(
        tiles, 1, heads * TILE
    )
    width = heads * HD
    dq, dkv = attention_backward(
        tile_position, doc_of_tile, team, qd[:, :width], qd[:, width:], delta, kv
    )
    if head_count == 1:
        dq = swap(dq, 0, 1)
    dkv = dkv.transpose(1, 0, 2).reshape(-1, 2 * HD)
    dkv = lax.all_to_all(dkv, "ctx", 0, 0, axis_index_groups=far, tiled=True)
    dkv = jnp.sum(dkv.reshape(parts, -1, 2 * HD).astype(jnp.float32), axis=0).astype(jnp.bfloat16)
    if head_count == 1:
        dkv = swap(dkv, 0, 1)
    dkv = dkv.reshape(dkv.shape[0], kv_heads, 2, HD)
    return (
        dq,
        dkv[:, :, 0].reshape(-1, kv_heads * HD),
        dkv[:, :, 1].reshape(-1, kv_heads * HD),
    )


def solution(mesh):
    placed = (
        P(("ctx", "head"), None),
        P("ctx", "head"),
        P("ctx", "head"),
        P(("ctx", "head"), None),
        P(("ctx", "head"), None),
        P(),
        P(),
    )
    slabs = mesh.shape["head"] == 1 and mesh.shape["ctx"] == 32
    return jax.shard_map(
        local_planes if slabs else local_any,
        mesh=mesh,
        in_specs=placed,
        out_specs=(P("ctx", "head"), P("ctx", "head"), P("ctx", "head")),
        check_vma=False,
    )
```
